32 devices in a mesh: dp: 8 (over z, y), chan: 4 (over x, core).
Axes of the slice: x: 2, y: 2, z: 4, core: 2. Of those that a mesh axis runs over, the one named last changes fastest.
Arguments:
- tokens: bfloat16 [1024, 8, 2048], P(None, 'dp'), may hold values from -6 to 6
- doc_lengths: int32 [8, 4], P('dp'), may hold values from 1 to 512, 1024 in all within a row
- gain_mix: float32 [2048], replicated, may hold values from 0.5 to 1.5
- value_weight: bfloat16 [2048, 2736], P('dp', 'chan'), may hold values from -0.125 to 0.125
- branch_weight: bfloat16 [2048, 2736], P('dp', 'chan'), may hold values from -0.125 to 0.125
- conv_weight: float32 [4, 2736], P(None, 'chan'), may hold values from -3 to 3
- conv_bias: float32 [2736], P('chan'), may hold values from -3 to 3
- recur_gate: bfloat16 [16, 171, 171], P('chan'), may hold values from -0.4375 to 0.4375
- input_gate: bfloat16 [16, 171, 171], P('chan'), may hold values from -0.4375 to 0.4375
- recur_bias: float32 [2736], P('chan'), may hold values from -3 to 3
- input_bias: float32 [2736], P('chan'), may hold values from -3 to 3
- decay_param: float32 [2736], P('chan'), may hold values from -9 to -4
- out_weight: bfloat16 [2736, 2048], P('chan', 'dp'), may hold values from -0.3125 to 0.3125
- gain_ffn: float32 [2048], replicated, may hold values from 0.5 to 1.5
- gate_weight: bfloat16 [2048, 6144], P('dp', 'chan'), may hold values from -0.125 to 0.125
- up_weight: bfloat16 [2048, 6144], P('dp', 'chan'), may hold values from -0.125 to 0.125
- down_weight: bfloat16 [6144, 2048], P('chan', 'dp'), may hold values from -0.109375 to 0.109375
- cotangent: bfloat16 [1024, 8, 2048], P('chan', 'dp'), may hold values from -6 to 6
Outputs:
- output: bfloat16 [1024, 8, 2048], P('chan', 'dp')
- grad_tokens: float32 [1024, 8, 2048], P('chan', 'dp')
- grad_gain_mix: float32 [2048], replicated
- grad_value_weight: float32 [2048, 2736], P('dp', 'chan')
- grad_branch_weight: float32 [2048, 2736], P('dp', 'chan')
- grad_conv_weight: float32 [4, 2736], P(None, 'chan')
- grad_conv_bias: float32 [2736], P('chan')
- grad_recur_gate: float32 [16, 171, 171], P('chan')
- grad_input_gate: float32 [16, 171, 171], P('chan')
- grad_recur_bias: float32 [2736], P('chan')
- grad_input_bias: float32 [2736], P('chan')
- grad_decay_param: float32 [2736], P('chan')
- grad_out_weight: float32 [2736, 2048], P('chan', 'dp')
- grad_gain_ffn: float32 [2048], replicated
- grad_gate_weight: float32 [2048, 6144], P('dp', 'chan')
- grad_up_weight: float32 [2048, 6144], P('dp', 'chan')
- grad_down_weight: float32 [6144, 2048], P('chan', 'dp')
The draws below stay inside these ranges and needn't reach their ends.
Inputs may be any that keep to these rules, and one draw needn't show every extreme that they name: `doc_lengths`: in every row the 4 lengths add up to 1024.
All inputs are finite; a program needn't handle non-finite values.
Results may differ from the reference program's by a relative error of at most 0.0089.
Values may be sent and summed in bfloat16 or wider, within the bound.
No kernel may reach another device: no remote copies, remote signals or barrier semaphores. Data moves between devices by JAX's collectives and lax.ppermute only.
A program may use at most 384 MiB of HBM per device.

```python
import math
import jax
import jax.numpy as jnp
import numpy as np
from jax import lax

D = 2048
F = 6144
HEADS = 16
HC = 171
CONV = 4
SEQ = 1024
DOCS = 4
ROWS = 8
R = 2736


def strengthened(values, key, source, target, parts, factor):
    def block_of(axis_at):
        return (jnp.arange(values.shape[axis_at]) // (values.shape[axis_at] // parts)).reshape((-1,) + (1,) * (values.ndim - 1 - axis_at))

    near = jax.random.permutation(key, parts)[block_of(target)]
    far = (block_of(target) + parts // 2) % parts
    return jnp.where((block_of(source) == near) | (block_of(source) == far), factor * values, values)


def levels(rng, extent, shards, low, top_value):
    def one(dim, blocks):
        steps = jax.random.uniform(jax.random.fold_in(jax.random.fold_in(rng, 6), dim), (blocks,), jnp.float32, low / len(shards), top_value / len(shards))
        return jnp.repeat(jnp.exp(steps), extent[dim] // blocks).reshape((-1,) + (1,) * (len(extent) - dim - 1))

    level = one(*shards[0])
    for cut in shards[1:]:
        level = level * one(*cut)
    return level


def profile(number_of, total, most, slope):
    portions = [(1 << 20) // math.isqrt(standing ** slope) + 1 for standing in range(2, number_of + 1)]
    surplus, given = total - most - (number_of - 1), [1] * (number_of - 1)
    while surplus > 0:
        candidates = [i for i in range(number_of - 1) if given[i] < most]
        pool, remaining = sum([portions[i] for i in candidates]), surplus
        for i in candidates:
            extra = min(most - given[i], max(1, remaining * portions[i] // pool), surplus)
            given[i] = given[i] + extra
            surplus = surplus - extra
    return np.array([most] + given)


def ragged(key, count, total, reach, skew):
    if count == 2:
        one = jax.random.randint(key, (), max(1, total - reach), min(reach, total - 1) + 1)
        return jnp.stack([one, total - one])
    sizes = jnp.asarray(profile(count, total, reach, skew), jnp.int32)
    twos = (count - 1) // 2
    giver, taker = sizes[1:1 + 2 * twos:2], sizes[2:2 + 2 * twos:2]
    slack = jnp.minimum(giver - 1, reach - taker)
    moved = jax.random.randint(jax.random.fold_in(key, 1), (twos,), 0, 1 << 20) % (slack + 1)
    sizes = sizes.at[1:1 + 2 * twos:2].set(giver - moved).at[2:2 + 2 * twos:2].set(taker + moved)
    return sizes[jax.random.permutation(jax.random.fold_in(key, 2), count)]


def gaussian(own_key, dims, spread, most, cuts=(), kind=jnp.bfloat16):
    array = jax.random.normal(own_key, dims, jnp.float32) * spread
    if len(cuts) > 0:
        array = levels(own_key, dims, cuts, -0.22, 0.18) * array
    return jnp.clip(array, min=-most, max=most).astype(kind)


def bell_draw_with(stream_key, extent, deviation, limit, shards, heavy, kind=jnp.bfloat16):
    entries = deviation * jax.random.normal(stream_key, extent, jnp.float32)
    if shards:
        entries = entries * levels(stream_key, extent, shards, -0.22, 0.18)
    return jnp.clip(strengthened(entries, jax.random.fold_in(stream_key, 3), *heavy), -limit, limit).astype(kind)


def setup_inputs(seed: int = 0) -> dict:
    key_of = jax.random.split(jax.random.key(seed), 19)
    tokens = bell_draw_with(key_of[0], (SEQ, ROWS, D), 1.0, 6.0, ((1, 8),), (1, 2, 8, 2.0))
    doc_lengths = jax.vmap(lambda own: ragged(own, DOCS, SEQ, SEQ // 2, 2))(jax.random.split(key_of[1], ROWS)).reshape((ROWS, DOCS)).astype(jnp.int32)
    gain_mix = jnp.clip(1.0 + 0.1 * jax.random.normal(key_of[2], (D,), jnp.float32), 0.5, 1.5)
    value_weight = gaussian(key_of[3], (D, R), D ** -0.5, 0.125, ((0, 8), (1, 4)))
    branch_weight = gaussian(key_of[4], (D, R), D ** -0.5, 0.125, ((0, 8), (1, 4)))
    conv_weight = gaussian(key_of[5], (CONV, R), CONV ** -0.5, 3.0, ((1, 4),), jnp.float32)
    conv_bias = gaussian(key_of[6], (R,), 0.5, 3.0, ((0, 4),), jnp.float32)
    recur_gate = gaussian(key_of[7], (HEADS, HC, HC), HC ** -0.5, 0.4375, ((0, 4),))
    input_gate = gaussian(key_of[8], (HEADS, HC, HC), HC ** -0.5, 0.4375, ((0, 4),))
    recur_bias = gaussian(key_of[9], (R,), 0.5, 3.0, ((0, 4),), jnp.float32)
    input_bias = gaussian(key_of[10], (R,), 0.5, 3.0, ((0, 4),), jnp.float32)
    decay_param = jnp.clip(-9.0 + 5.0 * jax.random.uniform(key_of[11], (R,), jnp.float32) ** levels(key_of[11], (R,), ((0, 4),), -0.2, 0.2), -9.0, -4.0)
    out_weight = gaussian(key_of[12], (R, D), (R // 9) ** -0.5, 0.3125, ((0, 4), (1, 8)))
    gain_ffn = jnp.clip(1.0 + 0.1 * jax.random.normal(key_of[13], (D,), jnp.float32), 0.5, 1.5)
    gate_weight = gaussian(key_of[14], (D, F), D ** -0.5, 0.125, ((0, 8), (1, 4)))
    up_weight = gaussian(key_of[15], (D, F), D ** -0.5, 0.125, ((0, 8), (1, 4)))
    down_weight = gaussian(key_of[16], (F, D), (F // 2) ** -0.5, 0.109375, ((0, 4), (1, 8)))
    cotangent = gaussian(key_of[17], (SEQ, ROWS, D), 1.0, 6.0, ((0, 4), (1, 8)))
    return {"tokens": tokens, "doc_lengths": doc_lengths, "gain_mix": gain_mix, "value_weight": value_weight, "branch_weight": branch_weight, "conv_weight": conv_weight, "conv_bias": conv_bias, "recur_gate": recur_gate, "input_gate": input_gate, "recur_bias": recur_bias, "input_bias": input_bias, "decay_param": decay_param, "out_weight": out_weight, "gain_ffn": gain_ffn, "gate_weight": gate_weight, "up_weight": up_weight, "down_weight": down_weight, "cotangent": cotangent}


@jax.custom_vjp
def low(v):
    return lax.optimization_barrier(v.astype(jnp.bfloat16)).astype(jnp.float32)

@jax.custom_vjp
def low_back(v):
    return v

def low_keep(v):
    return (low(v), None)

def low_pass(kept, grad):
    return (grad,)

def back_keep(v):
    return (v, None)

def back_low(kept, grad):
    return (low(grad),)
low.defvjp(low_keep, low_pass)
low_back.defvjp(back_keep, back_low)
epsilon = 1e-06
decay_scale = 8.0
floor_value = 0.0001
highest = lax.Precision.HIGHEST

def matmul(left, right):
    return jnp.dot(left, right, precision=highest, preferred_element_type=jnp.float32)

def rms_norm(inputs, scales):
    return inputs * lax.rsqrt(lax.optimization_barrier(jnp.mean(inputs * inputs, axis=-1, keepdims=True)) + epsilon) * scales

def link(earlier, later):
    return (earlier[0] * later[0], later[0] * earlier[1] + later[1])

def row_masks(lengths):
    doc_ends = jnp.cumsum(lengths).astype(jnp.int32)
    places = jnp.arange(SEQ, dtype=jnp.int32)
    segment = lax.optimization_barrier(jnp.sum((places[:, None] >= doc_ends[None, :-1]).astype(jnp.int32), axis=1)).astype(jnp.int32)
    earlier = jnp.concatenate([jnp.full((1,), -1, jnp.int32), segment[:-1]])
    starts = (segment != earlier).astype(jnp.float32)
    same_doc = []
    for offset in range(CONV):
        behind = jnp.concatenate([jnp.full((offset,), -1, jnp.int32), segment[:SEQ - offset]])
        same_doc.append((behind == segment).astype(jnp.float32))
    return (starts, same_doc)

def block_row(row_in, lengths, weights):
    gain_mix, value_weight, branch_weight, conv_weight, conv_bias, recur_gate, input_gate, recur_bias, input_bias, decay_param, out_weight, gain_ffn, gate_weight, up_weight, down_weight = weights
    starts, same_doc = row_masks(lengths)
    low_in = low(rms_norm(row_in, gain_mix))
    branch_x = low_back(matmul(low_in, value_weight))
    branch_y = low_back(matmul(low_in, branch_weight))
    conv_in = conv_bias + conv_weight[0] * branch_x * same_doc[0][:, None]
    for offset in range(1, CONV):
        leading = jnp.zeros((offset, HEADS * HC), jnp.float32)
        moved = jnp.concatenate([leading, branch_x[:SEQ - offset]], axis=0)
        conv_in = conv_in + conv_weight[offset] * moved * same_doc[offset][:, None]
    conv_in = low(conv_in)
    by_head = conv_in.reshape(SEQ, HEADS, HC)
    gate_pre = low_back(jnp.einsum('thc,hcd->thd', by_head, recur_gate, precision=highest).reshape(SEQ, HEADS * HC) + recur_bias)
    admit_pre = low_back(jnp.einsum('thc,hcd->thd', by_head, input_gate, precision=highest).reshape(SEQ, HEADS * HC) + input_bias)
    recur_rate = jax.nn.sigmoid(gate_pre)
    admit_rate = jax.nn.sigmoid(admit_pre)
    decay_rate = jax.nn.softplus(decay_param) * recur_rate
    retain = jnp.exp(-decay_scale * decay_rate)
    one_minus = jnp.maximum(-jnp.expm1(-2.0 * decay_scale * decay_rate), floor_value)
    scale_in = jnp.where(starts[:, None] > 0, 1.0, jnp.sqrt(one_minus))
    carry_coef = retain * (1.0 - starts[:, None])
    drive_in = scale_in * admit_rate * conv_in
    coef_sum, running = lax.associative_scan(link, (carry_coef, drive_in))
    low_mixed = low(running * jax.nn.gelu(branch_y, approximate=True))
    residual = row_in + low_back(matmul(low_mixed, out_weight))
    low_mid = low(rms_norm(residual, gain_ffn))
    gate_lin = low_back(matmul(low_mid, gate_weight))
    up_lin = low_back(matmul(low_mid, up_weight))
    hidden = low(jax.nn.gelu(gate_lin, approximate=True) * up_lin)
    return residual + matmul(hidden, down_weight)

def reference(tokens, doc_lengths, gain_mix, value_weight, branch_weight, conv_weight, conv_bias, recur_gate, input_gate, recur_bias, input_bias, decay_param, out_weight, gain_ffn, gate_weight, up_weight, down_weight, cotangent):
    params = (gain_mix.astype(jnp.float32), value_weight.astype(jnp.float32), branch_weight.astype(jnp.float32), conv_weight.astype(jnp.float32), conv_bias.astype(jnp.float32), recur_gate.astype(jnp.float32), input_gate.astype(jnp.float32), recur_bias.astype(jnp.float32), input_bias.astype(jnp.float32), decay_param.astype(jnp.float32), out_weight.astype(jnp.float32), gain_ffn.astype(jnp.float32), gate_weight.astype(jnp.float32), up_weight.astype(jnp.float32), down_weight.astype(jnp.float32))
    rows_first = jnp.swapaxes(tokens.astype(jnp.float32), 0, 1)
    cot_rows = jnp.swapaxes(cotangent.astype(jnp.float32), 0, 1)

    def forward(weights, inputs):

        def one_row(row_pair):
            return block_row(row_pair[0], row_pair[1], weights)
        return lax.map(jax.checkpoint(one_row), (inputs, doc_lengths))
    result, pullback = jax.vjp(forward, params, rows_first)
    grads, grad_rows = pullback(cot_rows)
    output = jnp.swapaxes(result, 0, 1).astype(jnp.bfloat16)
    grad_tokens = jnp.swapaxes(grad_rows, 0, 1)
    return (output, grad_tokens, grads[0], grads[1], grads[2], grads[3], grads[4], grads[5], grads[6], grads[7], grads[8], grads[9], grads[10], grads[11], grads[12], grads[13], grads[14])
```

```python
from functools import partial

import jax
import jax.numpy as jnp
from jax import lax
from jax.experimental import pallas as pl
from jax.experimental.pallas import tpu as pltpu
from jax.sharding import PartitionSpec as P

epsilon = 1e-06
decay_scale = 8.0
floor_value = 0.0001
gelu_root = 0.7978845608
gelu_cube = 0.044715
floats = jnp.float32
halves = jnp.bfloat16
contract_last = (((1,), (1,)), ((), ()))
contract_first = (((0,), (0,)), ((), ()))
CHUNK = 16
VMEM_BYTES = 48 * 1024 * 1024


def round_up(number, unit):
    return -(-number // unit) * unit


def pad_dim(array, axis, size):
    widths = [(0, 0)] * array.ndim
    widths[axis] = (0, size - array.shape[axis])
    return jnp.pad(array, widths)


class Grid:
    def __init__(self, axis, inner):
        self.axis = axis
        self.count = lax.axis_size(axis)
        self.inner = inner
        self.outer = self.count // inner
        place = lax.axis_index(axis)
        self.at_outer = place // inner
        self.at_inner = place % inner

    def hop_outer(self, value, step):
        pairs = [
            (o * self.inner + i, ((o + step) % self.outer) * self.inner + i)
            for o in range(self.outer)
            for i in range(self.inner)
        ]
        return lax.ppermute(value, self.axis, pairs)

    def hop_inner(self, value, step):
        pairs = [
            (o * self.inner + i, o * self.inner + (i + step) % self.inner)
            for o in range(self.outer)
            for i in range(self.inner)
        ]
        return lax.ppermute(value, self.axis, pairs)

    def order(self):
        k = jnp.arange(self.count, dtype=jnp.int32)
        outer = (self.at_outer + k % self.outer) % self.outer
        inner = (self.at_inner + k // self.outer) % self.inner
        return outer * self.inner + inner

    def place_of(self):
        k = jnp.arange(self.count, dtype=jnp.int32)
        outer = (k // self.inner - self.at_outer) % self.outer
        inner = (k % self.inner - self.at_inner) % self.inner
        return inner * self.outer + outer

    def gather(self, own, inner_first=False):
        blocks = {(0, 0): own}
        if inner_first:
            for t in range(1, self.inner):
                blocks[t, 0] = self.hop_inner(blocks[t - 1, 0], -1)
            for s in range(1, self.outer):
                for t in range(self.inner):
                    blocks[t, s] = self.hop_outer(blocks[t, s - 1], -1)
        else:
            for s in range(self.outer):
                if s:
                    blocks[0, s] = self.hop_outer(blocks[0, s - 1], -1)
                for t in range(1, self.inner):
                    blocks[t, s] = self.hop_inner(blocks[t - 1, s], -1)
        return [blocks[t, s] for t in range(self.inner) for s in range(self.outer)]

    def reduce(self, part):
        passing = None
        for s in reversed(range(self.outer)):
            total = part(self.inner - 1, s)
            for t in reversed(range(self.inner - 1)):
                total = part(t, s) + self.hop_inner(total.astype(halves), 1).astype(floats)
            if passing is not None:
                total = total + passing
            if s:
                passing = self.hop_outer(total.astype(halves), 1).astype(floats)
        return total

    def total(self, value):
        if self.count & (self.count - 1):
            return lax.psum(value, self.axis)
        bit = 1
        while bit < self.count:
            value = value + lax.ppermute(
                value, self.axis, [(i, i ^ bit) for i in range(self.count)]
            )
            bit *= 2
        return value


def gather_rows(grid, own):
    near = [own]
    for s in range(1, grid.outer):
        near.append(grid.hop_outer(near[-1], -1))
    near = jnp.concatenate(near, axis=0) if grid.outer > 1 else own
    halves_of = [near]
    for t in range(1, grid.inner):
        halves_of.append(grid.hop_inner(halves_of[-1], -1))
    return jnp.concatenate(halves_of, axis=0)


def reduce_rows(grid, product):
    rows = product.shape[0] // grid.inner
    total = product[(grid.inner - 1) * rows :]
    for t in reversed(range(grid.inner - 1)):
        total = product[t * rows : (t + 1) * rows] + grid.hop_inner(
            total.astype(halves), 1
        ).astype(floats)
    rows = rows // grid.outer
    passing = total[(grid.outer - 1) * rows :]
    for s in reversed(range(grid.outer - 1)):
        passing = total[s * rows : (s + 1) * rows] + grid.hop_outer(
            passing.astype(halves), 1
        ).astype(floats)
    return passing


def params():
    return pltpu.CompilerParams(vmem_limit_bytes=VMEM_BYTES)


def reorder_columns(array, order, back=False):
    rows, width = array.shape
    count = order.shape[0]
    block = width // count

    def body(order_ref, in_ref, out_ref):
        out_ref[...] = in_ref[...]

    straight = pl.BlockSpec((rows, block), lambda k, order_ref: (0, k))
    picked = pl.BlockSpec((rows, block), lambda k, order_ref: (0, order_ref[k]))
    return pl.pallas_call(
        body,
        out_shape=jax.ShapeDtypeStruct(array.shape, array.dtype),
        grid_spec=pltpu.PrefetchScalarGridSpec(
            num_scalar_prefetch=1,
            grid=(count,),
            in_specs=[straight if back else picked],
            out_specs=picked if back else straight,
        ),
        compiler_params=params(),
        name="reorder_columns",
    )(order, array)


def first_norm(tokens, gain, row_order, order):
    seq_len, width = tokens.shape
    tiles, count = row_order.shape[0], order.shape[0]
    part, block = seq_len // tiles, width // count

    def body(rows_ref, order_ref, tok_ref, gain_ref, out_ref, own_ref):
        whole = tok_ref[...].astype(floats)
        inverse = lax.rsqrt(jnp.mean(whole * whole, axis=-1, keepdims=True) + epsilon)
        for k in range(count):
            source = pl.ds(pl.multiple_of(order_ref[k] * block, block), block)
            raw = tok_ref[:, source]
            normed = raw.astype(floats) * inverse * gain_ref[:, source]
            out_ref[:, k * block : (k + 1) * block] = normed.astype(halves)

            @pl.when(pl.program_id(0) == 0)
            def _():
                own_ref[:, k * block : (k + 1) * block] = raw

    return pl.pallas_call(
        body,
        out_shape=(
            jax.ShapeDtypeStruct((seq_len, width), halves),
            jax.ShapeDtypeStruct((part, width), tokens.dtype),
        ),
        grid_spec=pltpu.PrefetchScalarGridSpec(
            num_scalar_prefetch=2,
            grid=(tiles,),
            in_specs=[
                pl.BlockSpec((part, width), lambda i, rows_ref, order_ref: (rows_ref[i], 0)),
                pl.BlockSpec((1, width), lambda i, rows_ref, order_ref: (0, 0)),
            ],
            out_specs=(
                pl.BlockSpec((part, width), lambda i, rows_ref, order_ref: (i, 0)),
                pl.BlockSpec((part, width), lambda i, rows_ref, order_ref: (0, 0)),
            ),
        ),
        compiler_params=params(),
        name="first_norm",
    )(row_order, order, tokens, gain.reshape(1, width))


def segment_of(places, ends_ref):
    segment = jnp.zeros(places.shape, jnp.int32)
    for j in range(ends_ref.shape[0] - 1):
        segment = segment + (places >= ends_ref[j]).astype(jnp.int32)
    return segment


def same_behind(places, ends_ref, offset):
    agree = segment_of(places, ends_ref) == segment_of(places - offset, ends_ref)
    return jnp.logical_and(agree, places >= offset).astype(floats)


def same_ahead(places, ends_ref, offset, seq_len):
    agree = segment_of(places, ends_ref) == segment_of(places + offset, ends_ref)
    return jnp.logical_and(agree, places + offset < seq_len).astype(floats)


def lane_chunks(width):
    step = 256 if width % 256 == 0 else 128
    return [slice(at, at + step) for at in range(0, width, step)]


def gate_values(pre_a, pre_i, decay8):
    rate = jax.nn.sigmoid(pre_a)
    admit = jax.nn.sigmoid(pre_i)
    power = decay8 * rate
    alpha = jnp.exp(-power)
    twice = 2.0 * power
    series = 1.0 - twice * (1.0 / 7.0)
    for order in (6.0, 5.0, 4.0, 3.0, 2.0):
        series = 1.0 - (twice * (1.0 / order)) * series
    raw = jnp.where(twice < 0.5, twice * series, 1.0 - alpha * alpha)
    one_minus = jnp.maximum(raw, floor_value)
    inverse = lax.rsqrt(one_minus)
    return rate, admit, alpha, raw, one_minus * inverse, inverse


def gelu_parts(value):
    square = value * value
    bend = jnp.tanh(gelu_root * (value + gelu_cube * (square * value)))
    half = 0.5 * (1.0 + bend)
    slope = half + 0.5 * value * (1.0 - bend * bend) * (
        gelu_root * (1.0 + 3.0 * gelu_cube * square)
    )
    return value * half, slope


def gelu(value):
    return gelu_parts(value)[0]


def recur_forward(branches, doc_ends, vectors, gates, places):
    seq_len, lanes = branches.shape[0], branches.shape[1] // 2
    tiles = places.shape[0]
    part = seq_len // tiles
    chunks = lane_chunks(lanes)

    def body(
        places_ref, ends_ref, x_ref, y_ref, vec_ref, gate_ref,
        mixed_ref, conv_ref, pre_ref, prev_ref, xs, carry,
    ):
        tile = pl.program_id(0)

        @pl.when(tile == 0)
        def _():
            xs[0:8] = jnp.zeros((8, lanes), floats)
            carry[...] = jnp.zeros_like(carry)

        xs[8 : 8 + part] = x_ref[...]
        rows = lax.broadcasted_iota(jnp.int32, (CHUNK, 1), 0)

        def convolve(c, _):
            at = pl.multiple_of(c * CHUNK, CHUNK)
            here = tile * part + at + rows
            same = [same_behind(here, ends_ref, k) for k in range(1, 4)]
            for lane in chunks:
                window = xs[pl.ds(at, CHUNK + 8), lane]
                total = vec_ref[4:5, lane] + vec_ref[0:1, lane] * window[8:]
                for k in range(1, 4):
                    moved = pltpu.roll(window, k, 0)[8:]
                    total = total + vec_ref[k : k + 1, lane] * moved * same[k - 1]
                conv_ref[pl.ds(at, CHUNK), lane] = total.astype(halves)
            return 0

        lax.fori_loop(0, part // CHUNK, convolve, 0)
        xs[0:8] = xs[part : part + 8]
        pre_ref[...] = jnp.dot(conv_ref[...], gate_ref[...], preferred_element_type=floats)

        def advance(c, entering):
            at = pl.multiple_of(c * CHUNK, CHUNK)
            here = tile * part + at + rows
            fresh = 1.0 - same_behind(here, ends_ref, 1)
            leaving = []
            for state, lane in zip(entering, chunks):
                span = lane.stop - lane.start
                shift_lane = slice(lane.start + lanes, lane.stop + lanes)
                pre_a = pre_ref[pl.ds(at, CHUNK), lane] + vec_ref[6:7, lane]
                pre_i = pre_ref[pl.ds(at, CHUNK), shift_lane] + vec_ref[7:8, lane]
                pre_ref[pl.ds(at, CHUNK), lane] = pre_a
                pre_ref[pl.ds(at, CHUNK), shift_lane] = pre_i
                conv_in = conv_ref[pl.ds(at, CHUNK), lane].astype(floats)
                _, admit, alpha, _, root, _ = gate_values(pre_a, pre_i, vec_ref[5:6, lane])
                keep = 1.0 - fresh
                coef = alpha * keep
                drive = (fresh + root * keep) * admit * conv_in
                index = lax.broadcasted_iota(jnp.int32, (CHUNK, span), 0)
                for d in (1, 2, 4):
                    inside = (index & 7) >= d
                    drive = jnp.where(inside, drive + coef * pltpu.roll(drive, d, 0), drive)
                    coef = jnp.where(inside, coef * pltpu.roll(coef, d, 0), coef)
                groups = []
                first = state
                for g in range(CHUNK // 8):
                    group = slice(g * 8, g * 8 + 8)
                    groups.append(coef[group] * state + drive[group])
                    state = groups[-1][7:8]
                states = jnp.concatenate(groups, axis=0)
                prev_ref[pl.ds(at, CHUNK), lane] = jnp.where(
                    index == 0, first, pltpu.roll(states, 1, 0)
                )
                mixed = states * gelu(y_ref[pl.ds(at, CHUNK), lane])
                mixed_ref[pl.ds(at, CHUNK), lane] = mixed.astype(halves)
                leaving.append(state)
            return tuple(leaving)

        ended = lax.fori_loop(
            0, part // CHUNK, advance, tuple(carry[0:1, lane] for lane in chunks)
        )
        for state, lane in zip(ended, chunks):
            carry[0:1, lane] = state

    own = lambda column: pl.BlockSpec((part, lanes), lambda i, p, e: (p[i], column))
    straight = lambda width: pl.BlockSpec((part, width), lambda i, p, e: (i, 0))
    whole = lambda array: pl.BlockSpec(array.shape, lambda i, p, e: (0, 0))
    return pl.pallas_call(
        body,
        out_shape=(
            jax.ShapeDtypeStruct((seq_len, lanes), halves),
            jax.ShapeDtypeStruct((seq_len, lanes), halves),
            jax.ShapeDtypeStruct((seq_len, 2 * lanes), floats),
            jax.ShapeDtypeStruct((seq_len, lanes), floats),
        ),
        grid_spec=pltpu.PrefetchScalarGridSpec(
            num_scalar_prefetch=2,
            grid=(tiles,),
            in_specs=[own(0), own(1), whole(vectors), whole(gates)],
            out_specs=(own(0), straight(lanes), straight(2 * lanes), straight(lanes)),
            scratch_shapes=[pltpu.VMEM((part + 8, lanes), floats), pltpu.VMEM((8, lanes), floats)],
        ),
        compiler_params=params(),
        cost_estimate=pl.CostEstimate(
            flops=4 * seq_len * lanes * lanes,
            bytes_accessed=seq_len * lanes * 32,
            transcendentals=seq_len * lanes * 6,
        ),
        name="recur_forward",
    )(places, doc_ends, branches, branches, vectors, gates)


def recur_backward(back_mixed, branches, conv_in, pre, previous, doc_ends, vectors, gates, places):
    seq_len, lanes = conv_in.shape
    tiles = places.shape[0]
    part = seq_len // tiles
    chunks = lane_chunks(lanes)
    steps = part // CHUNK

    def body(
        places_ref, ends_ref, bm_ref, x_ref, y_ref, conv_ref, pre_ref, prev_ref, vec_ref, gate_ref,
        bxy_ref, bai_ref, sums_ref, ahead, sums, carry,
    ):
        tile = tiles - 1 - pl.program_id(0)

        @pl.when(pl.program_id(0) == 0)
        def _():
            ahead[part : part + 8] = jnp.zeros((8, lanes), floats)
            sums[...] = jnp.zeros_like(sums)
            carry[...] = jnp.zeros_like(carry)

        rows = lax.broadcasted_iota(jnp.int32, (CHUNK, 1), 0)

        def add_rows(which, lane, value):
            for g in range(CHUNK // 8):
                sums[which * 8 : which * 8 + 8, lane] += value[g * 8 : g * 8 + 8]

        def retreat(c, entering):
            at = pl.multiple_of((steps - 1 - c) * CHUNK, CHUNK)
            span_rows = pl.ds(at, CHUNK)
            here = tile * part + at + rows
            keep = same_behind(here, ends_ref, 1)
            fresh = 1.0 - keep
            leaving = []
            for (back_next, coef_next), lane in zip(entering, chunks):
                span = lane.stop - lane.start
                shift_lane = slice(lane.start + lanes, lane.stop + lanes)
                decay8 = vec_ref[5:6, lane]
                rate, admit, alpha, raw, root, inverse = gate_values(
                    pre_ref[span_rows, lane], pre_ref[span_rows, shift_lane], decay8
                )
                conv = conv_ref[span_rows, lane].astype(floats)
                before = prev_ref[span_rows, lane]
                scale_in = fresh + root * keep
                coef = alpha * keep
                driven = scale_in * admit
                states = coef * before + driven * conv
                active, slope = gelu_parts(y_ref[span_rows, lane])
                back_mix = bm_ref[span_rows, lane]
                bxy_ref[span_rows, shift_lane] = (back_mix * states * slope).astype(halves)
                index = lax.broadcasted_iota(jnp.int32, (CHUNK, span), 0)
                back = back_mix * active
                chain = jnp.where(index == CHUNK - 1, coef_next, pltpu.roll(coef, CHUNK - 1, 0))
                for d in (1, 2, 4):
                    inside = (index & 7) < 8 - d
                    back = jnp.where(inside, back + chain * pltpu.roll(back, CHUNK - d, 0), back)
                    chain = jnp.where(inside, chain * pltpu.roll(chain, CHUNK - d, 0), chain)
                groups = []
                for g in reversed(range(CHUNK // 8)):
                    group = slice(g * 8, g * 8 + 8)
                    groups.insert(0, back[group] + chain[group] * back_next)
                    back_next = groups[0][0:1]
                back_state = jnp.concatenate(groups, axis=0)
                through = back_state * conv
                bound = jnp.where(raw > floor_value, through * admit * alpha * inverse, 0.0)
                back_alpha = (back_state * before - bound) * keep * alpha
                add_rows(5, lane, back_alpha * rate)
                back_a = (back_alpha * (-decay8) * rate * (1.0 - rate)).astype(halves)
                back_i = (through * scale_in * admit * (1.0 - admit)).astype(halves)
                add_rows(6, lane, back_a.astype(floats))
                add_rows(7, lane, back_i.astype(floats))
                bai_ref[span_rows, lane] = back_a
                bai_ref[span_rows, shift_lane] = back_i
                ahead[span_rows, lane] = back_state * driven
                leaving.append((back_next, coef[0:1]))
            return tuple(leaving)

        ended = lax.fori_loop(
            0, steps, retreat, tuple((carry[0:1, lane], carry[8:9, lane]) for lane in chunks)
        )
        for (back_next, coef_next), lane in zip(ended, chunks):
            carry[0:1, lane] = back_next
            carry[8:9, lane] = coef_next

        ahead[0:part] += lax.dot_general(
            bai_ref[...], gate_ref[...], contract_last, preferred_element_type=floats
        )

        def convolve(c, _):
            at = pl.multiple_of(c * CHUNK, CHUNK)
            here = tile * part + at + rows
            same = [same_ahead(here, ends_ref, k, seq_len) for k in range(1, 4)]
            for lane in chunks:
                window = ahead[pl.ds(at, CHUNK + 8), lane]
                x_part = x_ref[pl.ds(at, CHUNK), lane]
                direct = window[:CHUNK]
                back_x = vec_ref[0:1, lane] * direct
                add_rows(0, lane, x_part * direct)
                add_rows(4, lane, direct)
                for k in range(1, 4):
                    moved = pltpu.roll(window, CHUNK + 8 - k, 0)[:CHUNK] * same[k - 1]
                    back_x = back_x + vec_ref[k : k + 1, lane] * moved
                    add_rows(k, lane, x_part * moved)
                bxy_ref[pl.ds(at, CHUNK), lane] = back_x.astype(halves)
            return 0

        lax.fori_loop(0, steps, convolve, 0)
        ahead[part : part + 8] = ahead[0:8]

        @pl.when(pl.program_id(0) == tiles - 1)
        def _():
            for which in range(8):
                sums_ref[which : which + 1] = jnp.sum(
                    sums[which * 8 : which * 8 + 8], axis=0, keepdims=True
                )

    own = lambda width, column: pl.BlockSpec(
        (part, width), lambda i, p, e: (p[tiles - 1 - i], column)
    )
    straight = lambda width: pl.BlockSpec((part, width), lambda i, p, e: (tiles - 1 - i, 0))
    whole = lambda array: pl.BlockSpec(array.shape, lambda i, p, e: (0, 0))
    return pl.pallas_call(
        body,
        out_shape=(
            jax.ShapeDtypeStruct((seq_len, 2 * lanes), halves),
            jax.ShapeDtypeStruct((seq_len, 2 * lanes), halves),
            jax.ShapeDtypeStruct((8, lanes), floats),
        ),
        grid_spec=pltpu.PrefetchScalarGridSpec(
            num_scalar_prefetch=2,
            grid=(tiles,),
            in_specs=[
                own(lanes, 0), own(lanes, 0), own(lanes, 1),
                straight(lanes), straight(2 * lanes), straight(lanes),
                whole(vectors), whole(gates),
            ],
            out_specs=(
                own(2 * lanes, 0), straight(2 * lanes), pl.BlockSpec((8, lanes), lambda i, p, e: (0, 0)),
            ),
            scratch_shapes=[
                pltpu.VMEM((part + 8, lanes), floats),
                pltpu.VMEM((64, lanes), floats),
                pltpu.VMEM((16, lanes), floats),
            ],
        ),
        compiler_params=params(),
        cost_estimate=pl.CostEstimate(
            flops=4 * seq_len * lanes * lanes,
            bytes_accessed=seq_len * lanes * 36,
            transcendentals=seq_len * lanes * 6,
        ),
        name="recur_backward",
    )(places, doc_ends, back_mixed, branches, branches, conv_in, pre, previous, vectors, gates)


def rms_norm(inputs, scales):
    return inputs * lax.rsqrt(jnp.mean(inputs * inputs, axis=-1, keepdims=True) + epsilon) * scales


def gated(both):
    width = both.shape[1] // 2
    return gelu(both[:, :width]) * both[:, width:]


def gated_back(both, back_hidden):
    width = both.shape[1] // 2
    active, slope = gelu_parts(both[:, :width])
    back_gate = back_hidden * both[:, width:] * slope
    return jnp.concatenate(
        [back_gate.astype(halves), (back_hidden * active).astype(halves)], axis=1
    )


def inner_of(count):
    return max(d for d in range(1, count + 1) if count % d == 0 and d * d <= count)


def on_device(
    tokens,
    doc_lengths,
    gain_mix,
    value_weight,
    branch_weight,
    conv_weight,
    conv_bias,
    recur_gate,
    input_gate,
    recur_bias,
    input_bias,
    decay_param,
    out_weight,
    gain_ffn,
    gate_weight,
    up_weight,
    down_weight,
    cotangent,
):
    seq_len, _, width = tokens.shape
    heads, head_width = recur_gate.shape[:2]
    channels = value_weight.shape[1]
    hidden_width = gate_weight.shape[1]
    lanes = round_up(channels, 128)
    sent = round_up(channels, 16)
    dp = Grid("dp", inner_of(lax.axis_size("dp")))
    chan = Grid("chan", 2 if lax.axis_size("chan") % 2 == 0 else 1)
    part = seq_len // chan.count
    block = width // dp.count
    order = dp.order()
    row_order, row_place = chan.order(), chan.place_of()

    def columns(array, place):
        return array[:, place * block : (place + 1) * block]

    vb_own = jnp.concatenate(
        [pad_dim(value_weight.T, 0, sent), pad_dim(branch_weight.T, 0, sent)], axis=0
    )
    vb_full = jnp.concatenate(dp.gather(vb_own), axis=1)
    vb_full = jnp.concatenate(
        [pad_dim(vb_full[:sent], 0, lanes), pad_dim(vb_full[sent:], 0, lanes)], axis=0
    )
    out_full = jnp.concatenate(dp.gather(pad_dim(out_weight, 0, sent), inner_first=True), axis=1)
    out_full = pad_dim(out_full, 0, lanes)
    gu_full = jnp.concatenate(
        dp.gather(jnp.concatenate([gate_weight, up_weight], axis=1)), axis=0
    )
    down_full = jnp.concatenate(dp.gather(down_weight), axis=1)

    def spread(gate):
        total = 0.0
        for h in range(heads):
            low = h * head_width
            total = total + jnp.pad(gate[h], ((low, lanes - low - head_width),) * 2)
        return total

    gates = jnp.concatenate([spread(recur_gate), spread(input_gate)], axis=1)
    vectors = pad_dim(
        jnp.concatenate(
            [
                conv_weight,
                conv_bias[None],
                decay_scale * jax.nn.softplus(decay_param)[None],
                recur_bias[None],
                input_bias[None],
            ],
            axis=0,
        ),
        1,
        lanes,
    )
    doc_ends = jnp.cumsum(doc_lengths[0])
    gains = jnp.stack([gain_mix, gain_ffn]).reshape(2, dp.count, block)
    gains = jnp.take(gains, order, axis=1).reshape(2, width)

    low_in, own_tokens = first_norm(tokens.reshape(seq_len, width), gain_mix, row_order, order)
    own_tokens = own_tokens.astype(floats)
    branches = lax.dot_general(low_in, vb_full, contract_last, preferred_element_type=floats)
    mixed, conv_in, pre, previous = recur_forward(branches, doc_ends, vectors, gates, row_place)
    product = jnp.dot(mixed, out_full, preferred_element_type=floats)
    residual = own_tokens + reduce_rows(chan, product)
    normed_mid, mid_pull = jax.vjp(rms_norm, residual, gains[1])
    mid_full = gather_rows(chan, normed_mid.astype(halves))
    cot_own = reorder_columns(cotangent.reshape(part, width), order)
    cot_full = gather_rows(chan, cot_own)

    both = jnp.dot(mid_full, gu_full, preferred_element_type=floats)
    hidden = gated(both).astype(halves)
    grad_down = dp.reduce(
        lambda t, s: lax.dot_general(
            hidden,
            columns(cot_full, t * dp.outer + s),
            contract_first,
            preferred_element_type=floats,
        )
    )
    back_hidden = lax.dot_general(
        cot_full, down_full, contract_last, preferred_element_type=floats
    )
    back_both = gated_back(both, back_hidden)
    product = lax.dot_general(back_both, gu_full, contract_last, preferred_element_type=floats)
    back_mid = reduce_rows(chan, product)
    grad_gu = dp.reduce(
        lambda t, s: lax.dot_general(
            columns(mid_full, t * dp.outer + s),
            back_both,
            contract_first,
            preferred_element_type=floats,
        )
    )
    product = jnp.dot(hidden, down_full, preferred_element_type=floats)
    output = (residual + reduce_rows(chan, product)).astype(halves)

    back_norm, grad_gain_ffn = mid_pull(back_mid)
    back_resid = cot_own.astype(floats) + back_norm
    back_branch = gather_rows(chan, back_resid.astype(halves))
    back_mixed = lax.dot_general(
        back_branch, out_full, contract_last, preferred_element_type=floats
    )
    grad_out = dp.reduce(
        lambda t, s: lax.dot_general(
            mixed,
            columns(back_branch, t * dp.outer + s),
            contract_first,
            preferred_element_type=floats,
        )[:sent]
    )
    back_xy, back_ai, sums = recur_backward(
        back_mixed, branches, conv_in, pre, previous, doc_ends, vectors, gates, row_place
    )

    def vb_part(t, s):
        whole = lax.dot_general(
            back_xy,
            columns(low_in, t * dp.outer + s),
            contract_first,
            preferred_element_type=floats,
        )
        return jnp.concatenate([whole[:sent], whole[lanes : lanes + sent]], axis=0)

    grad_vb = dp.reduce(vb_part)
    product = lax.dot_general(
        back_xy,
        vb_full,
        (((1,), (0,)), ((), ())),
        preferred_element_type=floats,
    )
    back_norm_in = reduce_rows(chan, product)
    _, in_pull = jax.vjp(rms_norm, own_tokens, gains[0])
    back_tokens, grad_gain_mix = in_pull(back_norm_in)
    grad_tokens = back_resid + back_tokens

    gate_grads = lax.dot_general(conv_in, back_ai, contract_first, preferred_element_type=floats)
    gate_grads = jnp.stack(
        [
            gate_grads[
                h * head_width : (h + 1) * head_width,
                side * lanes + h * head_width : side * lanes + (h + 1) * head_width,
            ]
            for side in range(2)
            for h in range(heads)
        ]
    )
    gate_grads = lax.psum(gate_grads, "dp")
    sums = dp.total(sums)[:, :channels]
    grad_decay = sums[5] * (-decay_scale * jax.nn.sigmoid(decay_param))
    places = dp.place_of()

    def whole_gain(gradient):
        gradient = chan.total(gradient.reshape(dp.count, block))
        return dp.total(jnp.take(gradient, places, axis=0)).reshape(width)

    return (
        reorder_columns(output, order, back=True).reshape(part, 1, width),
        reorder_columns(grad_tokens, order, back=True).reshape(part, 1, width),
        whole_gain(grad_gain_mix),
        grad_vb[:channels].T,
        grad_vb[sent : sent + channels].T,
        sums[:4],
        sums[4],
        gate_grads[:heads],
        gate_grads[heads:],
        sums[6],
        sums[7],
        grad_decay,
        grad_out[:channels],
        whole_gain(grad_gain_ffn),
        grad_gu[:, :hidden_width],
        grad_gu[:, hidden_width:],
        grad_down,
    )


def solution(mesh):
    in_specs = (
        P(None, "dp", None),
        P("dp", None),
        P(),
        P("dp", "chan"),
        P("dp", "chan"),
        P(None, "chan"),
        P("chan"),
        P("chan", None, None),
        P("chan", None, None),
        P("chan"),
        P("chan"),
        P("chan"),
        P("chan", "dp"),
        P(),
        P("dp", "chan"),
        P("dp", "chan"),
        P("chan", "dp"),
        P("chan", "dp", None),
    )
    out_specs = (
        P("chan", "dp", None),
        P("chan", "dp", None),
        P(),
        P("dp", "chan"),
        P("dp", "chan"),
        P(None, "chan"),
        P("chan"),
        P("chan", None, None),
        P("chan", None, None),
        P("chan"),
        P("chan"),
        P("chan"),
        P("chan", "dp"),
        P(),
        P("dp", "chan"),
        P("dp", "chan"),
        P("chan", "dp"),
    )
    return jax.shard_map(
        on_device, mesh=mesh, in_specs=in_specs, out_specs=out_specs, check_vma=False
    )
```

```python
from functools import partial

import jax
import jax.numpy as jnp
from jax import lax
from jax.experimental import pallas as pl
from jax.experimental.pallas import tpu as pltpu
from jax.sharding import PartitionSpec as P

epsilon = 1e-06
decay_scale = 8.0
floor_value = 0.0001
gelu_root = 0.7978845608
gelu_cube = 0.044715
floats = jnp.float32
halves = jnp.bfloat16
contract_last = (((1,), (1,)), ((), ()))
contract_first = (((0,), (0,)), ((), ()))
CHUNK = 16
DP, CHAN = "dp", "chan"
VMEM_BYTES = 48 * 1024 * 1024
HEAVY = pl.CostEstimate(flops=2 * 10**11, bytes_accessed=1, transcendentals=0)


def round_up(number, unit):
    return -(-number // unit) * unit


def pad_dim(array, axis, size):
    widths = [(0, 0)] * array.ndim
    widths[axis] = (0, size - array.shape[axis])
    return jnp.pad(array, widths)


class Ring:
    def __init__(self, axis, inner):
        self.axis = axis
        self.count = lax.axis_size(axis)
        outer = self.count // inner
        self.path = [(o, 0) for o in range(outer)]
        for n, o in enumerate(reversed(range(outer))):
            columns = list(range(1, inner))
            self.path += [(o, i) for i in (reversed(columns) if n % 2 else columns)]
        self.path = [o * inner + i for o, i in self.path]
        spots = [self.path.index(i) for i in range(self.count)]
        self.spot = self.look(spots, lax.axis_index(axis))
        far = self.count // 2
        self.distances = [far]
        for j in range(1, far):
            self.distances += [far + j, far - j]
        self.distances += [0]
        self.slots = {distance: j for j, distance in enumerate(self.distances)}

    def look(self, table, index):
        return sum(jnp.where(index == i, entry, 0) for i, entry in enumerate(table))

    def hop(self, value, step):
        pairs = [
            (self.path[n], self.path[(n + step) % self.count]) for n in range(self.count)
        ]
        return lax.ppermute(value, self.axis, pairs)

    def order(self):
        ahead = self.look(self.distances, jnp.arange(self.count, dtype=jnp.int32))
        return self.look(self.path, (self.spot + ahead) % self.count).astype(jnp.int32)

    def ways(self, flip):
        ahead = (self.count - 1) // 2 if flip else self.count // 2
        return [
            (AHEAD, list(range(1, ahead + 1)), -1),
            (BACK, list(range(self.count - 1, ahead, -1)), 1),
        ]


LINK_RATE = 46e3
HOP_COST = 3.5
EARLY = 4.0
QUEUED = 2.5
CORE, AHEAD, BACK, CHIPS, CROSS, TWIN, SMALL = range(7)
DEPTHS = {AHEAD: 1, BACK: 1, CHIPS: 9, CROSS: 1, TWIN: 1, SMALL: 2}
STARTS = {AHEAD: 1.5, BACK: 0.8, CHIPS: 0.5, CROSS: 1.5, TWIN: 1.5, SMALL: 2.0}
HOPPING = (AHEAD, BACK, CROSS, TWIN, SMALL)
HOPS = 5
MARGINS = {CORE: 3.0, AHEAD: 0.5, BACK: 0.5, CHIPS: 1.0, CROSS: 0.5, TWIN: 0.5, SMALL: 2.0}


class Task:
    def __init__(self, number, resource, cost, needs, run, bias):
        self.number, self.resource, self.cost, self.needs = number, resource, cost, needs
        self.run, self.bias, self.level, self.users = run, bias, 0.0, []


class Plan:
    def __init__(self):
        self.tasks, self.log = [], []

    def add(self, resource, cost, needs, run, bias=0.0):
        task = Task(len(self.tasks), resource, cost, list(needs), run, bias)
        self.tasks.append(task)
        return task

    def compute(self, cost, needs, run, bias=0.0):
        return self.add(CORE, cost, needs, run, bias)

    def levels(self):
        for task in self.tasks:
            for need in task.needs:
                need.users.append(task)
        for task in reversed(self.tasks):
            task.level = task.cost + max([user.level for user in task.users], default=0.0)

    def execute(self, results):
        self.levels()
        waiting = sorted(self.tasks, key=lambda task: (-task.bias, -task.level))
        values, flying, free, shown = {}, {}, {}, set()
        now, fresh = 0.0, False

        def when(task):
            times = [
                0.0 if need in values else flying[need][0] if need in flying else None
                for need in task.needs
            ]
            if None in times:
                return None
            late = max(times, default=0.0)
            return late + MARGINS[task.resource] if late > 0.0 else 0.0

        def issue(task):
            nonlocal fresh
            ended = [need for need in task.needs if need in flying]
            if task.resource in HOPPING:
                under = sorted(
                    (end, other.number, other)
                    for other, (end, _) in flying.items()
                    if other.resource in HOPPING and other not in ended
                )
                ended += [other for _, _, other in under[: max(0, len(under) + 1 - HOPS)]]
            for need in ended:
                values[need] = flying.pop(need)[1]
                self.log.append((now, 1, need))
                fresh = True
            if fresh:
                wanted = {need for other in waiting for need in other.needs}
                first = {done for done in values if done in results} - shown
                names = sorted(
                    {done for done in values if done in wanted} | first,
                    key=lambda done: done.number,
                )
                tied = lax.optimization_barrier(tuple(values[done] for done in names))
                values.update(zip(names, tied))
                shown.update(first)
                fresh = False
            waiting.remove(task)
            self.log.append((now, 0, task))
            return task.run(values)

        while waiting:
            wakes, chosen = [], None
            for task in waiting:
                at, link = when(task), task.resource
                if at is None:
                    continue
                if link != CORE:
                    ends = sorted(
                        end for other, (end, _) in flying.items() if other.resource == link and end > now
                    )
                    if len(ends) >= DEPTHS[link]:
                        early = EARLY if link in (AHEAD, BACK) and len(ends) == 1 else 0.0
                        at = max(at, ends[-DEPTHS[link]] - early)
                    others = [
                        end
                        for other, (end, _) in flying.items()
                        if other.resource in HOPPING and other not in task.needs
                    ]
                    if link in HOPPING and len(others) >= HOPS:
                        at = max(at, sorted(others)[len(others) - HOPS] + MARGINS[SMALL])
                if at > now:
                    wakes.append(at)
                elif link != CORE:
                    chosen = task
                    break
                elif chosen is None:
                    chosen = task
            if chosen is None:
                now = min(wakes)
                continue
            result = issue(chosen)
            link = chosen.resource
            if link == CORE:
                values[chosen] = result
                now += chosen.cost
                fresh = True
                continue
            behind = free.get(link, 0.0) > now and link != SMALL
            end = free[link] + chosen.cost - QUEUED if behind else now + chosen.cost
            if link != SMALL:
                free[link] = end
            flying[chosen] = (end, result)
            now += STARTS[link]
        for task in results:
            if task in flying:
                values[task] = flying.pop(task)[1]
        self.log.append((now, 1, None))
        return [values[task] for task in results]


def dot_cost(rows, inner, columns):
    return 1.0 + 2.0 * rows * inner * columns / DOT_RATE


def move_cost(count):
    return 1.0 + count / 2e6


def ring_gather(plan, ring, own, count, flip=False, bias=0.0, after={}):
    blocks = {0: own}
    for link, way, step in ring.ways(flip):
        source = own
        for n, distance in enumerate(way):

            def move(v, source=source, step=step):
                return ring.hop(v[source], step)

            held = [after[link, n]] if (link, n) in after else []
            cost = HOP_COST + count * 2 / LINK_RATE
            source = plan.add(link, cost, [source, *held], move, bias)
            blocks[distance] = source
    return blocks


def ring_reduce(plan, ring, parts, count, finish, flip=False, bias=2.0, after=()):
    half = ring.count // 2

    def total(distance, sources):
        slot = ring.slots[distance]
        part = parts[slot // half]
        if not sources:
            return plan.compute(0.0, [part], lambda v: v[part][slot % half], 20.0)

        def add(v):
            terms = [v[part][slot % half], *(v[source] for source in sources)]
            if distance:
                return add_up([(term, 0) for term in terms], halves)
            return finish(sum(term.astype(floats) for term in terms))

        cost = move_cost((2.0 + len(sources)) * count)
        if not distance:
            cost = cost + move_cost(3 * count)
        return plan.compute(cost, [part, *sources], add, 10.0 if distance else -1.0)

    passings = []
    for link, way, step in ring.ways(flip):
        passing = []
        for distance in reversed(way):
            made = total(distance, passing)

            def move(v, made=made, step=step):
                return ring.hop(v[made], -step)

            cost = HOP_COST + count * 2 / LINK_RATE
            passing = [plan.add(link, cost, [made, *after], move, bias)]
        passings.extend(passing)
    return total(0, passings)


def params():
    return pltpu.CompilerParams(vmem_limit_bytes=VMEM_BYTES)


def place(full, piece, at, shape, steps, in_block, in_index, out_block, out_index):
    short = in_block[0] < out_block[0]

    def body(at_ref, in_ref, *refs):
        out_ref = refs[-1]
        if short:
            out_ref[: in_block[0]] = in_ref[...]
            out_ref[in_block[0] :] = jnp.zeros(
                (out_block[0] - in_block[0], out_block[1]), out_ref.dtype
            )
        else:
            out_ref[...] = in_ref[...]

    return pl.pallas_call(
        body,
        out_shape=jax.ShapeDtypeStruct(shape, piece.dtype),
        grid_spec=pltpu.PrefetchScalarGridSpec(
            num_scalar_prefetch=1,
            grid=(steps,),
            in_specs=[
                pl.BlockSpec(in_block, in_index),
                *([] if full is None else [pl.BlockSpec(memory_space=pl.ANY)]),
            ],
            out_specs=pl.BlockSpec(out_block, out_index),
        ),
        input_output_aliases={} if full is None else {2: 0},
        compiler_params=params(),
        cost_estimate=HEAVY,
    )(at, piece, *([] if full is None else [full]))


def add_up(terms, dtype, rows=None):
    rows = rows or terms[0][0].shape[0]
    width = terms[0][0].shape[1]
    steps = next(n for n in (4, 3, 2, 1) if rows % (16 * n) == 0)
    tile = rows // steps

    def body(*refs):
        total = refs[0][...].astype(floats)
        for ref in refs[1:-1]:
            total = total + ref[...].astype(floats)
        refs[-1][...] = total.astype(dtype)

    def spec(first):
        return pl.BlockSpec((tile, width), lambda i: (first // tile + i, 0))

    return pl.pallas_call(
        body,
        out_shape=jax.ShapeDtypeStruct((rows, width), dtype),
        grid=(steps,),
        in_specs=[spec(first) for _, first in terms],
        out_specs=spec(0),
        compiler_params=params(),
        cost_estimate=HEAVY,
    )(*(array for array, _ in terms))


def first_norm(tokens, gain, tiles, own):
    seq_len, width = tokens.shape
    part = seq_len // tiles

    def body(own_ref, tok_ref, gain_ref, out_ref, rows_ref, factor_ref):
        whole = tok_ref[...].astype(floats)
        inverse = lax.rsqrt(jnp.mean(whole * whole, axis=-1, keepdims=True) + epsilon)
        out_ref[...] = (whole * inverse * gain_ref[...]).astype(halves)
        factor_ref[...] = jnp.broadcast_to(inverse, factor_ref.shape)

        @pl.when(pl.program_id(0) == own_ref[0])
        def _():
            rows_ref[...] = tok_ref[...]

    return pl.pallas_call(
        body,
        out_shape=(
            jax.ShapeDtypeStruct((seq_len, width), halves),
            jax.ShapeDtypeStruct((part, width), tokens.dtype),
            jax.ShapeDtypeStruct((seq_len, 128), floats),
        ),
        grid_spec=pltpu.PrefetchScalarGridSpec(
            num_scalar_prefetch=1,
            grid=(tiles,),
            in_specs=[
                pl.BlockSpec((part, width), lambda i, own_ref: (i, 0)),
                pl.BlockSpec((1, width), lambda i, own_ref: (0, 0)),
            ],
            out_specs=(
                pl.BlockSpec((part, width), lambda i, own_ref: (i, 0)),
                pl.BlockSpec((part, width), lambda i, own_ref: (0, 0)),
                pl.BlockSpec((part, 128), lambda i, own_ref: (i, 0)),
            ),
        ),
        compiler_params=params(),
        cost_estimate=HEAVY,
    )(own, tokens, gain.reshape(1, width))


def tile_of(size):
    return max(step for step in range(128, 513, 128) if size % step == 0)


def gradient_blocks(lhs, rhs, order, half, tile=None, keep=None):
    sides, tokens, height = lhs.shape
    count = order.shape[0] // 2
    block = rhs.shape[1] // order.shape[0]
    tile = tile or tile_of(height)
    keep = keep or tile
    steps = height // tile

    def body(order_ref, lhs_ref, *refs):
        turned = lhs_ref[0].T
        for rhs_ref, out_ref in zip(refs[:count], refs[count:]):
            product = jnp.dot(turned, rhs_ref[...], preferred_element_type=floats)
            out_ref[...] = product[:keep].astype(halves)

    def column(j):
        return pl.BlockSpec(
            (tokens, block), lambda side, i, order_ref: (0, order_ref[half * count + j])
        )

    return pl.pallas_call(
        body,
        out_shape=[jax.ShapeDtypeStruct((sides * steps * keep, block), halves)] * count,
        grid_spec=pltpu.PrefetchScalarGridSpec(
            num_scalar_prefetch=1,
            grid=(sides, steps),
            in_specs=[
                pl.BlockSpec((1, tokens, tile), lambda side, i, order_ref: (side, 0, i)),
                *(column(j) for j in range(count)),
            ],
            out_specs=[
                pl.BlockSpec((keep, block), lambda side, i, order_ref: (side * steps + i, 0))
            ]
            * count,
        ),
        compiler_params=params(),
        cost_estimate=HEAVY,
    )(order, lhs, *([rhs] * count))


def matmul_across(lhs, rhs, first, count):
    tall, inner = lhs.shape
    tile = 256 if count % 256 == 0 and first % 256 == 0 else 128

    def body(lhs_ref, rhs_ref, out_ref):
        out_ref[...] = lax.dot_general(
            lhs_ref[...], rhs_ref[...], contract_last, preferred_element_type=floats
        )

    return pl.pallas_call(
        body,
        out_shape=jax.ShapeDtypeStruct((tall, count), floats),
        grid=(count // tile,),
        in_specs=[
            pl.BlockSpec((tall, inner), lambda j: (0, 0)),
            pl.BlockSpec((tile, inner), lambda j: (first // tile + j, 0)),
        ],
        out_specs=pl.BlockSpec((tall, tile), lambda j: (0, j)),
        compiler_params=params(),
        cost_estimate=HEAVY,
    )(lhs, rhs)


def halves_spec(parts, inner, tall, tile):
    half, part = tall // inner, tall // parts

    def put(places_ref, product, own_ref, other_ref):
        for a in range(parts):
            rows = product[a * part : (a + 1) * part]
            place = places_ref[a]

            @pl.when(place < parts // inner)
            def _():
                own_ref[pl.ds(pl.multiple_of(place * part, part), part)] = rows

            if inner > 1:

                @pl.when(place >= parts // inner)
                def _():
                    at = pl.multiple_of(place * part - half, part)
                    other_ref[pl.ds(at, part)] = rows.astype(halves)

    return half, pl.BlockSpec((half, tile), lambda j, p: (0, j)), put


def matmul_halves(lhs, rhs, places, inner, first=0, scaled=None):
    tall, depth = lhs.shape
    wide = rhs.shape[1]
    tile = 256 if wide % 256 == 0 else 128
    half, spec, put = halves_spec(places.shape[0], inner, tall, tile)

    def body(places_ref, lhs_ref, rhs_ref, *refs):
        product = jnp.dot(lhs_ref[...], rhs_ref[...], preferred_element_type=floats)
        put(places_ref, product, *refs[len(scaled or ()) :][:2])
        if scaled:
            array_ref, factor_ref, sums_ref = refs[0], refs[1], refs[-1]
            terms = product * array_ref[...].astype(floats) * factor_ref[:, :1]
            sums_ref[...] = jnp.sum(terms.reshape(tall // 8, 8, tile), axis=0)

    more_in, more_out, more_shapes = [], [], []
    if scaled:
        more_in = [
            pl.BlockSpec((tall, tile), lambda j, p: (0, j)),
            pl.BlockSpec(scaled[1].shape, lambda j, p: (0, 0)),
        ]
        more_out = [pl.BlockSpec((8, tile), lambda j, p: (0, j))]
        more_shapes = [jax.ShapeDtypeStruct((8, wide), floats)]
    return pl.pallas_call(
        body,
        out_shape=(
            jax.ShapeDtypeStruct((half, wide), floats),
            jax.ShapeDtypeStruct((half, wide), halves),
            *more_shapes,
        ),
        grid_spec=pltpu.PrefetchScalarGridSpec(
            num_scalar_prefetch=1,
            grid=(wide // tile,),
            in_specs=[
                pl.BlockSpec((tall, depth), lambda j, p: (0, 0)),
                pl.BlockSpec((depth, tile), lambda j, p: (first // depth, j)),
                *more_in,
            ],
            out_specs=(spec, spec, *more_out),
        ),
        compiler_params=params(),
        cost_estimate=HEAVY,
    )(places, lhs, rhs, *(scaled or ()))


def gated_forward(normed, weights):
    tokens, inner = normed.shape
    hidden = weights.shape[1] // 2
    tile = 256 if hidden % 256 == 0 else 128
    steps = hidden // tile

    def body(in_ref, gate_ref, up_ref, gate_out, up_out, hidden_out):
        gate = jnp.dot(in_ref[...], gate_ref[...], preferred_element_type=floats)
        up = jnp.dot(in_ref[...], up_ref[...], preferred_element_type=floats)
        gate_out[...] = gate
        up_out[...] = up
        hidden_out[...] = (gelu(gate) * up).astype(halves)

    column = pl.BlockSpec((tokens, tile), lambda j: (0, j))
    return pl.pallas_call(
        body,
        out_shape=(
            jax.ShapeDtypeStruct((tokens, hidden), floats),
            jax.ShapeDtypeStruct((tokens, hidden), floats),
            jax.ShapeDtypeStruct((tokens, hidden), halves),
        ),
        grid=(steps,),
        in_specs=[
            pl.BlockSpec((tokens, inner), lambda j: (0, 0)),
            pl.BlockSpec((inner, tile), lambda j: (0, j)),
            pl.BlockSpec((inner, tile), lambda j: (0, steps + j)),
        ],
        out_specs=(column, column, column),
        compiler_params=params(),
        cost_estimate=HEAVY,
    )(normed, weights, weights)


def gated_backward(cotangent, down, gate, up):
    tokens, inner = cotangent.shape
    hidden = down.shape[0]
    tile = 256 if hidden % 256 == 0 else 128

    def body(cot_ref, down_ref, gate_ref, up_ref, out_ref):
        back = lax.dot_general(
            cot_ref[...], down_ref[...], contract_last, preferred_element_type=floats
        )
        active, slope = gelu_parts(gate_ref[...])
        out_ref[0] = (back * up_ref[...] * slope).astype(halves)
        out_ref[1] = (back * active).astype(halves)

    column = pl.BlockSpec((tokens, tile), lambda j: (0, j))
    return pl.pallas_call(
        body,
        out_shape=jax.ShapeDtypeStruct((2, tokens, hidden), halves),
        grid=(hidden // tile,),
        in_specs=[
            pl.BlockSpec((tokens, inner), lambda j: (0, 0)),
            pl.BlockSpec((tile, inner), lambda j: (j, 0)),
            column,
            column,
        ],
        out_specs=pl.BlockSpec((2, tokens, tile), lambda j: (0, 0, j)),
        compiler_params=params(),
        cost_estimate=HEAVY,
    )(cotangent, down, gate, up)


def pair_halves(pair, weights, places, inner):
    _, tall, hidden = pair.shape
    wide = weights.shape[0]
    tile = 256 if wide % 256 == 0 else 128
    half, spec, put = halves_spec(places.shape[0], inner, tall, tile)

    def body(places_ref, pair_ref, gate_ref, up_ref, own_ref, other_ref):
        product = 0.0
        for side, ref in enumerate((gate_ref, up_ref)):
            product = product + lax.dot_general(
                pair_ref[side], ref[...], contract_last, preferred_element_type=floats
            )
        put(places_ref, product, own_ref, other_ref)

    weight = lambda side: pl.BlockSpec((tile, hidden), lambda j, p: (j, side))
    return pl.pallas_call(
        body,
        out_shape=(
            jax.ShapeDtypeStruct((half, wide), floats),
            jax.ShapeDtypeStruct((half, wide), halves),
        ),
        grid_spec=pltpu.PrefetchScalarGridSpec(
            num_scalar_prefetch=1,
            grid=(wide // tile,),
            in_specs=[pl.BlockSpec((2, tall, hidden), lambda j, p: (0, 0, 0)), weight(0), weight(1)],
            out_specs=(spec, spec),
        ),
        compiler_params=params(),
        cost_estimate=HEAVY,
    )(places, pair, weights, weights)


def segment_of(places, ends_ref):
    segment = jnp.zeros(places.shape, jnp.int32)
    for j in range(ends_ref.shape[0] - 1):
        segment = segment + (places >= ends_ref[j]).astype(jnp.int32)
    return segment


def same_behind(places, ends_ref, offset):
    agree = segment_of(places, ends_ref) == segment_of(places - offset, ends_ref)
    return jnp.logical_and(agree, places >= offset).astype(floats)


def same_ahead(places, ends_ref, offset, seq_len):
    agree = segment_of(places, ends_ref) == segment_of(places + offset, ends_ref)
    return jnp.logical_and(agree, places + offset < seq_len).astype(floats)


def lane_chunks(width):
    step = 256 if width % 256 == 0 else 128
    return [slice(at, at + step) for at in range(0, width, step)]


def gate_values(pre_a, pre_i, decay8):
    rate = jax.nn.sigmoid(pre_a)
    admit = jax.nn.sigmoid(pre_i)
    power = decay8 * rate
    alpha = jnp.exp(-power)
    twice = 2.0 * power
    series = 1.0 - twice * (1.0 / 7.0)
    for order in (6.0, 5.0, 4.0, 3.0, 2.0):
        series = 1.0 - (twice * (1.0 / order)) * series
    raw = jnp.where(twice < 0.5, twice * series, 1.0 - alpha * alpha)
    one_minus = jnp.maximum(raw, floor_value)
    inverse = lax.rsqrt(one_minus)
    return rate, admit, alpha, raw, one_minus * inverse, inverse


def gelu_parts(value):
    square = value * value
    bend = jnp.tanh(gelu_root * (value + gelu_cube * (square * value)))
    half = 0.5 * (1.0 + bend)
    slope = half + 0.5 * value * (1.0 - bend * bend) * (
        gelu_root * (1.0 + 3.0 * gelu_cube * square)
    )
    return value * half, slope


def gelu(value):
    return gelu_parts(value)[0]


def recur_forward(branches, doc_ends, vectors, gates, tiles):
    seq_len, lanes = branches.shape[0], branches.shape[1] // 2
    part = seq_len // tiles
    chunks = lane_chunks(lanes)

    def body(
        ends_ref, x_ref, y_ref, vec_ref, gate_ref,
        mixed_ref, conv_ref, pre_ref, prev_ref, xs, carry,
    ):
        tile = pl.program_id(0)

        @pl.when(tile == 0)
        def _():
            xs[0:8] = jnp.zeros((8, lanes), floats)
            carry[...] = jnp.zeros_like(carry)

        xs[8 : 8 + part] = x_ref[...]
        rows = lax.broadcasted_iota(jnp.int32, (CHUNK, 1), 0)

        def convolve(c, _):
            at = pl.multiple_of(c * CHUNK, CHUNK)
            here = tile * part + at + rows
            same = [same_behind(here, ends_ref, k) for k in range(1, 4)]
            for lane in chunks:
                window = xs[pl.ds(at, CHUNK + 8), lane]
                total = vec_ref[4:5, lane] + vec_ref[0:1, lane] * window[8:]
                for k in range(1, 4):
                    moved = pltpu.roll(window, k, 0)[8:]
                    total = total + vec_ref[k : k + 1, lane] * moved * same[k - 1]
                conv_ref[pl.ds(at, CHUNK), lane] = total.astype(halves)
            return 0

        lax.fori_loop(0, part // CHUNK, convolve, 0)
        xs[0:8] = xs[part : part + 8]
        pre_ref[...] = jnp.dot(conv_ref[...], gate_ref[...], preferred_element_type=floats)

        def advance(c, entering):
            at = pl.multiple_of(c * CHUNK, CHUNK)
            here = tile * part + at + rows
            fresh = 1.0 - same_behind(here, ends_ref, 1)
            leaving = []
            for state, lane in zip(entering, chunks):
                span = lane.stop - lane.start
                shift_lane = slice(lane.start + lanes, lane.stop + lanes)
                pre_a = pre_ref[pl.ds(at, CHUNK), lane] + vec_ref[6:7, lane]
                pre_i = pre_ref[pl.ds(at, CHUNK), shift_lane] + vec_ref[7:8, lane]
                pre_ref[pl.ds(at, CHUNK), lane] = pre_a
                pre_ref[pl.ds(at, CHUNK), shift_lane] = pre_i
                conv_in = conv_ref[pl.ds(at, CHUNK), lane].astype(floats)
                _, admit, alpha, _, root, _ = gate_values(pre_a, pre_i, vec_ref[5:6, lane])
                keep = 1.0 - fresh
                coef = alpha * keep
                drive = (fresh + root * keep) * admit * conv_in
                index = lax.broadcasted_iota(jnp.int32, (CHUNK, span), 0)
                for d in (1, 2, 4):
                    inside = (index & 7) >= d
                    drive = jnp.where(inside, drive + coef * pltpu.roll(drive, d, 0), drive)
                    coef = jnp.where(inside, coef * pltpu.roll(coef, d, 0), coef)
                groups = []
                first = state
                for g in range(CHUNK // 8):
                    group = slice(g * 8, g * 8 + 8)
                    groups.append(coef[group] * state + drive[group])
                    state = groups[-1][7:8]
                states = jnp.concatenate(groups, axis=0)
                prev_ref[pl.ds(at, CHUNK), lane] = jnp.where(
                    index == 0, first, pltpu.roll(states, 1, 0)
                )
                mixed = states * gelu(y_ref[pl.ds(at, CHUNK), lane])
                mixed_ref[pl.ds(at, CHUNK), lane] = mixed.astype(halves)
                leaving.append(state)
            return tuple(leaving)

        ended = lax.fori_loop(
            0, part // CHUNK, advance, tuple(carry[0:1, lane] for lane in chunks)
        )
        for state, lane in zip(ended, chunks):
            carry[0:1, lane] = state

    own = lambda column: pl.BlockSpec((part, lanes), lambda i, e: (i, column))
    straight = lambda width: pl.BlockSpec((part, width), lambda i, e: (i, 0))
    whole = lambda array: pl.BlockSpec(array.shape, lambda i, e: (0, 0))
    return pl.pallas_call(
        body,
        out_shape=(
            jax.ShapeDtypeStruct((seq_len, lanes), halves),
            jax.ShapeDtypeStruct((seq_len, lanes), halves),
            jax.ShapeDtypeStruct((seq_len, 2 * lanes), floats),
            jax.ShapeDtypeStruct((seq_len, lanes), floats),
        ),
        grid_spec=pltpu.PrefetchScalarGridSpec(
            num_scalar_prefetch=1,
            grid=(tiles,),
            in_specs=[own(0), own(1), whole(vectors), whole(gates)],
            out_specs=(own(0), straight(lanes), straight(2 * lanes), straight(lanes)),
            scratch_shapes=[pltpu.VMEM((part + 8, lanes), floats), pltpu.VMEM((8, lanes), floats)],
        ),
        compiler_params=params(),
        cost_estimate=HEAVY,
    )(doc_ends, branches, branches, vectors, gates)


def recur_backward(back_mixed, branches, conv_in, pre, previous, doc_ends, vectors, gates, tiles):
    seq_len, lanes = conv_in.shape
    part = seq_len // tiles
    chunks = lane_chunks(lanes)
    steps = part // CHUNK

    def body(
        ends_ref, bm_ref, x_ref, y_ref, conv_ref, pre_ref, prev_ref, vec_ref, gate_ref,
        bxy_ref, bai_ref, sums_ref, ahead, sums, carry,
    ):
        tile = tiles - 1 - pl.program_id(0)

        @pl.when(pl.program_id(0) == 0)
        def _():
            ahead[part : part + 8] = jnp.zeros((8, lanes), floats)
            sums[...] = jnp.zeros_like(sums)
            carry[...] = jnp.zeros_like(carry)

        rows = lax.broadcasted_iota(jnp.int32, (CHUNK, 1), 0)

        def add_rows(which, lane, value):
            for g in range(CHUNK // 8):
                sums[which * 8 : which * 8 + 8, lane] += value[g * 8 : g * 8 + 8]

        def retreat(c, entering):
            at = pl.multiple_of((steps - 1 - c) * CHUNK, CHUNK)
            span_rows = pl.ds(at, CHUNK)
            here = tile * part + at + rows
            keep = same_behind(here, ends_ref, 1)
            fresh = 1.0 - keep
            leaving = []
            for (back_next, coef_next), lane in zip(entering, chunks):
                span = lane.stop - lane.start
                shift_lane = slice(lane.start + lanes, lane.stop + lanes)
                decay8 = vec_ref[5:6, lane]
                rate, admit, alpha, raw, root, inverse = gate_values(
                    pre_ref[span_rows, lane], pre_ref[span_rows, shift_lane], decay8
                )
                conv = conv_ref[span_rows, lane].astype(floats)
                before = prev_ref[span_rows, lane]
                scale_in = fresh + root * keep
                coef = alpha * keep
                driven = scale_in * admit
                states = coef * before + driven * conv
                active, slope = gelu_parts(y_ref[span_rows, lane])
                back_mix = bm_ref[span_rows, lane]
                bxy_ref[span_rows, shift_lane] = (back_mix * states * slope).astype(halves)
                index = lax.broadcasted_iota(jnp.int32, (CHUNK, span), 0)
                back = back_mix * active
                chain = jnp.where(index == CHUNK - 1, coef_next, pltpu.roll(coef, CHUNK - 1, 0))
                for d in (1, 2, 4):
                    inside = (index & 7) < 8 - d
                    back = jnp.where(inside, back + chain * pltpu.roll(back, CHUNK - d, 0), back)
                    chain = jnp.where(inside, chain * pltpu.roll(chain, CHUNK - d, 0), chain)
                groups = []
                for g in reversed(range(CHUNK // 8)):
                    group = slice(g * 8, g * 8 + 8)
                    groups.insert(0, back[group] + chain[group] * back_next)
                    back_next = groups[0][0:1]
                back_state = jnp.concatenate(groups, axis=0)
                through = back_state * conv
                bound = jnp.where(raw > floor_value, through * admit * alpha * inverse, 0.0)
                back_alpha = (back_state * before - bound) * keep * alpha
                add_rows(5, lane, back_alpha * rate)
                back_a = (back_alpha * (-decay8) * rate * (1.0 - rate)).astype(halves)
                back_i = (through * scale_in * admit * (1.0 - admit)).astype(halves)
                add_rows(6, lane, back_a.astype(floats))
                add_rows(7, lane, back_i.astype(floats))
                bai_ref[span_rows, lane] = back_a
                bai_ref[span_rows, shift_lane] = back_i
                ahead[span_rows, lane] = back_state * driven
                leaving.append((back_next, coef[0:1]))
            return tuple(leaving)

        ended = lax.fori_loop(
            0, steps, retreat, tuple((carry[0:1, lane], carry[8:9, lane]) for lane in chunks)
        )
        for (back_next, coef_next), lane in zip(ended, chunks):
            carry[0:1, lane] = back_next
            carry[8:9, lane] = coef_next

        ahead[0:part] += lax.dot_general(
            bai_ref[...], gate_ref[...], contract_last, preferred_element_type=floats
        )

        def convolve(c, _):
            at = pl.multiple_of(c * CHUNK, CHUNK)
            here = tile * part + at + rows
            same = [same_ahead(here, ends_ref, k, seq_len) for k in range(1, 4)]
            for lane in chunks:
                window = ahead[pl.ds(at, CHUNK + 8), lane]
                x_part = x_ref[pl.ds(at, CHUNK), lane]
                direct = window[:CHUNK]
                back_x = vec_ref[0:1, lane] * direct
                add_rows(0, lane, x_part * direct)
                add_rows(4, lane, direct)
                for k in range(1, 4):
                    moved = pltpu.roll(window, CHUNK + 8 - k, 0)[:CHUNK] * same[k - 1]
                    back_x = back_x + vec_ref[k : k + 1, lane] * moved
                    add_rows(k, lane, x_part * moved)
                bxy_ref[pl.ds(at, CHUNK), lane] = back_x.astype(halves)
            return 0

        lax.fori_loop(0, steps, convolve, 0)
        ahead[part : part + 8] = ahead[0:8]

        @pl.when(pl.program_id(0) == tiles - 1)
        def _():
            for which in range(8):
                sums_ref[which : which + 1] = jnp.sum(
                    sums[which * 8 : which * 8 + 8], axis=0, keepdims=True
                )

    own = lambda width, column: pl.BlockSpec((part, width), lambda i, e: (tiles - 1 - i, column))
    straight = lambda width: pl.BlockSpec((part, width), lambda i, e: (tiles - 1 - i, 0))
    whole = lambda array: pl.BlockSpec(array.shape, lambda i, e: (0, 0))
    return pl.pallas_call(
        body,
        out_shape=(
            jax.ShapeDtypeStruct((seq_len, 2 * lanes), halves),
            jax.ShapeDtypeStruct((seq_len, 2 * lanes), halves),
            jax.ShapeDtypeStruct((8, lanes), floats),
        ),
        grid_spec=pltpu.PrefetchScalarGridSpec(
            num_scalar_prefetch=1,
            grid=(tiles,),
            in_specs=[
                own(lanes, 0), own(lanes, 0), own(lanes, 1),
                straight(lanes), straight(2 * lanes), straight(lanes),
                whole(vectors), whole(gates),
            ],
            out_specs=(
                own(2 * lanes, 0), straight(2 * lanes), pl.BlockSpec((8, lanes), lambda i, e: (0, 0)),
            ),
            scratch_shapes=[
                pltpu.VMEM((part + 8, lanes), floats),
                pltpu.VMEM((64, lanes), floats),
                pltpu.VMEM((16, lanes), floats),
            ],
        ),
        compiler_params=params(),
        cost_estimate=HEAVY,
    )(doc_ends, back_mixed, branches, branches, conv_in, pre, previous, vectors, gates)


def rms_norm(inputs, scales):
    return inputs * lax.rsqrt(jnp.mean(inputs * inputs, axis=-1, keepdims=True) + epsilon) * scales


def inner_of(count):
    return max(d for d in range(1, count + 1) if count % d == 0 and d * d <= count)


def on_device(
    tokens,
    doc_lengths,
    gain_mix,
    value_weight,
    branch_weight,
    conv_weight,
    conv_bias,
    recur_gate,
    input_gate,
    recur_bias,
    input_bias,
    decay_param,
    out_weight,
    gain_ffn,
    gate_weight,
    up_weight,
    down_weight,
    cotangent,
):
    seq_len, _, width = tokens.shape
    heads, head_width = recur_gate.shape[:2]
    channels = value_weight.shape[1]
    hidden_width = gate_weight.shape[1]
    lanes = round_up(channels, 128)
    sent = round_up(channels, 16)
    dp = Ring(DP, inner_of(lax.axis_size(DP)))
    parts = lax.axis_size(CHAN)
    part = seq_len // parts
    block = width // dp.count
    order = dp.order()
    chan = lax.axis_index(CHAN)
    own_tile = chan.reshape(1).astype(jnp.int32)
    cores = 2 if parts % 2 == 0 else 1
    chips = parts // cores
    tiles = jnp.arange(parts, dtype=jnp.int32)
    row_places = ((tiles - chan) % cores) * chips + (tiles // cores - chan // cores) % chips
    doc_ends = jnp.cumsum(doc_lengths[0])
    plan = Plan()
    compute = plan.compute

    def gather_weight(own, count, flip, bias, after, put):
        blocks = ring_gather(plan, dp, own, count, flip, bias, after)
        full = None
        for distance in sorted(blocks, key=lambda d: min(d, dp.count - d)):

            def extend(v, before=full, piece=blocks[distance], slot=dp.slots[distance]):
                return put(
                    None if before is None else v[before], v[piece], order[slot : slot + 1]
                )

            needs = [blocks[distance]] if full is None else [full, blocks[distance]]
            full = compute(3.5, needs, extend)
        return full, blocks

    def put_mix(full, piece, at):
        return place(
            full, piece, at, (3 * lanes, width), 3,
            (sent, block), lambda i, at: (i, 0),
            (lanes, block), lambda i, at: (i, at[0]),
        )

    def put_rows(full, piece, at):
        return place(
            full, piece, at, (width, 2 * hidden_width), 2,
            (block, hidden_width), lambda i, at: (0, i),
            (block, hidden_width), lambda i, at: (at[0], i),
        )

    def put_columns(full, piece, at):
        tall = hidden_width // 2
        return place(
            full, piece, at, (hidden_width, width), 2,
            (tall, block), lambda i, at: (i, 0),
            (tall, block), lambda i, at: (i, at[0]),
        )

    def mix_of(value, branch, out):
        return jnp.concatenate(
            [pad_dim(array, 0, sent) for array in (value.T, branch.T, out)], axis=0
        )

    mix = compute(3.0, [], lambda v: mix_of(value_weight, branch_weight, out_weight), 8.0)
    both_own = compute(2.0, [], lambda v: jnp.concatenate([gate_weight, up_weight], axis=1), 1.0)
    mix_full, mix_blocks = gather_weight(mix, 3 * sent * block, False, 9.0, {}, put_mix)
    far = dp.count // 2
    both_full, both_blocks = gather_weight(
        both_own, 2 * hidden_width * block, True, 8.0,
        {(AHEAD, 0): mix_blocks[far], (BACK, 0): mix_blocks[far + 1]}, put_rows,
    )
    down_own = compute(0.5, [], lambda v: down_weight)
    down_full, down_blocks = gather_weight(
        down_own, hidden_width * block, False, 7.0,
        {(AHEAD, 0): both_blocks[far - 1], (BACK, 0): both_blocks[far]}, put_columns,
    )

    def spread(gate):
        total = 0.0
        for h in range(heads):
            low = h * head_width
            total = total + jnp.pad(gate[h], ((low, lanes - low - head_width),) * 2)
        return total

    def small_parameters(v):
        gates = jnp.concatenate([spread(recur_gate), spread(input_gate)], axis=1)
        vectors = [
            conv_weight,
            conv_bias[None],
            decay_scale * jax.nn.softplus(decay_param)[None],
            recur_bias[None],
            input_bias[None],
        ]
        return gates, pad_dim(jnp.concatenate(vectors, axis=0), 1, lanes)

    small = compute(8.0, [], small_parameters)

    def cross(value, step):
        pairs = [
            (x * cores + c, ((x + step) % chips) * cores + c)
            for x in range(chips)
            for c in range(cores)
        ]
        return lax.ppermute(value, CHAN, pairs)

    def swap(value):
        pairs = [(x * cores + c, x * cores + (c + 1) % cores) for x in range(chips) for c in range(cores)]
        return lax.ppermute(value, CHAN, pairs)

    def gather_rows(own):
        return plan.add(
            CHIPS, 33.0, [own], lambda v: lax.all_gather(v[own], CHAN, axis=0, tiled=True)
        )

    def reduce_rows(product, after=()):
        terms = []
        if cores > 1:
            terms = [plan.add(TWIN, 9.0, [product, *after], lambda v: swap(v[product][1]), 3.0)]
        passing = []
        for s in reversed(range(chips)):

            def add(v, s=s, passing=tuple(passing)):
                pieces = [(v[product][0], s * part), *((v[term], s * part) for term in terms)]
                pieces += [(v[term], 0) for term in passing]
                return add_up(pieces, halves if s else floats, part)

            made = compute(3.0, [product, *terms, *passing], add, 10.0)
            if s:
                passing = [
                    plan.add(CROSS, 26.5, [made], lambda v, made=made: cross(v[made], 1), 3.0)
                ]
        return made

    def small_total(source, axes):
        for axis in axes:
            count = lax.axis_size(axis)
            assert count & (count - 1) == 0
            bit = 1
            while bit < count:
                pairs = [(i, i ^ bit) for i in range(count)]

                def send(v, source=source, axis=axis, pairs=pairs):
                    return lax.ppermute(v[source], axis, pairs)

                other = plan.add(SMALL, 18.0 if axis == DP else 8.0, [source], send)

                def add(v, source=source, other=other):
                    return v[source] + v[other]

                source = compute(0.5, [source, other], add)
                bit *= 2
        return source

    norm_in = compute(
        5.0, [], lambda v: first_norm(tokens.reshape(seq_len, width), gain_mix, parts, own_tile)
    )
    cot = compute(1.5, [], lambda v: cotangent.reshape(part, width))
    cot_full = gather_rows(cot)
    branches = compute(
        10.8,
        [norm_in, mix_full],
        lambda v: matmul_across(v[norm_in][0], v[mix_full], 0, 2 * lanes),
    )
    recur = compute(
        20.2,
        [branches, small],
        lambda v: recur_forward(v[branches], doc_ends, v[small][1], v[small][0], parts),
    )
    mixed = compute(0.0, [recur], lambda v: v[recur][0], 30.0)
    mixed_out = compute(
        9.2,
        [mixed, mix_full],
        lambda v: matmul_halves(v[mixed], v[mix_full], row_places, cores, 2 * lanes),
    )
    branch_out = reduce_rows(mixed_out)

    def middle_of(v):
        residual = v[norm_in][1].astype(floats) + v[branch_out]
        return residual, rms_norm(residual, gain_ffn).astype(halves)

    middle = compute(3.0, [norm_in, branch_out], middle_of)
    mid = compute(0.0, [middle], lambda v: v[middle][1], 30.0)
    mid_full = gather_rows(mid)

    gated = compute(
        19.7,
        [mid_full, both_full],
        lambda v: gated_forward(v[mid_full], v[both_full]),
    )
    hidden = compute(0.0, [gated], lambda v: v[gated][2], 30.0)

    def gradient(lhs, lhs_of, rhs, rhs_of, cost, bias, tile=None, keep=None):
        return [
            compute(
                cost,
                [lhs, rhs],
                lambda v, h=h: gradient_blocks(lhs_of(v), rhs_of(v), order, h, tile, keep),
                bias - 3 * h,
            )
            for h in range(2)
        ]

    grad_down = ring_reduce(
        plan,
        dp,
        gradient(
            hidden, lambda v: v[hidden][None], cot_full, lambda v: v[cot_full], 7.0, 6.0
        ),
        hidden_width * block,
        lambda total: total,
        after=[down_blocks[far]],
    )
    back_both = compute(
        14.7,
        [gated, cot_full, down_full],
        lambda v: gated_backward(v[cot_full], v[down_full], *v[gated][:2]),
    )
    back_product = compute(
        20.5,
        [back_both, both_full],
        lambda v: pair_halves(v[back_both], v[both_full], row_places, cores),
    )
    back_mid = reduce_rows(back_product)
    grad_both = ring_reduce(
        plan,
        dp,
        gradient(back_both, lambda v: v[back_both], mid_full, lambda v: v[mid_full], 11.0, 0.0),
        2 * hidden_width * block,
        lambda total: (total[:hidden_width].T, total[hidden_width:].T),
        True,
    )
    ffn_product = compute(
        12.0,
        [hidden, down_full],
        lambda v: matmul_halves(v[hidden], v[down_full], row_places, cores),
        -2.0,
    )

    def norm_back(inputs, gain, back):
        scale = lax.rsqrt(jnp.mean(inputs * inputs, axis=-1, keepdims=True) + epsilon)
        scaled = back * gain
        mean = jnp.mean(scaled * inputs, axis=-1, keepdims=True)
        through = scale * scaled - inputs * (scale * scale * scale * mean)
        return through

    def back_middle_of(v):
        residual, back = v[middle][0], v[back_mid]
        scale = lax.rsqrt(jnp.mean(residual * residual, axis=-1, keepdims=True) + epsilon)
        gain = jnp.sum((back * residual * scale).reshape(part // 8, 8, width), axis=0)
        back = v[cot].astype(floats) + norm_back(residual, gain_ffn, back)
        return back, back.astype(halves), gain

    back_middle = compute(4.0, [middle, back_mid, cot], back_middle_of)
    back_resid = compute(0.0, [back_middle], lambda v: v[back_middle][1], 30.0)
    branch_full = gather_rows(back_resid)
    ffn_out = reduce_rows(ffn_product, [branch_full])
    output = compute(
        4.0, [middle, ffn_out], lambda v: (v[middle][0] + v[ffn_out]).astype(halves), -1.0
    )
    back_mixed = compute(
        6.7,
        [branch_full, mix_full],
        lambda v: matmul_across(v[branch_full], v[mix_full], 2 * lanes, lanes),
    )
    recur_back = compute(
        26.5,
        [back_mixed, branches, recur, small],
        lambda v: recur_backward(
            v[back_mixed], v[branches], *v[recur][1:], doc_ends, v[small][1], v[small][0], parts
        ),
    )
    grad_out = ring_reduce(
        plan,
        dp,
        gradient(
            mixed, lambda v: v[mixed][None], branch_full, lambda v: v[branch_full],
            3.5, 2.0, lanes, sent,
        ),
        sent * block,
        lambda total: total[:channels],
        True,
    )
    grad_pair = ring_reduce(
        plan,
        dp,
        gradient(
            recur_back, lambda v: v[recur_back][0][None], norm_in, lambda v: v[norm_in][0],
            5.5, 4.0, lanes, sent,
        ),
        2 * sent * block,
        lambda total: (total[:channels].T, total[sent : sent + channels].T),
    )
    back_pair = compute(
        13.0,
        [recur_back, mix_full, norm_in],
        lambda v: matmul_halves(
            v[recur_back][0], v[mix_full], row_places, cores, 0,
            (tokens.reshape(seq_len, width), v[norm_in][2]),
        ),
        2.0,
    )
    back_norm_in = reduce_rows(back_pair)

    def back_first_of(v):
        through = norm_back(v[norm_in][1].astype(floats), gain_mix, v[back_norm_in])
        return v[back_middle][0] + through

    back_first = compute(5.0, [norm_in, back_norm_in, back_middle], back_first_of)

    def gate_grads_of(v):
        whole = lax.dot_general(
            v[recur][1], v[recur_back][1], contract_first, preferred_element_type=floats
        )
        return jnp.stack(
            [
                whole[
                    h * head_width : (h + 1) * head_width,
                    side * lanes + h * head_width : side * lanes + (h + 1) * head_width,
                ]
                for side in range(2)
                for h in range(heads)
            ]
        )

    gate_terms = compute(
        5.0, [recur, recur_back], lambda v: gate_grads_of(v).astype(halves), 3.5
    )
    gate_sums = plan.add(CHIPS, 60.0, [gate_terms], lambda v: lax.psum(v[gate_terms], DP), 3.0)
    gate_result = compute(
        4.0, [gate_sums], lambda v: tuple(jnp.split(v[gate_sums].astype(floats), 2))
    )
    def both_gains(v):
        gains = [jnp.sum(terms, axis=0).reshape(8, -1) for terms in (v[back_middle][2], v[back_pair][2])]
        return jnp.concatenate(gains, axis=1)

    gain_rows = small_total(compute(2.0, [back_middle, back_pair], both_gains, 1.0), [CHAN])
    sums = small_total(
        compute(
            1.0,
            [recur_back, gain_rows],
            lambda v: jnp.concatenate([v[recur_back][2], v[gain_rows]], axis=1),
        ),
        [DP],
    )

    def sum_results_of(v):
        total = v[sums][:, :channels]
        decay = total[5] * (-decay_scale * jax.nn.sigmoid(decay_param))
        gains = v[sums][:, lanes:]
        return (
            total[:4], total[4], total[6], total[7], decay,
            gains[:, : width // 8].reshape(width), gains[:, width // 8 :].reshape(width),
        )

    sum_results = compute(3.0, [sums], sum_results_of)

    done = plan.execute(
        [
            output, back_first, grad_pair, grad_out, sum_results, gate_result,
            grad_both, grad_down,
        ]
    )
    output, first, (value, branch), out, summed, (recur, admit), (gate, up), down = done
    return (
        output.reshape(part, 1, width),
        first.reshape(part, 1, width),
        summed[6],
        value,
        branch,
        summed[0],
        summed[1],
        recur,
        admit,
        summed[2],
        summed[3],
        summed[4],
        out,
        summed[5],
        gate,
        up,
        down,
    )


def solution(mesh):
    tokens, split, columns = P(None, DP, None), P(DP, CHAN), P(CHAN, DP)
    own, channels, heads = P(CHAN, DP, None), P(CHAN), P(CHAN, None, None)
    in_specs = (
        tokens, P(DP, None), P(), split, split, P(None, CHAN), channels, heads, heads,
        channels, channels, channels, columns, P(), split, split, columns, own,
    )
    out_specs = (
        own, own, P(), split, split, P(None, CHAN), channels, heads, heads,
        channels, channels, channels, columns, P(), split, split, columns,
    )
    return jax.shard_map(
        on_device, mesh=mesh, in_specs=in_specs, out_specs=out_specs, check_vma=False
    )
```

```python
from functools import partial

import jax
import jax.numpy as jnp
from jax import lax
from jax.experimental import pallas as pl
from jax.experimental.pallas import tpu as pltpu
from jax.sharding import PartitionSpec as P

epsilon = 1e-06
decay_scale = 8.0
floor_value = 0.0001
gelu_root = 0.7978845608
gelu_cube = 0.044715
floats = jnp.float32
halves = jnp.bfloat16
contract_last = (((1,), (1,)), ((), ()))
contract_first = (((0,), (0,)), ((), ()))
CHUNK = 16
DP, CHAN = "dp", "chan"
VMEM_BYTES = 48 * 1024 * 1024
HEAVY = pl.CostEstimate(flops=2 * 10**11, bytes_accessed=1, transcendentals=0)


def round_up(number, unit):
    return -(-number // unit) * unit


def pad_dim(array, axis, size):
    widths = [(0, 0)] * array.ndim
    widths[axis] = (0, size - array.shape[axis])
    return jnp.pad(array, widths)


class Ring:
    def __init__(self, axis, inner):
        self.axis = axis
        self.count = lax.axis_size(axis)
        outer = self.count // inner
        self.path = [(o, 0) for o in range(outer)]
        for n, o in enumerate(reversed(range(outer))):
            columns = list(range(1, inner))
            self.path += [(o, i) for i in (reversed(columns) if n % 2 else columns)]
        self.path = [o * inner + i for o, i in self.path]
        spots = [self.path.index(i) for i in range(self.count)]
        self.spot = self.look(spots, lax.axis_index(axis))
        far = self.count // 2
        self.distances = [far]
        for j in range(1, far):
            self.distances += [far + j, far - j]
        self.distances += [0]
        self.slots = {distance: j for j, distance in enumerate(self.distances)}

    def look(self, table, index):
        return sum(jnp.where(index == i, entry, 0) for i, entry in enumerate(table))

    def hop(self, value, step):
        pairs = [
            (self.path[n], self.path[(n + step) % self.count]) for n in range(self.count)
        ]
        return lax.ppermute(value, self.axis, pairs)

    def order(self):
        ahead = self.look(self.distances, jnp.arange(self.count, dtype=jnp.int32))
        return self.look(self.path, (self.spot + ahead) % self.count).astype(jnp.int32)

    def ways(self, flip):
        ahead = (self.count - 1) // 2 if flip else self.count // 2
        return [
            (AHEAD, list(range(1, ahead + 1)), -1),
            (BACK, list(range(self.count - 1, ahead, -1)), 1),
        ]


LINK_RATE = 46e3
HOP_COST = 3.5
EARLY = 4.0
QUEUED = 2.5
CORE, AHEAD, BACK, CHIPS, CROSS, TWIN, SMALL = range(7)
DEPTHS = {AHEAD: 1, BACK: 1, CHIPS: 9, CROSS: 1, TWIN: 1, SMALL: 2}
STARTS = {AHEAD: 1.5, BACK: 0.8, CHIPS: 0.5, CROSS: 1.5, TWIN: 1.5, SMALL: 2.0}
HOPPING = (AHEAD, BACK, CROSS, TWIN, SMALL)
HOPS = 5
MARGINS = {CORE: 3.0, AHEAD: 0.5, BACK: 0.5, CHIPS: 1.0, CROSS: 0.5, TWIN: 0.5, SMALL: 2.0}


class Task:
    def __init__(self, number, resource, cost, needs, run, bias):
        self.number, self.resource, self.cost, self.needs = number, resource, cost, needs
        self.run, self.bias, self.level, self.users = run, bias, 0.0, []


class Plan:
    def __init__(self):
        self.tasks, self.log = [], []

    def add(self, resource, cost, needs, run, bias=0.0):
        task = Task(len(self.tasks), resource, cost, list(needs), run, bias)
        self.tasks.append(task)
        return task

    def compute(self, cost, needs, run, bias=0.0):
        return self.add(CORE, cost, needs, run, bias)

    def levels(self):
        for task in self.tasks:
            for need in task.needs:
                need.users.append(task)
        for task in reversed(self.tasks):
            task.level = task.cost + max([user.level for user in task.users], default=0.0)

    def execute(self, results):
        self.levels()
        waiting = sorted(self.tasks, key=lambda task: (-task.bias, -task.level))
        values, flying, free, shown = {}, {}, {}, set()
        now, fresh = 0.0, False

        def when(task):
            times = [
                0.0 if need in values else flying[need][0] if need in flying else None
                for need in task.needs
            ]
            if None in times:
                return None
            late = max(times, default=0.0)
            return late + MARGINS[task.resource] if late > 0.0 else 0.0

        def issue(task):
            nonlocal fresh
            ended = [need for need in task.needs if need in flying]
            if task.resource in HOPPING:
                under = sorted(
                    (end, other.number, other)
                    for other, (end, _) in flying.items()
                    if other.resource in HOPPING and other not in ended
                )
                ended += [other for _, _, other in under[: max(0, len(under) + 1 - HOPS)]]
            for need in ended:
                values[need] = flying.pop(need)[1]
                self.log.append((now, 1, need))
                fresh = True
            if fresh:
                wanted = {need for other in waiting for need in other.needs}
                first = {done for done in values if done in results} - shown
                names = sorted(
                    {done for done in values if done in wanted} | first,
                    key=lambda done: done.number,
                )
                tied = lax.optimization_barrier(tuple(values[done] for done in names))
                values.update(zip(names, tied))
                shown.update(first)
                fresh = False
            waiting.remove(task)
            self.log.append((now, 0, task))
            return task.run(values)

        while waiting:
            wakes, chosen = [], None
            for task in waiting:
                at, link = when(task), task.resource
                if at is None:
                    continue
                if link != CORE:
                    ends = sorted(
                        end for other, (end, _) in flying.items() if other.resource == link and end > now
                    )
                    if len(ends) >= DEPTHS[link]:
                        early = EARLY if link in (AHEAD, BACK) and len(ends) == 1 else 0.0
                        at = max(at, ends[-DEPTHS[link]] - early)
                    others = [
                        end
                        for other, (end, _) in flying.items()
                        if other.resource in HOPPING and other not in task.needs
                    ]
                    if link in HOPPING and len(others) >= HOPS:
                        at = max(at, sorted(others)[len(others) - HOPS] + MARGINS[SMALL])
                if at > now:
                    wakes.append(at)
                elif link != CORE:
                    chosen = task
                    break
                elif chosen is None:
                    chosen = task
            if chosen is None:
                now = min(wakes)
                continue
            result = issue(chosen)
            link = chosen.resource
            if link == CORE:
                values[chosen] = result
                now += chosen.cost
                fresh = True
                continue
            behind = free.get(link, 0.0) > now and link != SMALL
            end = free[link] + chosen.cost - QUEUED if behind else now + chosen.cost
            if link != SMALL:
                free[link] = end
            flying[chosen] = (end, result)
            now += STARTS[link]
        for task in results:
            if task in flying:
                values[task] = flying.pop(task)[1]
        self.log.append((now, 1, None))
        return [values[task] for task in results]


def dot_cost(rows, inner, columns):
    return 1.0 + 2.0 * rows * inner * columns / DOT_RATE


def move_cost(count):
    return 1.0 + count / 2e6


def ring_gather(plan, ring, own, count, flip=False, bias=0.0, after={}):
    blocks = {0: own}
    for link, way, step in ring.ways(flip):
        source = own
        for n, distance in enumerate(way):

            def move(v, source=source, step=step):
                return ring.hop(v[source], step)

            held = [after[link, n]] if (link, n) in after else []
            cost = HOP_COST + count * 2 / LINK_RATE
            source = plan.add(link, cost, [source, *held], move, bias)
            blocks[distance] = source
    return blocks


def ring_reduce(plan, ring, parts, count, finish, flip=False, bias=2.0, after=()):
    half = ring.count // 2

    def total(distance, sources):
        slot = ring.slots[distance]
        part = parts[slot // half]
        if not sources:
            return plan.compute(0.0, [part], lambda v: v[part][slot % half], 20.0)

        def add(v):
            terms = [v[part][slot % half], *(v[source] for source in sources)]
            if distance:
                return add_up([(term, 0) for term in terms], halves)
            return finish(sum(term.astype(floats) for term in terms))

        cost = 0.5 + count / 5e5
        if not distance:
            cost = cost + move_cost(3 * count)
        return plan.compute(cost, [part, *sources], add, 10.0 if distance else -1.0)

    passings = []
    for link, way, step in ring.ways(flip):
        passing = []
        for distance in reversed(way):
            made = total(distance, passing)

            def move(v, made=made, step=step):
                return ring.hop(v[made], -step)

            cost = HOP_COST + count * 2 / LINK_RATE
            passing = [plan.add(link, cost, [made, *after], move, bias)]
        passings.extend(passing)
    return total(0, passings)


def params():
    return pltpu.CompilerParams(vmem_limit_bytes=VMEM_BYTES)


def add_up(terms, dtype, rows=None):
    rows = rows or terms[0][0].shape[0]
    return sum(array[first : first + rows].astype(floats) for array, first in terms).astype(dtype)


def first_norm(tokens, gain, tiles, own):
    seq_len, width = tokens.shape
    part = seq_len // tiles

    def body(own_ref, tok_ref, gain_ref, out_ref, rows_ref, factor_ref):
        whole = tok_ref[...].astype(floats)
        inverse = lax.rsqrt(jnp.mean(whole * whole, axis=-1, keepdims=True) + epsilon)
        out_ref[...] = (whole * inverse * gain_ref[...]).astype(halves)
        factor_ref[...] = jnp.broadcast_to(inverse, factor_ref.shape)

        @pl.when(pl.program_id(0) == own_ref[0])
        def _():
            rows_ref[...] = tok_ref[...]

    return pl.pallas_call(
        body,
        out_shape=(
            jax.ShapeDtypeStruct((seq_len, width), halves),
            jax.ShapeDtypeStruct((part, width), tokens.dtype),
            jax.ShapeDtypeStruct((seq_len, 128), floats),
        ),
        grid_spec=pltpu.PrefetchScalarGridSpec(
            num_scalar_prefetch=1,
            grid=(tiles,),
            in_specs=[
                pl.BlockSpec((part, width), lambda i, own_ref: (i, 0)),
                pl.BlockSpec((1, width), lambda i, own_ref: (0, 0)),
            ],
            out_specs=(
                pl.BlockSpec((part, width), lambda i, own_ref: (i, 0)),
                pl.BlockSpec((part, width), lambda i, own_ref: (0, 0)),
                pl.BlockSpec((part, 128), lambda i, own_ref: (i, 0)),
            ),
        ),
        compiler_params=params(),
        cost_estimate=HEAVY,
    )(own, tokens, gain.reshape(1, width))


def tile_of(size):
    return max(step for step in range(128, 513, 128) if size % step == 0)


def gradient_blocks(groups, order, half, tile, keep):
    count = order.shape[0] // 2
    block = groups[0][1].shape[1] // order.shape[0]
    starts, total = [], 0
    for lhs, _ in groups:
        starts.append(total)
        total += lhs.shape[0] * lhs.shape[2] // tile
    in_specs, operands = [], []
    for start, (lhs, rhs) in zip(starts, groups):
        sides, tokens, height = lhs.shape
        steps = height // tile

        def place_of(i, order_ref, start=start, sides=sides, steps=steps):
            step = jnp.clip(i - start, 0, sides * steps - 1)
            return step // steps, 0, step % steps

        def column(j, tokens=tokens):
            return pl.BlockSpec(
                (tokens, block), lambda i, order_ref: (0, order_ref[half * count + j])
            )

        in_specs += [pl.BlockSpec((1, tokens, tile), place_of), *(column(j) for j in range(count))]
        operands += [lhs, *([rhs] * count)]

    def body(order_ref, *refs):
        out_refs = refs[len(operands) :]
        step = pl.program_id(0)
        for n, start in enumerate(starts):
            end = starts[n + 1] if n + 1 < len(starts) else total
            lhs_ref, *rhs_refs = refs[n * (count + 1) : (n + 1) * (count + 1)]

            @pl.when(jnp.logical_and(step >= start, step < end))
            def _():
                turned = lhs_ref[0].T
                for rhs_ref, out_ref in zip(rhs_refs, out_refs):
                    product = jnp.dot(turned, rhs_ref[...], preferred_element_type=floats)
                    out_ref[...] = product[:keep].astype(halves)

    return pl.pallas_call(
        body,
        out_shape=[jax.ShapeDtypeStruct((total * keep, block), halves)] * count,
        grid_spec=pltpu.PrefetchScalarGridSpec(
            num_scalar_prefetch=1,
            grid=(total,),
            in_specs=in_specs,
            out_specs=[pl.BlockSpec((keep, block), lambda i, order_ref: (i, 0))] * count,
        ),
        compiler_params=params(),
        cost_estimate=HEAVY,
    )(order, *operands)


def matmul_across(lhs, rhs, first, count):
    tall, inner = lhs.shape
    tile = 256 if count % 256 == 0 and first % 256 == 0 else 128

    def body(lhs_ref, rhs_ref, out_ref):
        out_ref[...] = lax.dot_general(
            lhs_ref[...], rhs_ref[...], contract_last, preferred_element_type=floats
        )

    return pl.pallas_call(
        body,
        out_shape=jax.ShapeDtypeStruct((tall, count), floats),
        grid=(count // tile,),
        in_specs=[
            pl.BlockSpec((tall, inner), lambda j: (0, 0)),
            pl.BlockSpec((tile, inner), lambda j: (first // tile + j, 0)),
        ],
        out_specs=pl.BlockSpec((tall, tile), lambda j: (0, j)),
        compiler_params=params(),
        cost_estimate=HEAVY,
    )(lhs, rhs)


def halves_spec(parts, inner, tall, tile):
    half, part = tall // inner, tall // parts

    def put(places_ref, product, own_ref, other_ref):
        for a in range(parts):
            rows = product[a * part : (a + 1) * part]
            place = places_ref[a]

            @pl.when(place < parts // inner)
            def _():
                own_ref[pl.ds(pl.multiple_of(place * part, part), part)] = rows

            if inner > 1:

                @pl.when(place >= parts // inner)
                def _():
                    at = pl.multiple_of(place * part - half, part)
                    other_ref[pl.ds(at, part)] = rows.astype(halves)

    return half, pl.BlockSpec((half, tile), lambda j, p: (0, j)), put


def matmul_halves(lhs, rhs, places, inner, first=0, scaled=None):
    tall, depth = lhs.shape
    wide = rhs.shape[1]
    tile = 256 if wide % 256 == 0 else 128
    half, spec, put = halves_spec(places.shape[0], inner, tall, tile)

    def body(places_ref, lhs_ref, rhs_ref, *refs):
        product = jnp.dot(lhs_ref[...], rhs_ref[...], preferred_element_type=floats)
        put(places_ref, product, *refs[len(scaled or ()) :][:2])
        if scaled:
            array_ref, factor_ref, sums_ref = refs[0], refs[1], refs[-1]
            terms = product * array_ref[...].astype(floats) * factor_ref[:, :1]
            sums_ref[...] = jnp.sum(terms.reshape(tall // 8, 8, tile), axis=0)

    more_in, more_out, more_shapes = [], [], []
    if scaled:
        more_in = [
            pl.BlockSpec((tall, tile), lambda j, p: (0, j)),
            pl.BlockSpec(scaled[1].shape, lambda j, p: (0, 0)),
        ]
        more_out = [pl.BlockSpec((8, tile), lambda j, p: (0, j))]
        more_shapes = [jax.ShapeDtypeStruct((8, wide), floats)]
    return pl.pallas_call(
        body,
        out_shape=(
            jax.ShapeDtypeStruct((half, wide), floats),
            jax.ShapeDtypeStruct((half, wide), halves),
            *more_shapes,
        ),
        grid_spec=pltpu.PrefetchScalarGridSpec(
            num_scalar_prefetch=1,
            grid=(wide // tile,),
            in_specs=[
                pl.BlockSpec((tall, depth), lambda j, p: (0, 0)),
                pl.BlockSpec((depth, tile), lambda j, p: (first // depth, j)),
                *more_in,
            ],
            out_specs=(spec, spec, *more_out),
        ),
        compiler_params=params(),
        cost_estimate=HEAVY,
    )(places, lhs, rhs, *(scaled or ()))


def gated_forward(normed, weights):
    tokens, inner = normed.shape
    hidden = weights.shape[1] // 2
    tile = 256 if hidden % 256 == 0 else 128
    steps = hidden // tile

    def body(in_ref, gate_ref, up_ref, gate_out, up_out, hidden_out):
        gate = jnp.dot(in_ref[...], gate_ref[...], preferred_element_type=floats)
        up = jnp.dot(in_ref[...], up_ref[...], preferred_element_type=floats)
        gate_out[...] = gate
        up_out[...] = up
        hidden_out[...] = (gelu(gate) * up).astype(halves)

    column = pl.BlockSpec((tokens, tile), lambda j: (0, j))
    return pl.pallas_call(
        body,
        out_shape=(
            jax.ShapeDtypeStruct((tokens, hidden), floats),
            jax.ShapeDtypeStruct((tokens, hidden), floats),
            jax.ShapeDtypeStruct((tokens, hidden), halves),
        ),
        grid=(steps,),
        in_specs=[
            pl.BlockSpec((tokens, inner), lambda j: (0, 0)),
            pl.BlockSpec((inner, tile), lambda j: (0, j)),
            pl.BlockSpec((inner, tile), lambda j: (0, steps + j)),
        ],
        out_specs=(column, column, column),
        compiler_params=params(),
        cost_estimate=HEAVY,
    )(normed, weights, weights)


def gated_backward(cotangent, down, gate, up):
    tokens, inner = cotangent.shape
    hidden = down.shape[0]
    tile = 256 if hidden % 256 == 0 else 128

    def body(cot_ref, down_ref, gate_ref, up_ref, out_ref):
        back = lax.dot_general(
            cot_ref[...], down_ref[...], contract_last, preferred_element_type=floats
        )
        active, slope = gelu_parts(gate_ref[...])
        out_ref[0] = (back * up_ref[...] * slope).astype(halves)
        out_ref[1] = (back * active).astype(halves)

    column = pl.BlockSpec((tokens, tile), lambda j: (0, j))
    return pl.pallas_call(
        body,
        out_shape=jax.ShapeDtypeStruct((2, tokens, hidden), halves),
        grid=(hidden // tile,),
        in_specs=[
            pl.BlockSpec((tokens, inner), lambda j: (0, 0)),
            pl.BlockSpec((tile, inner), lambda j: (j, 0)),
            column,
            column,
        ],
        out_specs=pl.BlockSpec((2, tokens, tile), lambda j: (0, 0, j)),
        compiler_params=params(),
        cost_estimate=HEAVY,
    )(cotangent, down, gate, up)


def pair_halves(pair, weights, places, inner):
    _, tall, hidden = pair.shape
    wide = weights.shape[0]
    tile = 256 if wide % 256 == 0 else 128
    half, spec, put = halves_spec(places.shape[0], inner, tall, tile)

    def body(places_ref, pair_ref, gate_ref, up_ref, own_ref, other_ref):
        product = 0.0
        for side, ref in enumerate((gate_ref, up_ref)):
            product = product + lax.dot_general(
                pair_ref[side], ref[...], contract_last, preferred_element_type=floats
            )
        put(places_ref, product, own_ref, other_ref)

    weight = lambda side: pl.BlockSpec((tile, hidden), lambda j, p: (j, side))
    return pl.pallas_call(
        body,
        out_shape=(
            jax.ShapeDtypeStruct((half, wide), floats),
            jax.ShapeDtypeStruct((half, wide), halves),
        ),
        grid_spec=pltpu.PrefetchScalarGridSpec(
            num_scalar_prefetch=1,
            grid=(wide // tile,),
            in_specs=[pl.BlockSpec((2, tall, hidden), lambda j, p: (0, 0, 0)), weight(0), weight(1)],
            out_specs=(spec, spec),
        ),
        compiler_params=params(),
        cost_estimate=HEAVY,
    )(places, pair, weights, weights)


def segment_of(places, ends_ref):
    segment = jnp.zeros(places.shape, jnp.int32)
    for j in range(ends_ref.shape[0] - 1):
        segment = segment + (places >= ends_ref[j]).astype(jnp.int32)
    return segment


def same_behind(places, ends_ref, offset):
    agree = segment_of(places, ends_ref) == segment_of(places - offset, ends_ref)
    return jnp.logical_and(agree, places >= offset).astype(floats)


def same_ahead(places, ends_ref, offset, seq_len):
    agree = segment_of(places, ends_ref) == segment_of(places + offset, ends_ref)
    return jnp.logical_and(agree, places + offset < seq_len).astype(floats)


def lane_chunks(width):
    step = 256 if width % 256 == 0 else 128
    return [slice(at, at + step) for at in range(0, width, step)]


def gate_values(pre_a, pre_i, decay8):
    rate = jax.nn.sigmoid(pre_a)
    admit = jax.nn.sigmoid(pre_i)
    power = decay8 * rate
    alpha = jnp.exp(-power)
    twice = 2.0 * power
    series = 1.0 - twice * (1.0 / 7.0)
    for order in (6.0, 5.0, 4.0, 3.0, 2.0):
        series = 1.0 - (twice * (1.0 / order)) * series
    raw = jnp.where(twice < 0.5, twice * series, 1.0 - alpha * alpha)
    one_minus = jnp.maximum(raw, floor_value)
    inverse = lax.rsqrt(one_minus)
    return rate, admit, alpha, raw, one_minus * inverse, inverse


def gelu_parts(value):
    square = value * value
    bend = jnp.tanh(gelu_root * (value + gelu_cube * (square * value)))
    half = 0.5 * (1.0 + bend)
    slope = half + 0.5 * value * (1.0 - bend * bend) * (
        gelu_root * (1.0 + 3.0 * gelu_cube * square)
    )
    return value * half, slope


def gelu(value):
    return gelu_parts(value)[0]


def recur_forward(branches, doc_ends, vectors, gates, tiles):
    seq_len, lanes = branches.shape[0], branches.shape[1] // 2
    part = seq_len // tiles
    chunks = lane_chunks(lanes)

    def body(
        ends_ref, x_ref, y_ref, vec_ref, gate_ref,
        mixed_ref, conv_ref, pre_ref, prev_ref, xs, carry,
    ):
        tile = pl.program_id(0)

        @pl.when(tile == 0)
        def _():
            xs[0:8] = jnp.zeros((8, lanes), floats)
            carry[...] = jnp.zeros_like(carry)

        xs[8 : 8 + part] = x_ref[...]
        rows = lax.broadcasted_iota(jnp.int32, (CHUNK, 1), 0)

        def convolve(c, _):
            at = pl.multiple_of(c * CHUNK, CHUNK)
            here = tile * part + at + rows
            same = [same_behind(here, ends_ref, k) for k in range(1, 4)]
            for lane in chunks:
                window = xs[pl.ds(at, CHUNK + 8), lane]
                total = vec_ref[4:5, lane] + vec_ref[0:1, lane] * window[8:]
                for k in range(1, 4):
                    moved = pltpu.roll(window, k, 0)[8:]
                    total = total + vec_ref[k : k + 1, lane] * moved * same[k - 1]
                conv_ref[pl.ds(at, CHUNK), lane] = total.astype(halves)
            return 0

        lax.fori_loop(0, part // CHUNK, convolve, 0)
        xs[0:8] = xs[part : part + 8]
        pre_ref[...] = jnp.dot(conv_ref[...], gate_ref[...], preferred_element_type=floats)

        def advance(c, entering):
            at = pl.multiple_of(c * CHUNK, CHUNK)
            here = tile * part + at + rows
            fresh = 1.0 - same_behind(here, ends_ref, 1)
            leaving = []
            for state, lane in zip(entering, chunks):
                span = lane.stop - lane.start
                shift_lane = slice(lane.start + lanes, lane.stop + lanes)
                pre_a = pre_ref[pl.ds(at, CHUNK), lane] + vec_ref[6:7, lane]
                pre_i = pre_ref[pl.ds(at, CHUNK), shift_lane] + vec_ref[7:8, lane]
                pre_ref[pl.ds(at, CHUNK), lane] = pre_a
                pre_ref[pl.ds(at, CHUNK), shift_lane] = pre_i
                conv_in = conv_ref[pl.ds(at, CHUNK), lane].astype(floats)
                _, admit, alpha, _, root, _ = gate_values(pre_a, pre_i, vec_ref[5:6, lane])
                keep = 1.0 - fresh
                coef = alpha * keep
                drive = (fresh + root * keep) * admit * conv_in
                index = lax.broadcasted_iota(jnp.int32, (CHUNK, span), 0)
                for d in (1, 2, 4):
                    inside = (index & 7) >= d
                    drive = jnp.where(inside, drive + coef * pltpu.roll(drive, d, 0), drive)
                    coef = jnp.where(inside, coef * pltpu.roll(coef, d, 0), coef)
                groups = []
                first = state
                for g in range(CHUNK // 8):
                    group = slice(g * 8, g * 8 + 8)
                    groups.append(coef[group] * state + drive[group])
                    state = groups[-1][7:8]
                states = jnp.concatenate(groups, axis=0)
                prev_ref[pl.ds(at, CHUNK), lane] = jnp.where(
                    index == 0, first, pltpu.roll(states, 1, 0)
                )
                mixed = states * gelu(y_ref[pl.ds(at, CHUNK), lane])
                mixed_ref[pl.ds(at, CHUNK), lane] = mixed.astype(halves)
                leaving.append(state)
            return tuple(leaving)

        ended = lax.fori_loop(
            0, part // CHUNK, advance, tuple(carry[0:1, lane] for lane in chunks)
        )
        for state, lane in zip(ended, chunks):
            carry[0:1, lane] = state

    own = lambda column: pl.BlockSpec((part, lanes), lambda i, e: (i, column))
    straight = lambda width: pl.BlockSpec((part, width), lambda i, e: (i, 0))
    whole = lambda array: pl.BlockSpec(array.shape, lambda i, e: (0, 0))
    return pl.pallas_call(
        body,
        out_shape=(
            jax.ShapeDtypeStruct((seq_len, lanes), halves),
            jax.ShapeDtypeStruct((seq_len, lanes), halves),
            jax.ShapeDtypeStruct((seq_len, 2 * lanes), floats),
            jax.ShapeDtypeStruct((seq_len, lanes), floats),
        ),
        grid_spec=pltpu.PrefetchScalarGridSpec(
            num_scalar_prefetch=1,
            grid=(tiles,),
            in_specs=[own(0), own(1), whole(vectors), whole(gates)],
            out_specs=(own(0), straight(lanes), straight(2 * lanes), straight(lanes)),
            scratch_shapes=[pltpu.VMEM((part + 8, lanes), floats), pltpu.VMEM((8, lanes), floats)],
        ),
        compiler_params=params(),
        cost_estimate=HEAVY,
    )(doc_ends, branches, branches, vectors, gates)


def recur_backward(back_mixed, branches, conv_in, pre, previous, doc_ends, vectors, gates, tiles):
    seq_len, lanes = conv_in.shape
    part = seq_len // tiles
    chunks = lane_chunks(lanes)
    steps = part // CHUNK

    def body(
        ends_ref, bm_ref, x_ref, y_ref, conv_ref, pre_ref, prev_ref, vec_ref, gate_ref,
        bxy_ref, bai_ref, sums_ref, ahead, sums, carry,
    ):
        tile = tiles - 1 - pl.program_id(0)

        @pl.when(pl.program_id(0) == 0)
        def _():
            ahead[part : part + 8] = jnp.zeros((8, lanes), floats)
            sums[...] = jnp.zeros_like(sums)
            carry[...] = jnp.zeros_like(carry)

        rows = lax.broadcasted_iota(jnp.int32, (CHUNK, 1), 0)

        def add_rows(which, lane, value):
            for g in range(CHUNK // 8):
                sums[which * 8 : which * 8 + 8, lane] += value[g * 8 : g * 8 + 8]

        def retreat(c, entering):
            at = pl.multiple_of((steps - 1 - c) * CHUNK, CHUNK)
            span_rows = pl.ds(at, CHUNK)
            here = tile * part + at + rows
            keep = same_behind(here, ends_ref, 1)
            fresh = 1.0 - keep
            leaving = []
            for (back_next, coef_next), lane in zip(entering, chunks):
                span = lane.stop - lane.start
                shift_lane = slice(lane.start + lanes, lane.stop + lanes)
                decay8 = vec_ref[5:6, lane]
                rate, admit, alpha, raw, root, inverse = gate_values(
                    pre_ref[span_rows, lane], pre_ref[span_rows, shift_lane], decay8
                )
                conv = conv_ref[span_rows, lane].astype(floats)
                before = prev_ref[span_rows, lane]
                scale_in = fresh + root * keep
                coef = alpha * keep
                driven = scale_in * admit
                states = coef * before + driven * conv
                active, slope = gelu_parts(y_ref[span_rows, lane])
                back_mix = bm_ref[span_rows, lane]
                bxy_ref[span_rows, shift_lane] = (back_mix * states * slope).astype(halves)
                index = lax.broadcasted_iota(jnp.int32, (CHUNK, span), 0)
                back = back_mix * active
                chain = jnp.where(index == CHUNK - 1, coef_next, pltpu.roll(coef, CHUNK - 1, 0))
                for d in (1, 2, 4):
                    inside = (index & 7) < 8 - d
                    back = jnp.where(inside, back + chain * pltpu.roll(back, CHUNK - d, 0), back)
                    chain = jnp.where(inside, chain * pltpu.roll(chain, CHUNK - d, 0), chain)
                groups = []
                for g in reversed(range(CHUNK // 8)):
                    group = slice(g * 8, g * 8 + 8)
                    groups.insert(0, back[group] + chain[group] * back_next)
                    back_next = groups[0][0:1]
                back_state = jnp.concatenate(groups, axis=0)
                through = back_state * conv
                bound = jnp.where(raw > floor_value, through * admit * alpha * inverse, 0.0)
                back_alpha = (back_state * before - bound) * keep * alpha
                add_rows(5, lane, back_alpha * rate)
                back_a = (back_alpha * (-decay8) * rate * (1.0 - rate)).astype(halves)
                back_i = (through * scale_in * admit * (1.0 - admit)).astype(halves)
                add_rows(6, lane, back_a.astype(floats))
                add_rows(7, lane, back_i.astype(floats))
                bai_ref[span_rows, lane] = back_a
                bai_ref[span_rows, shift_lane] = back_i
                ahead[span_rows, lane] = back_state * driven
                leaving.append((back_next, coef[0:1]))
            return tuple(leaving)

        ended = lax.fori_loop(
            0, steps, retreat, tuple((carry[0:1, lane], carry[8:9, lane]) for lane in chunks)
        )
        for (back_next, coef_next), lane in zip(ended, chunks):
            carry[0:1, lane] = back_next
            carry[8:9, lane] = coef_next

        ahead[0:part] += lax.dot_general(
            bai_ref[...], gate_ref[...], contract_last, preferred_element_type=floats
        )

        def convolve(c, _):
            at = pl.multiple_of(c * CHUNK, CHUNK)
            here = tile * part + at + rows
            same = [same_ahead(here, ends_ref, k, seq_len) for k in range(1, 4)]
            for lane in chunks:
                window = ahead[pl.ds(at, CHUNK + 8), lane]
                x_part = x_ref[pl.ds(at, CHUNK), lane]
                direct = window[:CHUNK]
                back_x = vec_ref[0:1, lane] * direct
                add_rows(0, lane, x_part * direct)
                add_rows(4, lane, direct)
                for k in range(1, 4):
                    moved = pltpu.roll(window, CHUNK + 8 - k, 0)[:CHUNK] * same[k - 1]
                    back_x = back_x + vec_ref[k : k + 1, lane] * moved
                    add_rows(k, lane, x_part * moved)
                bxy_ref[pl.ds(at, CHUNK), lane] = back_x.astype(halves)
            return 0

        lax.fori_loop(0, steps, convolve, 0)
        ahead[part : part + 8] = ahead[0:8]

        @pl.when(pl.program_id(0) == tiles - 1)
        def _():
            for which in range(8):
                sums_ref[which : which + 1] = jnp.sum(
                    sums[which * 8 : which * 8 + 8], axis=0, keepdims=True
                )

    own = lambda width, column: pl.BlockSpec((part, width), lambda i, e: (tiles - 1 - i, column))
    straight = lambda width: pl.BlockSpec((part, width), lambda i, e: (tiles - 1 - i, 0))
    whole = lambda array: pl.BlockSpec(array.shape, lambda i, e: (0, 0))
    return pl.pallas_call(
        body,
        out_shape=(
            jax.ShapeDtypeStruct((seq_len, 2 * lanes), halves),
            jax.ShapeDtypeStruct((seq_len, 2 * lanes), halves),
            jax.ShapeDtypeStruct((8, lanes), floats),
        ),
        grid_spec=pltpu.PrefetchScalarGridSpec(
            num_scalar_prefetch=1,
            grid=(tiles,),
            in_specs=[
                own(lanes, 0), own(lanes, 0), own(lanes, 1),
                straight(lanes), straight(2 * lanes), straight(lanes),
                whole(vectors), whole(gates),
            ],
            out_specs=(
                own(2 * lanes, 0), straight(2 * lanes), pl.BlockSpec((8, lanes), lambda i, e: (0, 0)),
            ),
            scratch_shapes=[
                pltpu.VMEM((part + 8, lanes), floats),
                pltpu.VMEM((64, lanes), floats),
                pltpu.VMEM((16, lanes), floats),
            ],
        ),
        compiler_params=params(),
        cost_estimate=HEAVY,
    )(doc_ends, back_mixed, branches, branches, conv_in, pre, previous, vectors, gates)


def rms_norm(inputs, scales):
    return inputs * lax.rsqrt(jnp.mean(inputs * inputs, axis=-1, keepdims=True) + epsilon) * scales


def inner_of(count):
    return max(d for d in range(1, count + 1) if count % d == 0 and d * d <= count)


def on_device(
    tokens,
    doc_lengths,
    gain_mix,
    value_weight,
    branch_weight,
    conv_weight,
    conv_bias,
    recur_gate,
    input_gate,
    recur_bias,
    input_bias,
    decay_param,
    out_weight,
    gain_ffn,
    gate_weight,
    up_weight,
    down_weight,
    cotangent,
):
    seq_len, _, width = tokens.shape
    heads, head_width = recur_gate.shape[:2]
    channels = value_weight.shape[1]
    hidden_width = gate_weight.shape[1]
    lanes = round_up(channels, 128)
    sent = round_up(channels, 16)
    dp = Ring(DP, inner_of(lax.axis_size(DP)))
    parts = lax.axis_size(CHAN)
    part = seq_len // parts
    block = width // dp.count
    order = dp.order()
    chan = lax.axis_index(CHAN)
    own_tile = chan.reshape(1).astype(jnp.int32)
    cores = 2 if parts % 2 == 0 else 1
    chips = parts // cores
    tiles = jnp.arange(parts, dtype=jnp.int32)
    row_places = ((tiles - chan) % cores) * chips + (tiles // cores - chan // cores) % chips
    doc_ends = jnp.cumsum(doc_lengths[0])
    plan = Plan()
    compute = plan.compute

    def gather_weight(own, count, flip, bias, after, put):
        blocks = ring_gather(plan, dp, own, count, flip, bias, after)
        full = None
        for distance in sorted(blocks, key=lambda d: min(d, dp.count - d)):

            def extend(v, before=full, piece=blocks[distance], slot=dp.slots[distance]):
                return put(
                    None if before is None else v[before], v[piece], order[slot : slot + 1]
                )

            needs = [blocks[distance]] if full is None else [full, blocks[distance]]
            full = compute(1.0 + count / 1.2e6, needs, extend)
        return full, blocks

    def put_mix(full, piece, at):
        if full is None:
            full = jnp.zeros((3 * lanes, width), halves), jnp.zeros((hidden_width, width), halves)
        mix, down = full
        for i in range(3):
            rows = piece[i * sent : (i + 1) * sent]
            mix = lax.dynamic_update_slice(mix, rows, (i * lanes, at[0] * block))
        return mix, lax.dynamic_update_slice(down, piece[3 * sent :], (0, at[0] * block))

    def put_rows(full, piece, at):
        if full is None:
            full = jnp.zeros((width, 2 * hidden_width), halves)
        return lax.dynamic_update_slice(full, piece, (at[0] * block, 0))

    def mix_of(value, branch, out, down):
        pieces = [pad_dim(array, 0, sent) for array in (value.T, branch.T, out)]
        return jnp.concatenate([*pieces, down], axis=0)

    mix = compute(
        3.0, [], lambda v: mix_of(value_weight, branch_weight, out_weight, down_weight), 8.0
    )
    both_own = compute(2.0, [], lambda v: jnp.concatenate([gate_weight, up_weight], axis=1), 1.0)
    mix_full, mix_blocks = gather_weight(
        mix, (3 * sent + hidden_width) * block, False, 9.0, {}, put_mix
    )
    far = dp.count // 2
    both_full, _ = gather_weight(
        both_own, 2 * hidden_width * block, True, 8.0,
        {(AHEAD, 0): mix_blocks[far], (BACK, 0): mix_blocks[far + 1]}, put_rows,
    )

    def spread(gate):
        total = 0.0
        for h in range(heads):
            low = h * head_width
            total = total + jnp.pad(gate[h], ((low, lanes - low - head_width),) * 2)
        return total

    def small_parameters(v):
        gates = jnp.concatenate([spread(recur_gate), spread(input_gate)], axis=1)
        vectors = [
            conv_weight,
            conv_bias[None],
            decay_scale * jax.nn.softplus(decay_param)[None],
            recur_bias[None],
            input_bias[None],
        ]
        return gates, pad_dim(jnp.concatenate(vectors, axis=0), 1, lanes)

    small = compute(8.0, [], small_parameters)

    def cross(value, step):
        pairs = [
            (x * cores + c, ((x + step) % chips) * cores + c)
            for x in range(chips)
            for c in range(cores)
        ]
        return lax.ppermute(value, CHAN, pairs)

    def swap(value):
        pairs = [(x * cores + c, x * cores + (c + 1) % cores) for x in range(chips) for c in range(cores)]
        return lax.ppermute(value, CHAN, pairs)

    def gather_rows(own):
        return plan.add(
            CHIPS, 33.0, [own], lambda v: lax.all_gather(v[own], CHAN, axis=0, tiled=True)
        )

    def reduce_rows(product, after=()):
        terms = []
        if cores > 1:
            terms = [plan.add(TWIN, 9.0, [product, *after], lambda v: swap(v[product][1]), 3.0)]
        passing = []
        for s in reversed(range(chips)):

            def add(v, s=s, passing=tuple(passing)):
                pieces = [(v[product][0], s * part), *((v[term], s * part) for term in terms)]
                pieces += [(v[term], 0) for term in passing]
                return add_up(pieces, halves if s else floats, part)

            made = compute(2.0, [product, *terms, *passing], add, 10.0)
            if s:
                passing = [
                    plan.add(CROSS, 26.5, [made], lambda v, made=made: cross(v[made], 1), 3.0)
                ]
        return made

    def small_total(source, axes):
        for axis in axes:
            count = lax.axis_size(axis)
            assert count & (count - 1) == 0
            bit = 1
            while bit < count:
                pairs = [(i, i ^ bit) for i in range(count)]

                def send(v, source=source, axis=axis, pairs=pairs):
                    return lax.ppermute(v[source], axis, pairs)

                other = plan.add(SMALL, 18.0 if axis == DP else 8.0, [source], send)

                def add(v, source=source, other=other):
                    return v[source] + v[other]

                source = compute(0.5, [source, other], add)
                bit *= 2
        return source

    norm_in = compute(
        5.0, [], lambda v: first_norm(tokens.reshape(seq_len, width), gain_mix, parts, own_tile)
    )
    cot = compute(1.5, [], lambda v: cotangent.reshape(part, width))
    cot_full = gather_rows(cot)
    branches = compute(
        10.8,
        [norm_in, mix_full],
        lambda v: matmul_across(v[norm_in][0], v[mix_full][0], 0, 2 * lanes),
    )
    recur = compute(
        20.2,
        [branches, small],
        lambda v: recur_forward(v[branches], doc_ends, v[small][1], v[small][0], parts),
    )
    mixed = compute(0.0, [recur], lambda v: v[recur][0], 30.0)
    mixed_out = compute(
        9.2,
        [mixed, mix_full],
        lambda v: matmul_halves(v[mixed], v[mix_full][0], row_places, cores, 2 * lanes),
    )
    branch_out = reduce_rows(mixed_out)

    def middle_of(v):
        residual = v[norm_in][1].astype(floats) + v[branch_out]
        return residual, rms_norm(residual, gain_ffn).astype(halves)

    middle = compute(3.0, [norm_in, branch_out], middle_of)
    mid = compute(0.0, [middle], lambda v: v[middle][1], 30.0)
    mid_full = gather_rows(mid)

    gated = compute(
        19.7,
        [mid_full, both_full],
        lambda v: gated_forward(v[mid_full], v[both_full]),
    )
    hidden = compute(0.0, [gated], lambda v: v[gated][2], 30.0)

    def gradient(needs, groups, tile, keep, cost, bias):
        return [
            compute(
                cost,
                needs,
                lambda v, h=h: gradient_blocks(groups(v), order, h, tile, keep),
                bias - 3 * h,
            )
            for h in range(2)
        ]

    back_both = compute(
        14.7,
        [gated, cot_full, mix_full],
        lambda v: gated_backward(v[cot_full], v[mix_full][1], *v[gated][:2]),
    )
    back_product = compute(
        20.5,
        [back_both, both_full],
        lambda v: pair_halves(v[back_both], v[both_full], row_places, cores),
    )
    back_mid = reduce_rows(back_product)
    tile = tile_of(hidden_width)
    grad_ffn = ring_reduce(
        plan,
        dp,
        gradient(
            [hidden, cot_full, back_both, mid_full],
            lambda v: [(v[hidden][None], v[cot_full]), (v[back_both], v[mid_full])],
            tile, tile, 18.0, 2.0,
        ),
        3 * hidden_width * block,
        lambda total: (
            total[:hidden_width],
            total[hidden_width : 2 * hidden_width].T,
            total[2 * hidden_width :].T,
        ),
        False,
    )
    ffn_product = compute(
        12.0,
        [hidden, mix_full],
        lambda v: matmul_halves(v[hidden], v[mix_full][1], row_places, cores),
        -2.0,
    )

    def norm_back(inputs, gain, back):
        scale = lax.rsqrt(jnp.mean(inputs * inputs, axis=-1, keepdims=True) + epsilon)
        scaled = back * gain
        mean = jnp.mean(scaled * inputs, axis=-1, keepdims=True)
        through = scale * scaled - inputs * (scale * scale * scale * mean)
        return through

    def back_middle_of(v):
        residual, back = v[middle][0], v[back_mid]
        scale = lax.rsqrt(jnp.mean(residual * residual, axis=-1, keepdims=True) + epsilon)
        gain = jnp.sum((back * residual * scale).reshape(part // 8, 8, width), axis=0)
        back = v[cot].astype(floats) + norm_back(residual, gain_ffn, back)
        return back, back.astype(halves), gain

    back_middle = compute(4.0, [middle, back_mid, cot], back_middle_of)
    back_resid = compute(0.0, [back_middle], lambda v: v[back_middle][1], 30.0)
    branch_full = gather_rows(back_resid)
    ffn_out = reduce_rows(ffn_product, [branch_full])
    output = compute(
        4.0, [middle, ffn_out], lambda v: (v[middle][0] + v[ffn_out]).astype(halves), -1.0
    )
    back_mixed = compute(
        6.7,
        [branch_full, mix_full],
        lambda v: matmul_across(v[branch_full], v[mix_full][0], 2 * lanes, lanes),
    )
    recur_back = compute(
        26.5,
        [back_mixed, branches, recur, small],
        lambda v: recur_backward(
            v[back_mixed], v[branches], *v[recur][1:], doc_ends, v[small][1], v[small][0], parts
        ),
    )
    grad_mix = ring_reduce(
        plan,
        dp,
        gradient(
            [recur_back, norm_in, mixed, branch_full],
            lambda v: [(v[recur_back][0][None], v[norm_in][0]), (v[mixed][None], v[branch_full])],
            lanes, sent, 9.0, 4.0,
        ),
        3 * sent * block,
        lambda total: (
            total[:channels].T,
            total[sent : sent + channels].T,
            total[2 * sent : 2 * sent + channels],
        ),
        True,
    )
    back_pair = compute(
        13.0,
        [recur_back, mix_full, norm_in],
        lambda v: matmul_halves(
            v[recur_back][0], v[mix_full][0], row_places, cores, 0,
            (tokens.reshape(seq_len, width), v[norm_in][2]),
        ),
        2.0,
    )
    back_norm_in = reduce_rows(back_pair)

    def back_first_of(v):
        through = norm_back(v[norm_in][1].astype(floats), gain_mix, v[back_norm_in])
        return v[back_middle][0] + through

    back_first = compute(5.0, [norm_in, back_norm_in, back_middle], back_first_of)

    def gate_grads_of(v):
        whole = lax.dot_general(
            v[recur][1], v[recur_back][1], contract_first, preferred_element_type=floats
        )
        return jnp.stack(
            [
                whole[
                    h * head_width : (h + 1) * head_width,
                    side * lanes + h * head_width : side * lanes + (h + 1) * head_width,
                ]
                for side in range(2)
                for h in range(heads)
            ]
        )

    gate_terms = compute(
        5.0, [recur, recur_back], lambda v: gate_grads_of(v).astype(halves), 3.5
    )
    gate_sums = plan.add(CHIPS, 60.0, [gate_terms], lambda v: lax.psum(v[gate_terms], DP), 3.0)
    gate_result = compute(
        4.0, [gate_sums], lambda v: tuple(jnp.split(v[gate_sums].astype(floats), 2))
    )
    def both_gains(v):
        gains = [jnp.sum(terms, axis=0).reshape(8, -1) for terms in (v[back_middle][2], v[back_pair][2])]
        return jnp.concatenate(gains, axis=1)

    gain_rows = small_total(compute(2.0, [back_middle, back_pair], both_gains, 1.0), [CHAN])
    sums = small_total(
        compute(
            1.0,
            [recur_back, gain_rows],
            lambda v: jnp.concatenate([v[recur_back][2], v[gain_rows]], axis=1),
        ),
        [DP],
    )

    def sum_results_of(v):
        total = v[sums][:, :channels]
        decay = total[5] * (-decay_scale * jax.nn.sigmoid(decay_param))
        gains = v[sums][:, lanes:]
        return (
            total[:4], total[4], total[6], total[7], decay,
            gains[:, : width // 8].reshape(width), gains[:, width // 8 :].reshape(width),
        )

    sum_results = compute(3.0, [sums], sum_results_of)

    done = plan.execute(
        [
            output, back_first, grad_mix, sum_results, gate_result, grad_ffn,
        ]
    )
    output, first, (value, branch, out), summed, (recur, admit), (down, gate, up) = done
    return (
        output.reshape(part, 1, width),
        first.reshape(part, 1, width),
        summed[6],
        value,
        branch,
        summed[0],
        summed[1],
        recur,
        admit,
        summed[2],
        summed[3],
        summed[4],
        out,
        summed[5],
        gate,
        up,
        down,
    )


def solution(mesh):
    tokens, split, columns = P(None, DP, None), P(DP, CHAN), P(CHAN, DP)
    own, channels, heads = P(CHAN, DP, None), P(CHAN), P(CHAN, None, None)
    in_specs = (
        tokens, P(DP, None), P(), split, split, P(None, CHAN), channels, heads, heads,
        channels, channels, channels, columns, P(), split, split, columns, own,
    )
    out_specs = (
        own, own, P(), split, split, P(None, CHAN), channels, heads, heads,
        channels, channels, channels, columns, P(), split, split, columns,
    )
    return jax.shard_map(
        on_device, mesh=mesh, in_specs=in_specs, out_specs=out_specs, check_vma=False
    )
```

```python
from functools import partial

import jax
import jax.numpy as jnp
from jax import lax
from jax.experimental import pallas as pl
from jax.experimental.pallas import tpu as pltpu
from jax.sharding import PartitionSpec as P

epsilon = 1e-06
decay_scale = 8.0
floor_value = 0.0001
gelu_root = 0.7978845608
gelu_cube = 0.044715
floats = jnp.float32
halves = jnp.bfloat16
contract_last = (((1,), (1,)), ((), ()))
contract_first = (((0,), (0,)), ((), ()))
CHUNK = 16
DP, CHAN = "dp", "chan"
VMEM_BYTES = 48 * 1024 * 1024
HEAVY = pl.CostEstimate(flops=2 * 10**11, bytes_accessed=1, transcendentals=0)


def round_up(number, unit):
    return -(-number // unit) * unit


def pad_dim(array, axis, size):
    widths = [(0, 0)] * array.ndim
    widths[axis] = (0, size - array.shape[axis])
    return jnp.pad(array, widths)


class Ring:
    def __init__(self, axis, inner):
        self.axis = axis
        self.count = lax.axis_size(axis)
        outer = self.count // inner
        self.path = [(o, 0) for o in range(outer)]
        for n, o in enumerate(reversed(range(outer))):
            columns = list(range(1, inner))
            self.path += [(o, i) for i in (reversed(columns) if n % 2 else columns)]
        self.path = [o * inner + i for o, i in self.path]
        spots = [self.path.index(i) for i in range(self.count)]
        self.spot = self.look(spots, lax.axis_index(axis))
        far = self.count // 2
        self.distances = [far]
        for j in range(1, far):
            self.distances += [far + j, far - j]
        self.distances += [0]
        self.slots = {distance: j for j, distance in enumerate(self.distances)}

    def look(self, table, index):
        return sum(jnp.where(index == i, entry, 0) for i, entry in enumerate(table))

    def hop(self, value, step):
        pairs = [
            (self.path[n], self.path[(n + step) % self.count]) for n in range(self.count)
        ]
        return lax.ppermute(value, self.axis, pairs)

    def order(self):
        ahead = self.look(self.distances, jnp.arange(self.count, dtype=jnp.int32))
        return self.look(self.path, (self.spot + ahead) % self.count).astype(jnp.int32)

    def ways(self, flip):
        ahead = (self.count - 1) // 2 if flip else self.count // 2
        return [
            (AHEAD, list(range(1, ahead + 1)), -1),
            (BACK, list(range(self.count - 1, ahead, -1)), 1),
        ]


LINK_RATE = 46e3
HOP_COST = 3.5
EARLY = 0.0
QUEUED = 2.5
CORE, AHEAD, BACK, CHIPS, CROSS, TWIN, SMALL = range(7)
DEPTHS = {AHEAD: 1, BACK: 1, CHIPS: 9, CROSS: 1, TWIN: 1, SMALL: 2}
STARTS = {AHEAD: 1.5, BACK: 0.8, CHIPS: 0.5, CROSS: 1.5, TWIN: 1.5, SMALL: 2.0}
HOPPING = (AHEAD, BACK, CROSS, TWIN, SMALL)
HOPS = 5
PATIENCE, LONG = 6.0, 8.0
MARGINS = {CORE: 3.0, AHEAD: 1.5, BACK: 1.5, CHIPS: 1.0, CROSS: 0.5, TWIN: 0.5, SMALL: 2.0}


class Task:
    def __init__(self, number, resource, cost, needs, run, bias):
        self.number, self.resource, self.cost, self.needs = number, resource, cost, needs
        self.run, self.bias, self.level, self.users = run, bias, 0.0, []


class Plan:
    def __init__(self):
        self.tasks, self.log = [], []

    def add(self, resource, cost, needs, run, bias=0.0):
        task = Task(len(self.tasks), resource, cost, list(needs), run, bias)
        self.tasks.append(task)
        return task

    def compute(self, cost, needs, run, bias=0.0):
        return self.add(CORE, cost, needs, run, bias)

    def levels(self):
        for task in self.tasks:
            for need in task.needs:
                need.users.append(task)
        for task in reversed(self.tasks):
            task.level = task.cost + max([user.level for user in task.users], default=0.0)

    def execute(self, results):
        self.levels()
        waiting = sorted(self.tasks, key=lambda task: (-task.bias, -task.level))
        values, flying, free, shown = {}, {}, {}, set()
        now, fresh = 0.0, False

        def when(task):
            times = [
                0.0 if need in values else flying[need][0] if need in flying else None
                for need in task.needs
            ]
            if None in times:
                return None
            late = max(times, default=0.0)
            return late + MARGINS[task.resource] if late > 0.0 else 0.0

        def issue(task):
            nonlocal fresh
            ended = [need for need in task.needs if need in flying]
            if task.resource in HOPPING:
                under = sorted(
                    (end, other.number, other)
                    for other, (end, _) in flying.items()
                    if other.resource in HOPPING and other not in ended
                )
                ended += [other for _, _, other in under[: max(0, len(under) + 1 - HOPS)]]
            for need in ended:
                values[need] = flying.pop(need)[1]
                self.log.append((now, 1, need))
                fresh = True
            if fresh:
                wanted = {need for other in waiting for need in other.needs}
                first = {done for done in values if done in results} - shown
                names = sorted(
                    {done for done in values if done in wanted} | first,
                    key=lambda done: done.number,
                )
                tied = lax.optimization_barrier(tuple(values[done] for done in names))
                values.update(zip(names, tied))
                shown.update(first)
                fresh = False
            waiting.remove(task)
            self.log.append((now, 0, task))
            return task.run(values)

        while waiting:
            wakes, hops, chosen = [], [], None
            for task in waiting:
                at, link = when(task), task.resource
                if at is None:
                    continue
                if link != CORE:
                    ends = sorted(
                        end for other, (end, _) in flying.items() if other.resource == link and end > now
                    )
                    if len(ends) >= DEPTHS[link]:
                        early = EARLY if link in (AHEAD, BACK) and len(ends) == 1 else 0.0
                        at = max(at, ends[-DEPTHS[link]] - early)
                    others = [
                        end
                        for other, (end, _) in flying.items()
                        if other.resource in HOPPING and other not in task.needs
                    ]
                    if link in HOPPING and len(others) >= HOPS:
                        at = max(at, sorted(others)[len(others) - HOPS] + MARGINS[SMALL])
                if at > now:
                    wakes.append(at)
                    if link in (AHEAD, BACK) or task.bias >= 10.0:
                        hops.append(at)
                elif link != CORE:
                    chosen = task
                    break
                elif chosen is None:
                    chosen = task
            soon = [at for at in hops if now < at <= now + PATIENCE]
            if chosen is None or (chosen.resource == CORE and chosen.cost > LONG and soon):
                now = min(soon) if chosen else min(wakes)
                continue
            result = issue(chosen)
            link = chosen.resource
            if link == CORE:
                values[chosen] = result
                now += chosen.cost
                fresh = True
                continue
            behind = free.get(link, 0.0) > now and link != SMALL
            end = free[link] + chosen.cost - QUEUED if behind else now + chosen.cost
            if link != SMALL:
                free[link] = end
            flying[chosen] = (end, result)
            now += STARTS[link]
        for task in results:
            if task in flying:
                values[task] = flying.pop(task)[1]
        self.log.append((now, 1, None))
        return [values[task] for task in results]


def dot_cost(rows, inner, columns):
    return 1.0 + 2.0 * rows * inner * columns / DOT_RATE


def move_cost(count):
    return 1.0 + count / 2e6


def ring_gather(plan, ring, own, count, flip=False, bias=0.0, after={}):
    blocks = {0: own}
    for link, way, step in ring.ways(flip):
        source = own
        for n, distance in enumerate(way):

            def move(v, source=source, step=step):
                return ring.hop(v[source], step)

            held = [after[link, n]] if (link, n) in after else []
            cost = HOP_COST + count * 2 / LINK_RATE
            source = plan.add(link, cost, [source, *held], move, bias)
            blocks[distance] = source
    return blocks


def ring_reduce(plan, ring, parts, count, finish, flip=False, bias=2.0, after=()):
    def total(distance, sources):
        slot = ring.slots[distance]
        part, index = next(
            (task, slot - first) for task, first, count in parts if 0 <= slot - first < count
        )
        if not sources:
            return plan.compute(0.0, [part], lambda v: v[part][index], 20.0)

        def add(v):
            terms = [v[part][index], *(v[source] for source in sources)]
            if distance:
                return add_up([(term, 0) for term in terms], halves)
            return finish(sum(term.astype(floats) for term in terms))

        cost = 0.5 + count / 3e5
        if not distance:
            cost = cost + move_cost(3 * count)
        return plan.compute(cost, [part, *sources], add, 10.0 if distance else -1.0)

    passings = []
    for link, way, step in ring.ways(flip):
        passing = []
        for distance in reversed(way):
            made = total(distance, passing)

            def move(v, made=made, step=step):
                return ring.hop(v[made], -step)

            cost = HOP_COST + count * 2 / LINK_RATE
            passing = [plan.add(link, cost, [made, *after], move, bias)]
        passings.extend(passing)
    return total(0, passings)


def params():
    return pltpu.CompilerParams(vmem_limit_bytes=VMEM_BYTES)


def add_up(terms, dtype, rows=None):
    rows = rows or terms[0][0].shape[0]
    return sum(array[first : first + rows].astype(floats) for array, first in terms).astype(dtype)


def first_norm(tokens, gain, tiles, own):
    seq_len, width = tokens.shape
    part = seq_len // tiles

    def body(own_ref, tok_ref, gain_ref, out_ref, rows_ref, factor_ref):
        whole = tok_ref[...].astype(floats)
        inverse = lax.rsqrt(jnp.mean(whole * whole, axis=-1, keepdims=True) + epsilon)
        out_ref[...] = (whole * inverse * gain_ref[...]).astype(halves)
        factor_ref[...] = jnp.broadcast_to(inverse, factor_ref.shape)

        @pl.when(pl.program_id(0) == own_ref[0])
        def _():
            rows_ref[...] = tok_ref[...]

    return pl.pallas_call(
        body,
        out_shape=(
            jax.ShapeDtypeStruct((seq_len, width), halves),
            jax.ShapeDtypeStruct((part, width), tokens.dtype),
            jax.ShapeDtypeStruct((seq_len, 128), floats),
        ),
        grid_spec=pltpu.PrefetchScalarGridSpec(
            num_scalar_prefetch=1,
            grid=(tiles,),
            in_specs=[
                pl.BlockSpec((part, width), lambda i, own_ref: (i, 0)),
                pl.BlockSpec((1, width), lambda i, own_ref: (0, 0)),
            ],
            out_specs=(
                pl.BlockSpec((part, width), lambda i, own_ref: (i, 0)),
                pl.BlockSpec((part, width), lambda i, own_ref: (0, 0)),
                pl.BlockSpec((part, 128), lambda i, own_ref: (i, 0)),
            ),
        ),
        compiler_params=params(),
        cost_estimate=HEAVY,
    )(own, tokens, gain.reshape(1, width))


def tile_of(size):
    return max(step for step in range(128, 513, 128) if size % step == 0)


def gradient_blocks(groups, order, base, count, tile, keep):
    block = groups[0][1].shape[1] // order.shape[0]
    starts, total = [], 0
    for lhs, _ in groups:
        starts.append(total)
        total += lhs.shape[0] * lhs.shape[2] // tile
    in_specs, operands = [], []
    for start, (lhs, rhs) in zip(starts, groups):
        sides, tokens, height = lhs.shape
        steps = height // tile

        def place_of(i, order_ref, start=start, sides=sides, steps=steps):
            step = jnp.clip(i - start, 0, sides * steps - 1)
            return step // steps, 0, step % steps

        def column(j, tokens=tokens):
            return pl.BlockSpec(
                (tokens, block), lambda i, order_ref: (0, order_ref[base + j])
            )

        in_specs += [pl.BlockSpec((1, tokens, tile), place_of), *(column(j) for j in range(count))]
        operands += [lhs, *([rhs] * count)]

    def body(order_ref, *refs):
        out_refs = refs[len(operands) :]
        step = pl.program_id(0)
        for n, start in enumerate(starts):
            end = starts[n + 1] if n + 1 < len(starts) else total
            lhs_ref, *rhs_refs = refs[n * (count + 1) : (n + 1) * (count + 1)]

            @pl.when(jnp.logical_and(step >= start, step < end))
            def _():
                turned = lhs_ref[0].T
                for rhs_ref, out_ref in zip(rhs_refs, out_refs):
                    product = jnp.dot(turned, rhs_ref[...], preferred_element_type=floats)
                    out_ref[...] = product[:keep].astype(halves)

    return pl.pallas_call(
        body,
        out_shape=[jax.ShapeDtypeStruct((total * keep, block), halves)] * count,
        grid_spec=pltpu.PrefetchScalarGridSpec(
            num_scalar_prefetch=1,
            grid=(total,),
            in_specs=in_specs,
            out_specs=[pl.BlockSpec((keep, block), lambda i, order_ref: (i, 0))] * count,
        ),
        compiler_params=params(),
        cost_estimate=HEAVY,
    )(order, *operands)


def matmul_across(lhs, rhs, first, count):
    tall, inner = lhs.shape
    tile = 256 if count % 256 == 0 and first % 256 == 0 else 128

    def body(lhs_ref, rhs_ref, out_ref):
        out_ref[...] = lax.dot_general(
            lhs_ref[...], rhs_ref[...], contract_last, preferred_element_type=floats
        )

    return pl.pallas_call(
        body,
        out_shape=jax.ShapeDtypeStruct((tall, count), floats),
        grid=(count // tile,),
        in_specs=[
            pl.BlockSpec((tall, inner), lambda j: (0, 0)),
            pl.BlockSpec((tile, inner), lambda j: (first // tile + j, 0)),
        ],
        out_specs=pl.BlockSpec((tall, tile), lambda j: (0, j)),
        compiler_params=params(),
        cost_estimate=HEAVY,
    )(lhs, rhs)


def halves_spec(parts, inner, tall, tile):
    half, part = tall // inner, tall // parts

    def put(places_ref, product, own_ref, other_ref):
        for a in range(parts):
            rows = product[a * part : (a + 1) * part]
            place = places_ref[a]

            @pl.when(place < parts // inner)
            def _():
                own_ref[pl.ds(pl.multiple_of(place * part, part), part)] = rows

            if inner > 1:

                @pl.when(place >= parts // inner)
                def _():
                    at = pl.multiple_of(place * part - half, part)
                    other_ref[pl.ds(at, part)] = rows.astype(halves)

    return half, pl.BlockSpec((half, tile), lambda j, p: (0, j)), put


def matmul_halves(lhs, rhs, places, inner, first=0, scaled=None):
    tall, depth = lhs.shape
    wide = rhs.shape[1]
    tile = 256 if wide % 256 == 0 else 128
    half, spec, put = halves_spec(places.shape[0], inner, tall, tile)

    def body(places_ref, lhs_ref, rhs_ref, *refs):
        product = jnp.dot(lhs_ref[...], rhs_ref[...], preferred_element_type=floats)
        put(places_ref, product, *refs[len(scaled or ()) :][:2])
        if scaled:
            array_ref, factor_ref, sums_ref = refs[0], refs[1], refs[-1]
            terms = product * array_ref[...].astype(floats) * factor_ref[:, :1]
            sums_ref[...] = jnp.sum(terms.reshape(tall // 8, 8, tile), axis=0)

    more_in, more_out, more_shapes = [], [], []
    if scaled:
        more_in = [
            pl.BlockSpec((tall, tile), lambda j, p: (0, j)),
            pl.BlockSpec(scaled[1].shape, lambda j, p: (0, 0)),
        ]
        more_out = [pl.BlockSpec((8, tile), lambda j, p: (0, j))]
        more_shapes = [jax.ShapeDtypeStruct((8, wide), floats)]
    return pl.pallas_call(
        body,
        out_shape=(
            jax.ShapeDtypeStruct((half, wide), floats),
            jax.ShapeDtypeStruct((half, wide), halves),
            *more_shapes,
        ),
        grid_spec=pltpu.PrefetchScalarGridSpec(
            num_scalar_prefetch=1,
            grid=(wide // tile,),
            in_specs=[
                pl.BlockSpec((tall, depth), lambda j, p: (0, 0)),
                pl.BlockSpec((depth, tile), lambda j, p: (first // depth, j)),
                *more_in,
            ],
            out_specs=(spec, spec, *more_out),
        ),
        compiler_params=params(),
        cost_estimate=HEAVY,
    )(places, lhs, rhs, *(scaled or ()))


def gated_forward(normed, weights):
    tokens, inner = normed.shape
    hidden = weights.shape[1] // 2
    tile = 256 if hidden % 256 == 0 else 128
    steps = hidden // tile

    def body(in_ref, gate_ref, up_ref, gate_out, up_out, hidden_out):
        gate = jnp.dot(in_ref[...], gate_ref[...], preferred_element_type=floats)
        up = jnp.dot(in_ref[...], up_ref[...], preferred_element_type=floats)
        gate_out[...] = gate
        up_out[...] = up
        hidden_out[...] = (gelu(gate) * up).astype(halves)

    column = pl.BlockSpec((tokens, tile), lambda j: (0, j))
    return pl.pallas_call(
        body,
        out_shape=(
            jax.ShapeDtypeStruct((tokens, hidden), floats),
            jax.ShapeDtypeStruct((tokens, hidden), floats),
            jax.ShapeDtypeStruct((tokens, hidden), halves),
        ),
        grid=(steps,),
        in_specs=[
            pl.BlockSpec((tokens, inner), lambda j: (0, 0)),
            pl.BlockSpec((inner, tile), lambda j: (0, j)),
            pl.BlockSpec((inner, tile), lambda j: (0, steps + j)),
        ],
        out_specs=(column, column, column),
        compiler_params=params(),
        cost_estimate=HEAVY,
    )(normed, weights, weights)


def gated_backward(cotangent, down, gate, up):
    tokens, inner = cotangent.shape
    hidden = down.shape[0]
    tile = 256 if hidden % 256 == 0 else 128

    def body(cot_ref, down_ref, gate_ref, up_ref, out_ref):
        back = lax.dot_general(
            cot_ref[...], down_ref[...], contract_last, preferred_element_type=floats
        )
        active, slope = gelu_parts(gate_ref[...])
        out_ref[0] = (back * up_ref[...] * slope).astype(halves)
        out_ref[1] = (back * active).astype(halves)

    column = pl.BlockSpec((tokens, tile), lambda j: (0, j))
    return pl.pallas_call(
        body,
        out_shape=jax.ShapeDtypeStruct((2, tokens, hidden), halves),
        grid=(hidden // tile,),
        in_specs=[
            pl.BlockSpec((tokens, inner), lambda j: (0, 0)),
            pl.BlockSpec((tile, inner), lambda j: (j, 0)),
            column,
            column,
        ],
        out_specs=pl.BlockSpec((2, tokens, tile), lambda j: (0, 0, j)),
        compiler_params=params(),
        cost_estimate=HEAVY,
    )(cotangent, down, gate, up)


def pair_halves(pair, weights, places, inner):
    _, tall, hidden = pair.shape
    wide = weights.shape[0]
    tile = 256 if wide % 256 == 0 else 128
    half, spec, put = halves_spec(places.shape[0], inner, tall, tile)

    def body(places_ref, pair_ref, gate_ref, up_ref, own_ref, other_ref):
        product = 0.0
        for side, ref in enumerate((gate_ref, up_ref)):
            product = product + lax.dot_general(
                pair_ref[side], ref[...], contract_last, preferred_element_type=floats
            )
        put(places_ref, product, own_ref, other_ref)

    weight = lambda side: pl.BlockSpec((tile, hidden), lambda j, p: (j, side))
    return pl.pallas_call(
        body,
        out_shape=(
            jax.ShapeDtypeStruct((half, wide), floats),
            jax.ShapeDtypeStruct((half, wide), halves),
        ),
        grid_spec=pltpu.PrefetchScalarGridSpec(
            num_scalar_prefetch=1,
            grid=(wide // tile,),
            in_specs=[pl.BlockSpec((2, tall, hidden), lambda j, p: (0, 0, 0)), weight(0), weight(1)],
            out_specs=(spec, spec),
        ),
        compiler_params=params(),
        cost_estimate=HEAVY,
    )(places, pair, weights, weights)


def segment_of(places, ends_ref):
    segment = jnp.zeros(places.shape, jnp.int32)
    for j in range(ends_ref.shape[0] - 1):
        segment = segment + (places >= ends_ref[j]).astype(jnp.int32)
    return segment


def same_behind(places, ends_ref, offset):
    agree = segment_of(places, ends_ref) == segment_of(places - offset, ends_ref)
    return jnp.logical_and(agree, places >= offset).astype(floats)


def same_ahead(places, ends_ref, offset, seq_len):
    agree = segment_of(places, ends_ref) == segment_of(places + offset, ends_ref)
    return jnp.logical_and(agree, places + offset < seq_len).astype(floats)


def lane_chunks(width):
    step = 256 if width % 256 == 0 else 128
    return [slice(at, at + step) for at in range(0, width, step)]


def gate_values(pre_a, pre_i, decay8):
    rate = jax.nn.sigmoid(pre_a)
    admit = jax.nn.sigmoid(pre_i)
    power = decay8 * rate
    alpha = jnp.exp(-power)
    twice = 2.0 * power
    series = 1.0 - twice * (1.0 / 7.0)
    for order in (6.0, 5.0, 4.0, 3.0, 2.0):
        series = 1.0 - (twice * (1.0 / order)) * series
    raw = jnp.where(twice < 0.5, twice * series, 1.0 - alpha * alpha)
    one_minus = jnp.maximum(raw, floor_value)
    inverse = lax.rsqrt(one_minus)
    return rate, admit, alpha, raw, one_minus * inverse, inverse


def gelu_parts(value):
    square = value * value
    bend = jnp.tanh(gelu_root * (value + gelu_cube * (square * value)))
    half = 0.5 * (1.0 + bend)
    slope = half + 0.5 * value * (1.0 - bend * bend) * (
        gelu_root * (1.0 + 3.0 * gelu_cube * square)
    )
    return value * half, slope


def gelu(value):
    return gelu_parts(value)[0]


def recur_forward(branches, doc_ends, vectors, gates, tiles):
    seq_len, lanes = branches.shape[0], branches.shape[1] // 2
    part = seq_len // tiles
    chunks = lane_chunks(lanes)

    def body(
        ends_ref, x_ref, y_ref, vec_ref, gate_ref,
        mixed_ref, conv_ref, pre_ref, prev_ref, xs, carry,
    ):
        tile = pl.program_id(0)

        @pl.when(tile == 0)
        def _():
            xs[0:8] = jnp.zeros((8, lanes), floats)
            carry[...] = jnp.zeros_like(carry)

        xs[8 : 8 + part] = x_ref[...]
        rows = lax.broadcasted_iota(jnp.int32, (CHUNK, 1), 0)

        def convolve(c, _):
            at = pl.multiple_of(c * CHUNK, CHUNK)
            here = tile * part + at + rows
            same = [same_behind(here, ends_ref, k) for k in range(1, 4)]
            for lane in chunks:
                window = xs[pl.ds(at, CHUNK + 8), lane]
                total = vec_ref[4:5, lane] + vec_ref[0:1, lane] * window[8:]
                for k in range(1, 4):
                    moved = pltpu.roll(window, k, 0)[8:]
                    total = total + vec_ref[k : k + 1, lane] * moved * same[k - 1]
                conv_ref[pl.ds(at, CHUNK), lane] = total.astype(halves)
            return 0

        lax.fori_loop(0, part // CHUNK, convolve, 0)
        xs[0:8] = xs[part : part + 8]
        pre_ref[...] = jnp.dot(conv_ref[...], gate_ref[...], preferred_element_type=floats)

        def advance(c, entering):
            at = pl.multiple_of(c * CHUNK, CHUNK)
            here = tile * part + at + rows
            fresh = 1.0 - same_behind(here, ends_ref, 1)
            leaving = []
            for state, lane in zip(entering, chunks):
                span = lane.stop - lane.start
                shift_lane = slice(lane.start + lanes, lane.stop + lanes)
                pre_a = pre_ref[pl.ds(at, CHUNK), lane] + vec_ref[6:7, lane]
                pre_i = pre_ref[pl.ds(at, CHUNK), shift_lane] + vec_ref[7:8, lane]
                pre_ref[pl.ds(at, CHUNK), lane] = pre_a
                pre_ref[pl.ds(at, CHUNK), shift_lane] = pre_i
                conv_in = conv_ref[pl.ds(at, CHUNK), lane].astype(floats)
                _, admit, alpha, _, root, _ = gate_values(pre_a, pre_i, vec_ref[5:6, lane])
                keep = 1.0 - fresh
                coef = alpha * keep
                drive = (fresh + root * keep) * admit * conv_in
                index = lax.broadcasted_iota(jnp.int32, (CHUNK, span), 0)
                for d in (1, 2, 4):
                    inside = (index & 7) >= d
                    drive = jnp.where(inside, drive + coef * pltpu.roll(drive, d, 0), drive)
                    coef = jnp.where(inside, coef * pltpu.roll(coef, d, 0), coef)
                groups = []
                first = state
                for g in range(CHUNK // 8):
                    group = slice(g * 8, g * 8 + 8)
                    groups.append(coef[group] * state + drive[group])
                    state = groups[-1][7:8]
                states = jnp.concatenate(groups, axis=0)
                prev_ref[pl.ds(at, CHUNK), lane] = jnp.where(
                    index == 0, first, pltpu.roll(states, 1, 0)
                )
                mixed = states * gelu(y_ref[pl.ds(at, CHUNK), lane])
                mixed_ref[pl.ds(at, CHUNK), lane] = mixed.astype(halves)
                leaving.append(state)
            return tuple(leaving)

        ended = lax.fori_loop(
            0, part // CHUNK, advance, tuple(carry[0:1, lane] for lane in chunks)
        )
        for state, lane in zip(ended, chunks):
            carry[0:1, lane] = state

    own = lambda column: pl.BlockSpec((part, lanes), lambda i, e: (i, column))
    straight = lambda width: pl.BlockSpec((part, width), lambda i, e: (i, 0))
    whole = lambda array: pl.BlockSpec(array.shape, lambda i, e: (0, 0))
    return pl.pallas_call(
        body,
        out_shape=(
            jax.ShapeDtypeStruct((seq_len, lanes), halves),
            jax.ShapeDtypeStruct((seq_len, lanes), halves),
            jax.ShapeDtypeStruct((seq_len, 2 * lanes), floats),
            jax.ShapeDtypeStruct((seq_len, lanes), floats),
        ),
        grid_spec=pltpu.PrefetchScalarGridSpec(
            num_scalar_prefetch=1,
            grid=(tiles,),
            in_specs=[own(0), own(1), whole(vectors), whole(gates)],
            out_specs=(own(0), straight(lanes), straight(2 * lanes), straight(lanes)),
            scratch_shapes=[pltpu.VMEM((part + 8, lanes), floats), pltpu.VMEM((8, lanes), floats)],
        ),
        compiler_params=params(),
        cost_estimate=HEAVY,
    )(doc_ends, branches, branches, vectors, gates)


def recur_backward(back_mixed, branches, conv_in, pre, previous, doc_ends, vectors, gates, tiles):
    seq_len, lanes = conv_in.shape
    part = seq_len // tiles
    chunks = lane_chunks(lanes)
    steps = part // CHUNK

    def body(
        ends_ref, bm_ref, x_ref, y_ref, conv_ref, pre_ref, prev_ref, vec_ref, gate_ref,
        bxy_ref, bai_ref, sums_ref, ahead, sums, carry,
    ):
        tile = tiles - 1 - pl.program_id(0)

        @pl.when(pl.program_id(0) == 0)
        def _():
            ahead[part : part + 8] = jnp.zeros((8, lanes), floats)
            sums[...] = jnp.zeros_like(sums)
            carry[...] = jnp.zeros_like(carry)

        rows = lax.broadcasted_iota(jnp.int32, (CHUNK, 1), 0)

        def add_rows(which, lane, value):
            for g in range(CHUNK // 8):
                sums[which * 8 : which * 8 + 8, lane] += value[g * 8 : g * 8 + 8]

        def retreat(c, entering):
            at = pl.multiple_of((steps - 1 - c) * CHUNK, CHUNK)
            span_rows = pl.ds(at, CHUNK)
            here = tile * part + at + rows
            keep = same_behind(here, ends_ref, 1)
            fresh = 1.0 - keep
            leaving = []
            for (back_next, coef_next), lane in zip(entering, chunks):
                span = lane.stop - lane.start
                shift_lane = slice(lane.start + lanes, lane.stop + lanes)
                decay8 = vec_ref[5:6, lane]
                rate, admit, alpha, raw, root, inverse = gate_values(
                    pre_ref[span_rows, lane], pre_ref[span_rows, shift_lane], decay8
                )
                conv = conv_ref[span_rows, lane].astype(floats)
                before = prev_ref[span_rows, lane]
                scale_in = fresh + root * keep
                coef = alpha * keep
                driven = scale_in * admit
                states = coef * before + driven * conv
                active, slope = gelu_parts(y_ref[span_rows, lane])
                back_mix = bm_ref[span_rows, lane]
                bxy_ref[span_rows, shift_lane] = (back_mix * states * slope).astype(halves)
                index = lax.broadcasted_iota(jnp.int32, (CHUNK, span), 0)
                back = back_mix * active
                chain = jnp.where(index == CHUNK - 1, coef_next, pltpu.roll(coef, CHUNK - 1, 0))
                for d in (1, 2, 4):
                    inside = (index & 7) < 8 - d
                    back = jnp.where(inside, back + chain * pltpu.roll(back, CHUNK - d, 0), back)
                    chain = jnp.where(inside, chain * pltpu.roll(chain, CHUNK - d, 0), chain)
                groups = []
                for g in reversed(range(CHUNK // 8)):
                    group = slice(g * 8, g * 8 + 8)
                    groups.insert(0, back[group] + chain[group] * back_next)
                    back_next = groups[0][0:1]
                back_state = jnp.concatenate(groups, axis=0)
                through = back_state * conv
                bound = jnp.where(raw > floor_value, through * admit * alpha * inverse, 0.0)
                back_alpha = (back_state * before - bound) * keep * alpha
                add_rows(5, lane, back_alpha * rate)
                back_a = (back_alpha * (-decay8) * rate * (1.0 - rate)).astype(halves)
                back_i = (through * scale_in * admit * (1.0 - admit)).astype(halves)
                add_rows(6, lane, back_a.astype(floats))
                add_rows(7, lane, back_i.astype(floats))
                bai_ref[span_rows, lane] = back_a
                bai_ref[span_rows, shift_lane] = back_i
                ahead[span_rows, lane] = back_state * driven
                leaving.append((back_next, coef[0:1]))
            return tuple(leaving)

        ended = lax.fori_loop(
            0, steps, retreat, tuple((carry[0:1, lane], carry[8:9, lane]) for lane in chunks)
        )
        for (back_next, coef_next), lane in zip(ended, chunks):
            carry[0:1, lane] = back_next
            carry[8:9, lane] = coef_next

        ahead[0:part] += lax.dot_general(
            bai_ref[...], gate_ref[...], contract_last, preferred_element_type=floats
        )

        def convolve(c, _):
            at = pl.multiple_of(c * CHUNK, CHUNK)
            here = tile * part + at + rows
            same = [same_ahead(here, ends_ref, k, seq_len) for k in range(1, 4)]
            for lane in chunks:
                window = ahead[pl.ds(at, CHUNK + 8), lane]
                x_part = x_ref[pl.ds(at, CHUNK), lane]
                direct = window[:CHUNK]
                back_x = vec_ref[0:1, lane] * direct
                add_rows(0, lane, x_part * direct)
                add_rows(4, lane, direct)
                for k in range(1, 4):
                    moved = pltpu.roll(window, CHUNK + 8 - k, 0)[:CHUNK] * same[k - 1]
                    back_x = back_x + vec_ref[k : k + 1, lane] * moved
                    add_rows(k, lane, x_part * moved)
                bxy_ref[pl.ds(at, CHUNK), lane] = back_x.astype(halves)
            return 0

        lax.fori_loop(0, steps, convolve, 0)
        ahead[part : part + 8] = ahead[0:8]

        @pl.when(pl.program_id(0) == tiles - 1)
        def _():
            for which in range(8):
                sums_ref[which : which + 1] = jnp.sum(
                    sums[which * 8 : which * 8 + 8], axis=0, keepdims=True
                )

    own = lambda width, column: pl.BlockSpec((part, width), lambda i, e: (tiles - 1 - i, column))
    straight = lambda width: pl.BlockSpec((part, width), lambda i, e: (tiles - 1 - i, 0))
    whole = lambda array: pl.BlockSpec(array.shape, lambda i, e: (0, 0))
    return pl.pallas_call(
        body,
        out_shape=(
            jax.ShapeDtypeStruct((seq_len, 2 * lanes), halves),
            jax.ShapeDtypeStruct((seq_len, 2 * lanes), halves),
            jax.ShapeDtypeStruct((8, lanes), floats),
        ),
        grid_spec=pltpu.PrefetchScalarGridSpec(
            num_scalar_prefetch=1,
            grid=(tiles,),
            in_specs=[
                own(lanes, 0), own(lanes, 0), own(lanes, 1),
                straight(lanes), straight(2 * lanes), straight(lanes),
                whole(vectors), whole(gates),
            ],
            out_specs=(
                own(2 * lanes, 0), straight(2 * lanes), pl.BlockSpec((8, lanes), lambda i, e: (0, 0)),
            ),
            scratch_shapes=[
                pltpu.VMEM((part + 8, lanes), floats),
                pltpu.VMEM((64, lanes), floats),
                pltpu.VMEM((16, lanes), floats),
            ],
        ),
        compiler_params=params(),
        cost_estimate=HEAVY,
    )(doc_ends, back_mixed, branches, branches, conv_in, pre, previous, vectors, gates)


def rms_norm(inputs, scales):
    return inputs * lax.rsqrt(jnp.mean(inputs * inputs, axis=-1, keepdims=True) + epsilon) * scales


def inner_of(count):
    return max(d for d in range(1, count + 1) if count % d == 0 and d * d <= count)


def on_device(
    tokens,
    doc_lengths,
    gain_mix,
    value_weight,
    branch_weight,
    conv_weight,
    conv_bias,
    recur_gate,
    input_gate,
    recur_bias,
    input_bias,
    decay_param,
    out_weight,
    gain_ffn,
    gate_weight,
    up_weight,
    down_weight,
    cotangent,
):
    seq_len, _, width = tokens.shape
    heads, head_width = recur_gate.shape[:2]
    channels = value_weight.shape[1]
    hidden_width = gate_weight.shape[1]
    lanes = round_up(channels, 128)
    sent = round_up(channels, 16)
    dp = Ring(DP, inner_of(lax.axis_size(DP)))
    parts = lax.axis_size(CHAN)
    part = seq_len // parts
    block = width // dp.count
    order = dp.order()
    chan = lax.axis_index(CHAN)
    own_tile = chan.reshape(1).astype(jnp.int32)
    cores = 2 if parts % 2 == 0 else 1
    chips = parts // cores
    tiles = jnp.arange(parts, dtype=jnp.int32)
    row_places = ((tiles - chan) % cores) * chips + (tiles // cores - chan // cores) % chips
    doc_ends = jnp.cumsum(doc_lengths[0])
    plan = Plan()
    compute = plan.compute

    def gather_weight(own, count, flip, bias, after, put):
        blocks = ring_gather(plan, dp, own, count, flip, bias, after)
        full = None
        for distance in sorted(blocks, key=lambda d: min(d, dp.count - d)):

            def extend(v, before=full, piece=blocks[distance], slot=dp.slots[distance]):
                return put(
                    None if before is None else v[before], v[piece], order[slot : slot + 1]
                )

            needs = [blocks[distance]] if full is None else [full, blocks[distance]]
            first = 0.0 if full else 6.0
            full = compute(0.6 + count / 2.6e5 + first, needs, extend)
        return full, blocks

    def put_mix(full, piece, at):
        if full is None:
            full = jnp.zeros((3 * lanes, width), halves), jnp.zeros((hidden_width, width), halves)
        mix, down = full
        for i in range(3):
            rows = piece[i * sent : (i + 1) * sent]
            mix = lax.dynamic_update_slice(mix, rows, (i * lanes, at[0] * block))
        return mix, lax.dynamic_update_slice(down, piece[3 * sent :], (0, at[0] * block))

    def put_rows(full, piece, at):
        if full is None:
            full = jnp.zeros((width, 2 * hidden_width), halves)
        return lax.dynamic_update_slice(full, piece, (at[0] * block, 0))

    def mix_of(value, branch, out, down):
        pieces = [pad_dim(array, 0, sent) for array in (value.T, branch.T, out)]
        return jnp.concatenate([*pieces, down], axis=0)

    mix = compute(
        3.0, [], lambda v: mix_of(value_weight, branch_weight, out_weight, down_weight), 8.0
    )
    both_own = compute(2.0, [], lambda v: jnp.concatenate([gate_weight, up_weight], axis=1), 1.0)
    mix_full, mix_blocks = gather_weight(
        mix, (3 * sent + hidden_width) * block, False, 9.0, {}, put_mix
    )
    far = dp.count // 2
    both_full, _ = gather_weight(
        both_own, 2 * hidden_width * block, True, 8.0,
        {(AHEAD, 0): mix_blocks[far], (BACK, 0): mix_blocks[far + 1]}, put_rows,
    )

    def spread(gate):
        total = 0.0
        for h in range(heads):
            low = h * head_width
            total = total + jnp.pad(gate[h], ((low, lanes - low - head_width),) * 2)
        return total

    def small_parameters(v):
        gates = jnp.concatenate([spread(recur_gate), spread(input_gate)], axis=1)
        vectors = [
            conv_weight,
            conv_bias[None],
            decay_scale * jax.nn.softplus(decay_param)[None],
            recur_bias[None],
            input_bias[None],
        ]
        return gates, pad_dim(jnp.concatenate(vectors, axis=0), 1, lanes)

    small = compute(8.0, [], small_parameters)

    def cross(value, step):
        pairs = [
            (x * cores + c, ((x + step) % chips) * cores + c)
            for x in range(chips)
            for c in range(cores)
        ]
        return lax.ppermute(value, CHAN, pairs)

    def swap(value):
        pairs = [(x * cores + c, x * cores + (c + 1) % cores) for x in range(chips) for c in range(cores)]
        return lax.ppermute(value, CHAN, pairs)

    def gather_rows(own):
        return plan.add(
            CHIPS, 33.0, [own], lambda v: lax.all_gather(v[own], CHAN, axis=0, tiled=True)
        )

    def reduce_rows(product, after=()):
        terms = []
        if cores > 1:
            terms = [plan.add(TWIN, 9.0, [product, *after], lambda v: swap(v[product][1]), 3.0)]
        passing = []
        for s in reversed(range(chips)):

            def add(v, s=s, passing=tuple(passing)):
                pieces = [(v[product][0], s * part), *((v[term], s * part) for term in terms)]
                pieces += [(v[term], 0) for term in passing]
                return add_up(pieces, halves if s else floats, part)

            made = compute(2.8, [product, *terms, *passing], add, 10.0)
            if s:
                passing = [
                    plan.add(CROSS, 26.5, [made], lambda v, made=made: cross(v[made], 1), 3.0)
                ]
        return made

    def small_total(source, axes):
        for axis in axes:
            count = lax.axis_size(axis)
            assert count & (count - 1) == 0
            bit = 1
            while bit < count:
                pairs = [(i, i ^ bit) for i in range(count)]

                def send(v, source=source, axis=axis, pairs=pairs):
                    return lax.ppermute(v[source], axis, pairs)

                other = plan.add(SMALL, 26.0 if axis == DP else 8.0, [source], send)

                def add(v, source=source, other=other):
                    return v[source] + v[other]

                source = compute(0.5, [source, other], add)
                bit *= 2
        return source

    norm_in = compute(
        5.0, [], lambda v: first_norm(tokens.reshape(seq_len, width), gain_mix, parts, own_tile)
    )
    cot = compute(1.5, [], lambda v: cotangent.reshape(part, width))
    cot_full = gather_rows(cot)
    branches = compute(
        10.8,
        [norm_in, mix_full],
        lambda v: matmul_across(v[norm_in][0], v[mix_full][0], 0, 2 * lanes),
    )
    recur = compute(
        20.2,
        [branches, small],
        lambda v: recur_forward(v[branches], doc_ends, v[small][1], v[small][0], parts),
    )
    mixed = compute(0.0, [recur], lambda v: v[recur][0], 30.0)
    mixed_out = compute(
        9.2,
        [mixed, mix_full],
        lambda v: matmul_halves(v[mixed], v[mix_full][0], row_places, cores, 2 * lanes),
    )
    branch_out = reduce_rows(mixed_out)

    def middle_of(v):
        residual = v[norm_in][1].astype(floats) + v[branch_out]
        return residual, rms_norm(residual, gain_ffn).astype(halves)

    middle = compute(3.0, [norm_in, branch_out], middle_of)
    mid = compute(0.0, [middle], lambda v: v[middle][1], 30.0)
    mid_full = gather_rows(mid)

    gated = compute(
        19.7,
        [mid_full, both_full],
        lambda v: gated_forward(v[mid_full], v[both_full]),
    )
    hidden = compute(0.0, [gated], lambda v: v[gated][2], 30.0)

    def gradient(needs, groups, tile, keep, quarters, costs, bias):
        first, parts = 0, []
        for n, (quarter, cost) in enumerate(zip(quarters, costs)):
            count = quarter * dp.count // 4

            def blocks(v, first=first, count=count):
                return gradient_blocks(groups(v), order, first, count, tile, keep)

            parts.append((compute(cost, needs, blocks, -0.5 * n if n else bias), first, count))
            first += count
        return parts

    back_both = compute(
        14.7,
        [gated, cot_full, mix_full],
        lambda v: gated_backward(v[cot_full], v[mix_full][1], *v[gated][:2]),
    )
    back_product = compute(
        20.5,
        [back_both, both_full],
        lambda v: pair_halves(v[back_both], v[both_full], row_places, cores),
    )
    back_mid = reduce_rows(back_product)
    tile = tile_of(hidden_width)
    grad_ffn = ring_reduce(
        plan,
        dp,
        gradient(
            [hidden, cot_full, back_both, mid_full],
            lambda v: [(v[hidden][None], v[cot_full]), (v[back_both], v[mid_full])],
            tile, tile, (1, 1, 2), (12.0, 12.0, 17.5), 2.0,
        ),
        3 * hidden_width * block,
        lambda total: (
            total[:hidden_width],
            total[hidden_width : 2 * hidden_width].T,
            total[2 * hidden_width :].T,
        ),
        False,
    )
    ffn_product = compute(
        12.0,
        [hidden, mix_full],
        lambda v: matmul_halves(v[hidden], v[mix_full][1], row_places, cores),
        -2.0,
    )

    def norm_back(inputs, gain, back):
        scale = lax.rsqrt(jnp.mean(inputs * inputs, axis=-1, keepdims=True) + epsilon)
        scaled = back * gain
        mean = jnp.mean(scaled * inputs, axis=-1, keepdims=True)
        through = scale * scaled - inputs * (scale * scale * scale * mean)
        return through

    def back_middle_of(v):
        residual, back = v[middle][0], v[back_mid]
        scale = lax.rsqrt(jnp.mean(residual * residual, axis=-1, keepdims=True) + epsilon)
        gain = jnp.sum((back * residual * scale).reshape(part // 8, 8, width), axis=0)
        back = v[cot].astype(floats) + norm_back(residual, gain_ffn, back)
        return back, back.astype(halves), gain

    back_middle = compute(4.0, [middle, back_mid, cot], back_middle_of)
    back_resid = compute(0.0, [back_middle], lambda v: v[back_middle][1], 30.0)
    branch_full = gather_rows(back_resid)
    ffn_out = reduce_rows(ffn_product, [branch_full])
    output = compute(
        4.0, [middle, ffn_out], lambda v: (v[middle][0] + v[ffn_out]).astype(halves), -1.0
    )
    back_mixed = compute(
        6.7,
        [branch_full, mix_full],
        lambda v: matmul_across(v[branch_full], v[mix_full][0], 2 * lanes, lanes),
    )
    recur_back = compute(
        26.5,
        [back_mixed, branches, recur, small],
        lambda v: recur_backward(
            v[back_mixed], v[branches], *v[recur][1:], doc_ends, v[small][1], v[small][0], parts
        ),
    )
    grad_mix = ring_reduce(
        plan,
        dp,
        gradient(
            [recur_back, norm_in, mixed, branch_full],
            lambda v: [(v[recur_back][0][None], v[norm_in][0]), (v[mixed][None], v[branch_full])],
            lanes, sent, (1, 3), (6.0, 14.0), 4.0,
        ),
        3 * sent * block,
        lambda total: (
            total[:channels].T,
            total[sent : sent + channels].T,
            total[2 * sent : 2 * sent + channels],
        ),
        True,
    )
    back_pair = compute(
        13.0,
        [recur_back, mix_full, norm_in],
        lambda v: matmul_halves(
            v[recur_back][0], v[mix_full][0], row_places, cores, 0,
            (tokens.reshape(seq_len, width), v[norm_in][2]),
        ),
        2.0,
    )
    back_norm_in = reduce_rows(back_pair)

    def back_first_of(v):
        through = norm_back(v[norm_in][1].astype(floats), gain_mix, v[back_norm_in])
        return v[back_middle][0] + through

    back_first = compute(5.0, [norm_in, back_norm_in, back_middle], back_first_of)

    def gate_grads_of(v):
        whole = lax.dot_general(
            v[recur][1], v[recur_back][1], contract_first, preferred_element_type=floats
        )
        return jnp.stack(
            [
                whole[
                    h * head_width : (h + 1) * head_width,
                    side * lanes + h * head_width : side * lanes + (h + 1) * head_width,
                ]
                for side in range(2)
                for h in range(heads)
            ]
        )

    gate_terms = compute(
        5.0, [recur, recur_back], lambda v: gate_grads_of(v).astype(halves), 3.5
    )
    gate_sums = plan.add(CHIPS, 110.0, [gate_terms], lambda v: lax.psum(v[gate_terms], DP), 3.0)
    gate_result = compute(
        4.0, [gate_sums], lambda v: tuple(jnp.split(v[gate_sums].astype(floats), 2)), -5.0
    )

    def both_gains(v):
        gains = [jnp.sum(terms, axis=0).reshape(8, -1) for terms in (v[back_middle][2], v[back_pair][2])]
        return jnp.concatenate(gains, axis=1)

    gain_rows = small_total(compute(2.0, [back_middle, back_pair], both_gains, 1.0), [CHAN])
    sums = small_total(
        compute(
            1.0,
            [recur_back, gain_rows],
            lambda v: jnp.concatenate([v[recur_back][2], v[gain_rows]], axis=1),
        ),
        [DP],
    )

    def sum_results_of(v):
        total = v[sums][:, :channels]
        decay = total[5] * (-decay_scale * jax.nn.sigmoid(decay_param))
        gains = v[sums][:, lanes:]
        return (
            total[:4], total[4], total[6], total[7], decay,
            gains[:, : width // 8].reshape(width), gains[:, width // 8 :].reshape(width),
        )

    sum_results = compute(3.0, [sums], sum_results_of)

    done = plan.execute(
        [
            output, back_first, grad_mix, sum_results, gate_result, grad_ffn,
        ]
    )
    output, first, (value, branch, out), summed, (recur, admit), (down, gate, up) = done
    return (
        output.reshape(part, 1, width),
        first.reshape(part, 1, width),
        summed[6],
        value,
        branch,
        summed[0],
        summed[1],
        recur,
        admit,
        summed[2],
        summed[3],
        summed[4],
        out,
        summed[5],
        gate,
        up,
        down,
    )


def solution(mesh):
    tokens, split, columns = P(None, DP, None), P(DP, CHAN), P(CHAN, DP)
    own, channels, heads = P(CHAN, DP, None), P(CHAN), P(CHAN, None, None)
    in_specs = (
        tokens, P(DP, None), P(), split, split, P(None, CHAN), channels, heads, heads,
        channels, channels, channels, columns, P(), split, split, columns, own,
    )
    out_specs = (
        own, own, P(), split, split, P(None, CHAN), channels, heads, heads,
        channels, channels, channels, columns, P(), split, split, columns,
    )
    return jax.shard_map(
        on_device, mesh=mesh, in_specs=in_specs, out_specs=out_specs, check_vma=False
    )
```

```python
from functools import partial

import jax
import jax.numpy as jnp
from jax import lax
from jax.experimental import pallas as pl
from jax.experimental.pallas import tpu as pltpu
from jax.sharding import PartitionSpec as P

epsilon = 1e-06
decay_scale = 8.0
floor_value = 0.0001
gelu_root = 0.7978845608
gelu_cube = 0.044715
floats = jnp.float32
halves = jnp.bfloat16
contract_last = (((1,), (1,)), ((), ()))
contract_first = (((0,), (0,)), ((), ()))
CHUNK = 16
DP, CHAN = "dp", "chan"
VMEM_BYTES = 48 * 1024 * 1024
HEAVY = pl.CostEstimate(flops=2 * 10**11, bytes_accessed=1, transcendentals=0)


def round_up(number, unit):
    return -(-number // unit) * unit


def pad_dim(array, axis, size):
    widths = [(0, 0)] * array.ndim
    widths[axis] = (0, size - array.shape[axis])
    return jnp.pad(array, widths)


class Ring:
    def __init__(self, axis, inner):
        self.axis = axis
        self.count = lax.axis_size(axis)
        outer = self.count // inner
        self.path = [(o, 0) for o in range(outer)]
        for n, o in enumerate(reversed(range(outer))):
            columns = list(range(1, inner))
            self.path += [(o, i) for i in (reversed(columns) if n % 2 else columns)]
        self.path = [o * inner + i for o, i in self.path]
        spots = [self.path.index(i) for i in range(self.count)]
        self.spot = self.look(spots, lax.axis_index(axis))
        far = self.count // 2
        self.distances = [far]
        for j in range(1, far):
            self.distances += [far + j, far - j]
        self.distances += [0]
        self.slots = {distance: j for j, distance in enumerate(self.distances)}

    def look(self, table, index):
        return sum(jnp.where(index == i, entry, 0) for i, entry in enumerate(table))

    def hop(self, value, step):
        pairs = [
            (self.path[n], self.path[(n + step) % self.count]) for n in range(self.count)
        ]
        return lax.ppermute(value, self.axis, pairs)

    def order(self):
        ahead = self.look(self.distances, jnp.arange(self.count, dtype=jnp.int32))
        return self.look(self.path, (self.spot + ahead) % self.count).astype(jnp.int32)

    def ways(self, flip):
        ahead = (self.count - 1) // 2 if flip else self.count // 2
        return [
            (AHEAD, list(range(1, ahead + 1)), -1),
            (BACK, list(range(self.count - 1, ahead, -1)), 1),
        ]


LINK_RATE = 46e3
HOP_COST = 3.5
EARLY = 0.0
QUEUED = 2.5
CORE, AHEAD, BACK, CHIPS, CROSS, TWIN, SMALL = range(7)
DEPTHS = {AHEAD: 1, BACK: 1, CHIPS: 9, CROSS: 1, TWIN: 1, SMALL: 2}
STARTS = {AHEAD: 1.5, BACK: 0.8, CHIPS: 0.5, CROSS: 1.5, TWIN: 1.5, SMALL: 2.0}
HOPPING = (AHEAD, BACK, CROSS, TWIN, SMALL)
HOPS = 5
PATIENCE, LONG = 6.0, 8.0
MARGINS = {CORE: 3.0, AHEAD: 1.5, BACK: 1.5, CHIPS: 1.0, CROSS: 0.5, TWIN: 0.5, SMALL: 2.0}


class Task:
    def __init__(self, number, resource, cost, needs, run, bias):
        self.number, self.resource, self.cost, self.needs = number, resource, cost, needs
        self.run, self.bias, self.level, self.users = run, bias, 0.0, []


class Plan:
    def __init__(self):
        self.tasks, self.log = [], []

    def add(self, resource, cost, needs, run, bias=0.0):
        task = Task(len(self.tasks), resource, cost, list(needs), run, bias)
        self.tasks.append(task)
        return task

    def compute(self, cost, needs, run, bias=0.0):
        return self.add(CORE, cost, needs, run, bias)

    def levels(self):
        for task in self.tasks:
            for need in task.needs:
                need.users.append(task)
        for task in reversed(self.tasks):
            task.level = task.cost + max([user.level for user in task.users], default=0.0)

    def execute(self, results):
        self.levels()
        waiting = sorted(self.tasks, key=lambda task: (-task.bias, -task.level))
        values, flying, free, shown = {}, {}, {}, set()
        now, fresh = 0.0, False

        def when(task):
            times = [
                0.0 if need in values else flying[need][0] if need in flying else None
                for need in task.needs
            ]
            if None in times:
                return None
            late = max(times, default=0.0)
            return late + MARGINS[task.resource] if late > 0.0 else 0.0

        def issue(task):
            nonlocal fresh
            ended = [need for need in task.needs if need in flying]
            if task.resource in HOPPING:
                under = sorted(
                    (end, other.number, other)
                    for other, (end, _) in flying.items()
                    if other.resource in HOPPING and other not in ended
                )
                ended += [other for _, _, other in under[: max(0, len(under) + 1 - HOPS)]]
            for need in ended:
                values[need] = flying.pop(need)[1]
                self.log.append((now, 1, need))
                fresh = True
            if fresh:
                wanted = {need for other in waiting for need in other.needs}
                first = {done for done in values if done in results} - shown
                names = sorted(
                    {done for done in values if done in wanted} | first,
                    key=lambda done: done.number,
                )
                tied = lax.optimization_barrier(tuple(values[done] for done in names))
                values.update(zip(names, tied))
                shown.update(first)
                fresh = False
            waiting.remove(task)
            self.log.append((now, 0, task))
            return task.run(values)

        while waiting:
            wakes, hops, chosen = [], [], None
            for task in waiting:
                at, link = when(task), task.resource
                if at is None:
                    continue
                if link != CORE:
                    ends = sorted(
                        end for other, (end, _) in flying.items() if other.resource == link and end > now
                    )
                    if len(ends) >= DEPTHS[link]:
                        early = EARLY if link in (AHEAD, BACK) and len(ends) == 1 else 0.0
                        at = max(at, ends[-DEPTHS[link]] - early)
                    others = [
                        end
                        for other, (end, _) in flying.items()
                        if other.resource in HOPPING and other not in task.needs
                    ]
                    if link in HOPPING and len(others) >= HOPS:
                        at = max(at, sorted(others)[len(others) - HOPS] + MARGINS[SMALL])
                if at > now:
                    wakes.append(at)
                    if link in (AHEAD, BACK) or task.bias >= 10.0:
                        hops.append(at)
                elif link != CORE:
                    chosen = task
                    break
                elif chosen is None:
                    chosen = task
            soon = [at for at in hops if now < at <= now + PATIENCE]
            if chosen is None or (chosen.resource == CORE and chosen.cost > LONG and soon):
                now = min(soon) if chosen else min(wakes)
                continue
            result = issue(chosen)
            link = chosen.resource
            if link == CORE:
                values[chosen] = result
                now += chosen.cost
                fresh = True
                continue
            behind = free.get(link, 0.0) > now and link != SMALL
            end = free[link] + chosen.cost - QUEUED if behind else now + chosen.cost
            if link != SMALL:
                free[link] = end
            flying[chosen] = (end, result)
            now += STARTS[link]
        for task in results:
            if task in flying:
                values[task] = flying.pop(task)[1]
        self.log.append((now, 1, None))
        return [values[task] for task in results]


def dot_cost(rows, inner, columns):
    return 1.0 + 2.0 * rows * inner * columns / DOT_RATE


def move_cost(count):
    return 1.0 + count / 2e6


def ring_gather(plan, ring, own, count, flip=False, bias=0.0, after={}):
    blocks = {0: own}
    for link, way, step in ring.ways(flip):
        source = own
        for n, distance in enumerate(way):

            def move(v, source=source, step=step):
                return ring.hop(v[source], step)

            held = [after[link, n]] if (link, n) in after else []
            cost = HOP_COST + count * 2 / LINK_RATE
            source = plan.add(link, cost, [source, *held], move, bias)
            blocks[distance] = source
    return blocks


def ring_reduce(plan, ring, parts, count, finish, flip=False, bias=2.0, after=()):
    def total(distance, sources):
        slot = ring.slots[distance]
        part, index = next(
            (task, slot - first) for task, first, count in parts if 0 <= slot - first < count
        )
        if not sources:
            return plan.compute(0.0, [part], lambda v: v[part][index], 20.0)

        def add(v):
            terms = [v[part][index], *(v[source] for source in sources)]
            if distance:
                return add_up([(term, 0) for term in terms], halves)
            return finish(sum(term.astype(floats) for term in terms))

        cost = 0.5 + count / 3e5
        if not distance:
            cost = cost + move_cost(3 * count)
        return plan.compute(cost, [part, *sources], add, 10.0 if distance else -1.0)

    passings = []
    for link, way, step in ring.ways(flip):
        passing = []
        for distance in reversed(way):
            made = total(distance, passing)

            def move(v, made=made, step=step):
                return ring.hop(v[made], -step)

            cost = HOP_COST + count * 2 / LINK_RATE
            passing = [plan.add(link, cost, [made, *after], move, bias)]
        passings.extend(passing)
    return total(0, passings)


def params():
    return pltpu.CompilerParams(vmem_limit_bytes=VMEM_BYTES)


def add_up(terms, dtype, rows=None):
    rows = rows or terms[0][0].shape[0]
    return sum(array[first : first + rows].astype(floats) for array, first in terms).astype(dtype)


def first_norm(tokens, gain, tiles, own):
    seq_len, width = tokens.shape
    part = seq_len // tiles

    def body(own_ref, tok_ref, gain_ref, out_ref, rows_ref, factor_ref):
        whole = tok_ref[...].astype(floats)
        inverse = lax.rsqrt(jnp.mean(whole * whole, axis=-1, keepdims=True) + epsilon)
        out_ref[...] = (whole * inverse * gain_ref[...]).astype(halves)
        factor_ref[...] = jnp.broadcast_to(inverse, factor_ref.shape)

        @pl.when(pl.program_id(0) == own_ref[0])
        def _():
            rows_ref[...] = tok_ref[...]

    return pl.pallas_call(
        body,
        out_shape=(
            jax.ShapeDtypeStruct((seq_len, width), halves),
            jax.ShapeDtypeStruct((part, width), tokens.dtype),
            jax.ShapeDtypeStruct((seq_len, 128), floats),
        ),
        grid_spec=pltpu.PrefetchScalarGridSpec(
            num_scalar_prefetch=1,
            grid=(tiles,),
            in_specs=[
                pl.BlockSpec((part, width), lambda i, own_ref: (i, 0)),
                pl.BlockSpec((1, width), lambda i, own_ref: (0, 0)),
            ],
            out_specs=(
                pl.BlockSpec((part, width), lambda i, own_ref: (i, 0)),
                pl.BlockSpec((part, width), lambda i, own_ref: (0, 0)),
                pl.BlockSpec((part, 128), lambda i, own_ref: (i, 0)),
            ),
        ),
        compiler_params=params(),
        cost_estimate=HEAVY,
    )(own, tokens, gain.reshape(1, width))


def tile_of(size):
    return max(step for step in range(128, 513, 128) if size % step == 0)


def gradient_blocks(groups, order, base, count, tile, keep):
    block = groups[0][1].shape[1] // order.shape[0]
    starts, total = [], 0
    for lhs, _ in groups:
        starts.append(total)
        total += lhs.shape[0] * lhs.shape[2] // tile
    in_specs, operands = [], []
    for start, (lhs, rhs) in zip(starts, groups):
        sides, tokens, height = lhs.shape
        steps = height // tile

        def place_of(i, order_ref, start=start, sides=sides, steps=steps):
            step = jnp.clip(i - start, 0, sides * steps - 1)
            return step // steps, 0, step % steps

        def column(j, tokens=tokens):
            return pl.BlockSpec(
                (tokens, block), lambda i, order_ref: (0, order_ref[base + j])
            )

        in_specs += [pl.BlockSpec((1, tokens, tile), place_of), *(column(j) for j in range(count))]
        operands += [lhs, *([rhs] * count)]

    def body(order_ref, *refs):
        out_refs = refs[len(operands) :]
        step = pl.program_id(0)
        for n, start in enumerate(starts):
            end = starts[n + 1] if n + 1 < len(starts) else total
            lhs_ref, *rhs_refs = refs[n * (count + 1) : (n + 1) * (count + 1)]

            @pl.when(jnp.logical_and(step >= start, step < end))
            def _():
                turned = lhs_ref[0].T
                for rhs_ref, out_ref in zip(rhs_refs, out_refs):
                    product = jnp.dot(turned, rhs_ref[...], preferred_element_type=floats)
                    out_ref[...] = product[:keep].astype(halves)

    return pl.pallas_call(
        body,
        out_shape=[jax.ShapeDtypeStruct((total * keep, block), halves)] * count,
        grid_spec=pltpu.PrefetchScalarGridSpec(
            num_scalar_prefetch=1,
            grid=(total,),
            in_specs=in_specs,
            out_specs=[pl.BlockSpec((keep, block), lambda i, order_ref: (i, 0))] * count,
        ),
        compiler_params=params(),
        cost_estimate=HEAVY,
    )(order, *operands)


def matmul_across(lhs, rhs, first, count):
    tall, inner = lhs.shape
    tile = 256 if count % 256 == 0 and first % 256 == 0 else 128

    def body(lhs_ref, rhs_ref, out_ref):
        out_ref[...] = lax.dot_general(
            lhs_ref[...], rhs_ref[...], contract_last, preferred_element_type=floats
        )

    return pl.pallas_call(
        body,
        out_shape=jax.ShapeDtypeStruct((tall, count), floats),
        grid=(count // tile,),
        in_specs=[
            pl.BlockSpec((tall, inner), lambda j: (0, 0)),
            pl.BlockSpec((tile, inner), lambda j: (first // tile + j, 0)),
        ],
        out_specs=pl.BlockSpec((tall, tile), lambda j: (0, j)),
        compiler_params=params(),
        cost_estimate=HEAVY,
    )(lhs, rhs)


def halves_spec(parts, inner, tall, tile):
    half, part = tall // inner, tall // parts

    def put(places_ref, product, own_ref, other_ref):
        for a in range(parts):
            rows = product[a * part : (a + 1) * part]
            place = places_ref[a]

            @pl.when(place < parts // inner)
            def _():
                own_ref[pl.ds(pl.multiple_of(place * part, part), part)] = rows

            if inner > 1:

                @pl.when(place >= parts // inner)
                def _():
                    at = pl.multiple_of(place * part - half, part)
                    other_ref[pl.ds(at, part)] = rows.astype(halves)

    return half, pl.BlockSpec((half, tile), lambda j, p: (0, j)), put


def matmul_halves(lhs, rhs, places, inner, first=0, scaled=None):
    tall, depth = lhs.shape
    wide = rhs.shape[1]
    tile = 256 if wide % 256 == 0 else 128
    half, spec, put = halves_spec(places.shape[0], inner, tall, tile)

    def body(places_ref, lhs_ref, rhs_ref, *refs):
        product = jnp.dot(lhs_ref[...], rhs_ref[...], preferred_element_type=floats)
        put(places_ref, product, *refs[len(scaled or ()) :][:2])
        if scaled:
            array_ref, factor_ref, sums_ref = refs[0], refs[1], refs[-1]
            terms = product * array_ref[...].astype(floats) * factor_ref[:, :1]
            sums_ref[...] = jnp.sum(terms.reshape(tall // 8, 8, tile), axis=0)

    more_in, more_out, more_shapes = [], [], []
    if scaled:
        more_in = [
            pl.BlockSpec((tall, tile), lambda j, p: (0, j)),
            pl.BlockSpec(scaled[1].shape, lambda j, p: (0, 0)),
        ]
        more_out = [pl.BlockSpec((8, tile), lambda j, p: (0, j))]
        more_shapes = [jax.ShapeDtypeStruct((8, wide), floats)]
    return pl.pallas_call(
        body,
        out_shape=(
            jax.ShapeDtypeStruct((half, wide), floats),
            jax.ShapeDtypeStruct((half, wide), halves),
            *more_shapes,
        ),
        grid_spec=pltpu.PrefetchScalarGridSpec(
            num_scalar_prefetch=1,
            grid=(wide // tile,),
            in_specs=[
                pl.BlockSpec((tall, depth), lambda j, p: (0, 0)),
                pl.BlockSpec((depth, tile), lambda j, p: (first // depth, j)),
                *more_in,
            ],
            out_specs=(spec, spec, *more_out),
        ),
        compiler_params=params(),
        cost_estimate=HEAVY,
    )(places, lhs, rhs, *(scaled or ()))


def gated_forward(normed, weights):
    tokens, inner = normed.shape
    hidden = weights.shape[1] // 2
    tile = 256 if hidden % 256 == 0 else 128
    steps = hidden // tile

    def body(in_ref, gate_ref, up_ref, gate_out, up_out, hidden_out):
        gate = jnp.dot(in_ref[...], gate_ref[...], preferred_element_type=floats)
        up = jnp.dot(in_ref[...], up_ref[...], preferred_element_type=floats)
        gate_out[...] = gate
        up_out[...] = up
        hidden_out[...] = (gelu(gate) * up).astype(halves)

    column = pl.BlockSpec((tokens, tile), lambda j: (0, j))
    return pl.pallas_call(
        body,
        out_shape=(
            jax.ShapeDtypeStruct((tokens, hidden), floats),
            jax.ShapeDtypeStruct((tokens, hidden), floats),
            jax.ShapeDtypeStruct((tokens, hidden), halves),
        ),
        grid=(steps,),
        in_specs=[
            pl.BlockSpec((tokens, inner), lambda j: (0, 0)),
            pl.BlockSpec((inner, tile), lambda j: (0, j)),
            pl.BlockSpec((inner, tile), lambda j: (0, steps + j)),
        ],
        out_specs=(column, column, column),
        compiler_params=params(),
        cost_estimate=HEAVY,
    )(normed, weights, weights)


def gated_backward(cotangent, down, gate, up):
    tokens, inner = cotangent.shape
    hidden = down.shape[0]
    tile = 256 if hidden % 256 == 0 else 128

    def body(cot_ref, down_ref, gate_ref, up_ref, out_ref):
        back = lax.dot_general(
            cot_ref[...], down_ref[...], contract_last, preferred_element_type=floats
        )
        active, slope = gelu_parts(gate_ref[...])
        out_ref[0] = (back * up_ref[...] * slope).astype(halves)
        out_ref[1] = (back * active).astype(halves)

    column = pl.BlockSpec((tokens, tile), lambda j: (0, j))
    return pl.pallas_call(
        body,
        out_shape=jax.ShapeDtypeStruct((2, tokens, hidden), halves),
        grid=(hidden // tile,),
        in_specs=[
            pl.BlockSpec((tokens, inner), lambda j: (0, 0)),
            pl.BlockSpec((tile, inner), lambda j: (j, 0)),
            column,
            column,
        ],
        out_specs=pl.BlockSpec((2, tokens, tile), lambda j: (0, 0, j)),
        compiler_params=params(),
        cost_estimate=HEAVY,
    )(cotangent, down, gate, up)


def pair_halves(pair, weights, places, inner):
    _, tall, hidden = pair.shape
    wide = weights.shape[0]
    tile = 256 if wide % 256 == 0 else 128
    half, spec, put = halves_spec(places.shape[0], inner, tall, tile)

    def body(places_ref, pair_ref, gate_ref, up_ref, own_ref, other_ref):
        product = 0.0
        for side, ref in enumerate((gate_ref, up_ref)):
            product = product + lax.dot_general(
                pair_ref[side], ref[...], contract_last, preferred_element_type=floats
            )
        put(places_ref, product, own_ref, other_ref)

    weight = lambda side: pl.BlockSpec((tile, hidden), lambda j, p: (j, side))
    return pl.pallas_call(
        body,
        out_shape=(
            jax.ShapeDtypeStruct((half, wide), floats),
            jax.ShapeDtypeStruct((half, wide), halves),
        ),
        grid_spec=pltpu.PrefetchScalarGridSpec(
            num_scalar_prefetch=1,
            grid=(wide // tile,),
            in_specs=[pl.BlockSpec((2, tall, hidden), lambda j, p: (0, 0, 0)), weight(0), weight(1)],
            out_specs=(spec, spec),
        ),
        compiler_params=params(),
        cost_estimate=HEAVY,
    )(places, pair, weights, weights)


def segment_of(places, ends_ref):
    segment = jnp.zeros(places.shape, jnp.int32)
    for j in range(ends_ref.shape[0] - 1):
        segment = segment + (places >= ends_ref[j]).astype(jnp.int32)
    return segment


def same_behind(places, ends_ref, offset):
    agree = segment_of(places, ends_ref) == segment_of(places - offset, ends_ref)
    return jnp.logical_and(agree, places >= offset).astype(floats)


def same_ahead(places, ends_ref, offset, seq_len):
    agree = segment_of(places, ends_ref) == segment_of(places + offset, ends_ref)
    return jnp.logical_and(agree, places + offset < seq_len).astype(floats)


def lane_chunks(width):
    step = 256 if width % 256 == 0 else 128
    return [slice(at, at + step) for at in range(0, width, step)]


def gate_values(pre_a, pre_i, decay8):
    rate = jax.nn.sigmoid(pre_a)
    admit = jax.nn.sigmoid(pre_i)
    power = decay8 * rate
    alpha = jnp.exp(-power)
    twice = 2.0 * power
    series = 1.0 - twice * (1.0 / 7.0)
    for order in (6.0, 5.0, 4.0, 3.0, 2.0):
        series = 1.0 - (twice * (1.0 / order)) * series
    raw = jnp.where(twice < 0.5, twice * series, 1.0 - alpha * alpha)
    one_minus = jnp.maximum(raw, floor_value)
    inverse = lax.rsqrt(one_minus)
    return rate, admit, alpha, raw, one_minus * inverse, inverse


def gelu_parts(value):
    square = value * value
    bend = jnp.tanh(gelu_root * (value + gelu_cube * (square * value)))
    half = 0.5 * (1.0 + bend)
    slope = half + 0.5 * value * (1.0 - bend * bend) * (
        gelu_root * (1.0 + 3.0 * gelu_cube * square)
    )
    return value * half, slope


def gelu(value):
    return gelu_parts(value)[0]


def recur_forward(branches, doc_ends, vectors, gates, tiles):
    seq_len, lanes = branches.shape[0], branches.shape[1] // 2
    part = seq_len // tiles
    chunks = lane_chunks(lanes)

    def body(
        ends_ref, x_ref, y_ref, vec_ref, gate_ref,
        mixed_ref, conv_ref, pre_ref, prev_ref, xs, carry,
    ):
        tile = pl.program_id(0)

        @pl.when(tile == 0)
        def _():
            xs[0:8] = jnp.zeros((8, lanes), floats)
            carry[...] = jnp.zeros_like(carry)

        xs[8 : 8 + part] = x_ref[...]
        rows = lax.broadcasted_iota(jnp.int32, (CHUNK, 1), 0)

        def convolve(c, _):
            at = pl.multiple_of(c * CHUNK, CHUNK)
            here = tile * part + at + rows
            same = [same_behind(here, ends_ref, k) for k in range(1, 4)]
            for lane in chunks:
                window = xs[pl.ds(at, CHUNK + 8), lane]
                total = vec_ref[4:5, lane] + vec_ref[0:1, lane] * window[8:]
                for k in range(1, 4):
                    moved = pltpu.roll(window, k, 0)[8:]
                    total = total + vec_ref[k : k + 1, lane] * moved * same[k - 1]
                conv_ref[pl.ds(at, CHUNK), lane] = total.astype(halves)
            return 0

        lax.fori_loop(0, part // CHUNK, convolve, 0)
        xs[0:8] = xs[part : part + 8]
        pre_ref[...] = jnp.dot(conv_ref[...], gate_ref[...], preferred_element_type=floats)

        def advance(c, entering):
            at = pl.multiple_of(c * CHUNK, CHUNK)
            here = tile * part + at + rows
            fresh = 1.0 - same_behind(here, ends_ref, 1)
            leaving = []
            for state, lane in zip(entering, chunks):
                span = lane.stop - lane.start
                shift_lane = slice(lane.start + lanes, lane.stop + lanes)
                pre_a = pre_ref[pl.ds(at, CHUNK), lane] + vec_ref[6:7, lane]
                pre_i = pre_ref[pl.ds(at, CHUNK), shift_lane] + vec_ref[7:8, lane]
                pre_ref[pl.ds(at, CHUNK), lane] = pre_a
                pre_ref[pl.ds(at, CHUNK), shift_lane] = pre_i
                conv_in = conv_ref[pl.ds(at, CHUNK), lane].astype(floats)
                _, admit, alpha, _, root, _ = gate_values(pre_a, pre_i, vec_ref[5:6, lane])
                keep = 1.0 - fresh
                coef = alpha * keep
                drive = (fresh + root * keep) * admit * conv_in
                index = lax.broadcasted_iota(jnp.int32, (CHUNK, span), 0)
                for d in (1, 2, 4):
                    inside = (index & 7) >= d
                    drive = jnp.where(inside, drive + coef * pltpu.roll(drive, d, 0), drive)
                    coef = jnp.where(inside, coef * pltpu.roll(coef, d, 0), coef)
                groups = []
                first = state
                for g in range(CHUNK // 8):
                    group = slice(g * 8, g * 8 + 8)
                    groups.append(coef[group] * state + drive[group])
                    state = groups[-1][7:8]
                states = jnp.concatenate(groups, axis=0)
                prev_ref[pl.ds(at, CHUNK), lane] = jnp.where(
                    index == 0, first, pltpu.roll(states, 1, 0)
                )
                mixed = states * gelu(y_ref[pl.ds(at, CHUNK), lane])
                mixed_ref[pl.ds(at, CHUNK), lane] = mixed.astype(halves)
                leaving.append(state)
            return tuple(leaving)

        ended = lax.fori_loop(
            0, part // CHUNK, advance, tuple(carry[0:1, lane] for lane in chunks)
        )
        for state, lane in zip(ended, chunks):
            carry[0:1, lane] = state

    own = lambda column: pl.BlockSpec((part, lanes), lambda i, e: (i, column))
    straight = lambda width: pl.BlockSpec((part, width), lambda i, e: (i, 0))
    whole = lambda array: pl.BlockSpec(array.shape, lambda i, e: (0, 0))
    return pl.pallas_call(
        body,
        out_shape=(
            jax.ShapeDtypeStruct((seq_len, lanes), halves),
            jax.ShapeDtypeStruct((seq_len, lanes), halves),
            jax.ShapeDtypeStruct((seq_len, 2 * lanes), floats),
            jax.ShapeDtypeStruct((seq_len, lanes), floats),
        ),
        grid_spec=pltpu.PrefetchScalarGridSpec(
            num_scalar_prefetch=1,
            grid=(tiles,),
            in_specs=[own(0), own(1), whole(vectors), whole(gates)],
            out_specs=(own(0), straight(lanes), straight(2 * lanes), straight(lanes)),
            scratch_shapes=[pltpu.VMEM((part + 8, lanes), floats), pltpu.VMEM((8, lanes), floats)],
        ),
        compiler_params=params(),
        cost_estimate=HEAVY,
    )(doc_ends, branches, branches, vectors, gates)


def recur_backward(back_mixed, branches, conv_in, pre, previous, doc_ends, vectors, gates, tiles):
    seq_len, lanes = conv_in.shape
    part = seq_len // tiles
    chunks = lane_chunks(lanes)
    steps = part // CHUNK

    def body(
        ends_ref, bm_ref, x_ref, y_ref, conv_ref, pre_ref, prev_ref, vec_ref, gate_ref,
        bxy_ref, bai_ref, sums_ref, ahead, sums, carry,
    ):
        tile = tiles - 1 - pl.program_id(0)

        @pl.when(pl.program_id(0) == 0)
        def _():
            ahead[part : part + 8] = jnp.zeros((8, lanes), floats)
            sums[...] = jnp.zeros_like(sums)
            carry[...] = jnp.zeros_like(carry)

        rows = lax.broadcasted_iota(jnp.int32, (CHUNK, 1), 0)

        def add_rows(which, lane, value):
            for g in range(CHUNK // 8):
                sums[which * 8 : which * 8 + 8, lane] += value[g * 8 : g * 8 + 8]

        def retreat(c, entering):
            at = pl.multiple_of((steps - 1 - c) * CHUNK, CHUNK)
            span_rows = pl.ds(at, CHUNK)
            here = tile * part + at + rows
            keep = same_behind(here, ends_ref, 1)
            fresh = 1.0 - keep
            leaving = []
            for (back_next, coef_next), lane in zip(entering, chunks):
                span = lane.stop - lane.start
                shift_lane = slice(lane.start + lanes, lane.stop + lanes)
                decay8 = vec_ref[5:6, lane]
                rate, admit, alpha, raw, root, inverse = gate_values(
                    pre_ref[span_rows, lane], pre_ref[span_rows, shift_lane], decay8
                )
                conv = conv_ref[span_rows, lane].astype(floats)
                before = prev_ref[span_rows, lane]
                scale_in = fresh + root * keep
                coef = alpha * keep
                driven = scale_in * admit
                states = coef * before + driven * conv
                active, slope = gelu_parts(y_ref[span_rows, lane])
                back_mix = bm_ref[span_rows, lane]
                bxy_ref[span_rows, shift_lane] = (back_mix * states * slope).astype(halves)
                index = lax.broadcasted_iota(jnp.int32, (CHUNK, span), 0)
                back = back_mix * active
                chain = jnp.where(index == CHUNK - 1, coef_next, pltpu.roll(coef, CHUNK - 1, 0))
                for d in (1, 2, 4):
                    inside = (index & 7) < 8 - d
                    back = jnp.where(inside, back + chain * pltpu.roll(back, CHUNK - d, 0), back)
                    chain = jnp.where(inside, chain * pltpu.roll(chain, CHUNK - d, 0), chain)
                groups = []
                for g in reversed(range(CHUNK // 8)):
                    group = slice(g * 8, g * 8 + 8)
                    groups.insert(0, back[group] + chain[group] * back_next)
                    back_next = groups[0][0:1]
                back_state = jnp.concatenate(groups, axis=0)
                through = back_state * conv
                bound = jnp.where(raw > floor_value, through * admit * alpha * inverse, 0.0)
                back_alpha = (back_state * before - bound) * keep * alpha
                add_rows(5, lane, back_alpha * rate)
                back_a = (back_alpha * (-decay8) * rate * (1.0 - rate)).astype(halves)
                back_i = (through * scale_in * admit * (1.0 - admit)).astype(halves)
                add_rows(6, lane, back_a.astype(floats))
                add_rows(7, lane, back_i.astype(floats))
                bai_ref[span_rows, lane] = back_a
                bai_ref[span_rows, shift_lane] = back_i
                ahead[span_rows, lane] = back_state * driven
                leaving.append((back_next, coef[0:1]))
            return tuple(leaving)

        ended = lax.fori_loop(
            0, steps, retreat, tuple((carry[0:1, lane], carry[8:9, lane]) for lane in chunks)
        )
        for (back_next, coef_next), lane in zip(ended, chunks):
            carry[0:1, lane] = back_next
            carry[8:9, lane] = coef_next

        ahead[0:part] += lax.dot_general(
            bai_ref[...], gate_ref[...], contract_last, preferred_element_type=floats
        )

        def convolve(c, _):
            at = pl.multiple_of(c * CHUNK, CHUNK)
            here = tile * part + at + rows
            same = [same_ahead(here, ends_ref, k, seq_len) for k in range(1, 4)]
            for lane in chunks:
                window = ahead[pl.ds(at, CHUNK + 8), lane]
                x_part = x_ref[pl.ds(at, CHUNK), lane]
                direct = window[:CHUNK]
                back_x = vec_ref[0:1, lane] * direct
                add_rows(0, lane, x_part * direct)
                add_rows(4, lane, direct)
                for k in range(1, 4):
                    moved = pltpu.roll(window, CHUNK + 8 - k, 0)[:CHUNK] * same[k - 1]
                    back_x = back_x + vec_ref[k : k + 1, lane] * moved
                    add_rows(k, lane, x_part * moved)
                bxy_ref[pl.ds(at, CHUNK), lane] = back_x.astype(halves)
            return 0

        lax.fori_loop(0, steps, convolve, 0)
        ahead[part : part + 8] = ahead[0:8]

        @pl.when(pl.program_id(0) == tiles - 1)
        def _():
            for which in range(8):
                sums_ref[which : which + 1] = jnp.sum(
                    sums[which * 8 : which * 8 + 8], axis=0, keepdims=True
                )

    own = lambda width, column: pl.BlockSpec((part, width), lambda i, e: (tiles - 1 - i, column))
    straight = lambda width: pl.BlockSpec((part, width), lambda i, e: (tiles - 1 - i, 0))
    whole = lambda array: pl.BlockSpec(array.shape, lambda i, e: (0, 0))
    return pl.pallas_call(
        body,
        out_shape=(
            jax.ShapeDtypeStruct((seq_len, 2 * lanes), halves),
            jax.ShapeDtypeStruct((seq_len, 2 * lanes), halves),
            jax.ShapeDtypeStruct((8, lanes), floats),
        ),
        grid_spec=pltpu.PrefetchScalarGridSpec(
            num_scalar_prefetch=1,
            grid=(tiles,),
            in_specs=[
                own(lanes, 0), own(lanes, 0), own(lanes, 1),
                straight(lanes), straight(2 * lanes), straight(lanes),
                whole(vectors), whole(gates),
            ],
            out_specs=(
                own(2 * lanes, 0), straight(2 * lanes), pl.BlockSpec((8, lanes), lambda i, e: (0, 0)),
            ),
            scratch_shapes=[
                pltpu.VMEM((part + 8, lanes), floats),
                pltpu.VMEM((64, lanes), floats),
                pltpu.VMEM((16, lanes), floats),
            ],
        ),
        compiler_params=params(),
        cost_estimate=HEAVY,
    )(doc_ends, back_mixed, branches, branches, conv_in, pre, previous, vectors, gates)


def rms_norm(inputs, scales):
    return inputs * lax.rsqrt(jnp.mean(inputs * inputs, axis=-1, keepdims=True) + epsilon) * scales


def inner_of(count):
    return max(d for d in range(1, count + 1) if count % d == 0 and d * d <= count)


def on_device(
    tokens,
    doc_lengths,
    gain_mix,
    value_weight,
    branch_weight,
    conv_weight,
    conv_bias,
    recur_gate,
    input_gate,
    recur_bias,
    input_bias,
    decay_param,
    out_weight,
    gain_ffn,
    gate_weight,
    up_weight,
    down_weight,
    cotangent,
):
    seq_len, _, width = tokens.shape
    heads, head_width = recur_gate.shape[:2]
    channels = value_weight.shape[1]
    hidden_width = gate_weight.shape[1]
    lanes = round_up(channels, 128)
    sent = round_up(channels, 16)
    dp = Ring(DP, inner_of(lax.axis_size(DP)))
    parts = lax.axis_size(CHAN)
    part = seq_len // parts
    block = width // dp.count
    order = dp.order()
    chan = lax.axis_index(CHAN)
    own_tile = chan.reshape(1).astype(jnp.int32)
    cores = 2 if parts % 2 == 0 else 1
    chips = parts // cores
    tiles = jnp.arange(parts, dtype=jnp.int32)
    row_places = ((tiles - chan) % cores) * chips + (tiles // cores - chan // cores) % chips
    doc_ends = jnp.cumsum(doc_lengths[0])
    plan = Plan()
    compute = plan.compute

    def gather_weight(own, count, flip, bias, after, put):
        blocks = ring_gather(plan, dp, own, count, flip, bias, after)
        full = None
        for distance in sorted(blocks, key=lambda d: min(d, dp.count - d)):

            def extend(v, before=full, piece=blocks[distance], slot=dp.slots[distance]):
                return put(
                    None if before is None else v[before], v[piece], order[slot : slot + 1]
                )

            needs = [blocks[distance]] if full is None else [full, blocks[distance]]
            first = 0.0 if full else 6.0
            full = compute(0.6 + count / 2.6e5 + first, needs, extend)
        return full, blocks

    def put_mix(full, piece, at):
        if full is None:
            full = jnp.zeros((3 * lanes, width), halves), jnp.zeros((hidden_width, width), halves)
        mix, down = full
        for i in range(3):
            rows = piece[i * sent : (i + 1) * sent]
            mix = lax.dynamic_update_slice(mix, rows, (i * lanes, at[0] * block))
        return mix, lax.dynamic_update_slice(down, piece[3 * sent :], (0, at[0] * block))

    def put_rows(full, piece, at):
        if full is None:
            full = jnp.zeros((width, 2 * hidden_width), halves)
        return lax.dynamic_update_slice(full, piece, (at[0] * block, 0))

    def mix_of(value, branch, out, down):
        pieces = [pad_dim(array, 0, sent) for array in (value.T, branch.T, out)]
        return jnp.concatenate([*pieces, down], axis=0)

    mix = compute(
        3.0, [], lambda v: mix_of(value_weight, branch_weight, out_weight, down_weight), 8.0
    )
    both_own = compute(2.0, [], lambda v: jnp.concatenate([gate_weight, up_weight], axis=1), 1.0)
    mix_full, mix_blocks = gather_weight(
        mix, (3 * sent + hidden_width) * block, False, 9.0, {}, put_mix
    )
    far = dp.count // 2
    both_full, _ = gather_weight(
        both_own, 2 * hidden_width * block, True, 8.0,
        {(AHEAD, 0): mix_blocks[far], (BACK, 0): mix_blocks[far + 1]}, put_rows,
    )

    def spread(gate):
        total = 0.0
        for h in range(heads):
            low = h * head_width
            total = total + jnp.pad(gate[h], ((low, lanes - low - head_width),) * 2)
        return total

    def small_parameters(v):
        gates = jnp.concatenate([spread(recur_gate), spread(input_gate)], axis=1)
        vectors = [
            conv_weight,
            conv_bias[None],
            decay_scale * jax.nn.softplus(decay_param)[None],
            recur_bias[None],
            input_bias[None],
        ]
        return gates, pad_dim(jnp.concatenate(vectors, axis=0), 1, lanes)

    small = compute(8.0, [], small_parameters)

    def cross(value, step):
        pairs = [
            (x * cores + c, ((x + step) % chips) * cores + c)
            for x in range(chips)
            for c in range(cores)
        ]
        return lax.ppermute(value, CHAN, pairs)

    def swap(value):
        pairs = [(x * cores + c, x * cores + (c + 1) % cores) for x in range(chips) for c in range(cores)]
        return lax.ppermute(value, CHAN, pairs)

    def gather_rows(own):
        return plan.add(
            CHIPS, 33.0, [own], lambda v: lax.all_gather(v[own], CHAN, axis=0, tiled=True)
        )

    def reduce_rows(product, after=()):
        terms = []
        if cores > 1:
            terms = [plan.add(TWIN, 9.0, [product, *after], lambda v: swap(v[product][1]), 3.0)]
        passing = []
        for s in reversed(range(chips)):

            def add(v, s=s, passing=tuple(passing)):
                pieces = [(v[product][0], s * part), *((v[term], s * part) for term in terms)]
                pieces += [(v[term], 0) for term in passing]
                return add_up(pieces, halves if s else floats, part)

            made = compute(2.8, [product, *terms, *passing], add, 10.0)
            if s:
                passing = [
                    plan.add(CROSS, 26.5, [made], lambda v, made=made: cross(v[made], 1), 3.0)
                ]
        return made

    def small_total(source, axes):
        for axis in axes:
            count = lax.axis_size(axis)
            assert count & (count - 1) == 0
            bit = count // 2
            while bit:
                pairs = [(i, i ^ bit) for i in range(count)]

                def send(v, source=source, axis=axis, pairs=pairs):
                    return lax.ppermute(v[source], axis, pairs)

                other = plan.add(SMALL, 26.0 if axis == DP else 8.0, [source], send)

                def add(v, source=source, other=other):
                    return v[source] + v[other]

                source = compute(0.5, [source, other], add)
                bit //= 2
        return source

    norm_in = compute(
        5.0, [], lambda v: first_norm(tokens.reshape(seq_len, width), gain_mix, parts, own_tile)
    )
    cot = compute(1.5, [], lambda v: cotangent.reshape(part, width))
    cot_full = gather_rows(cot)
    branches = compute(
        10.8,
        [norm_in, mix_full],
        lambda v: matmul_across(v[norm_in][0], v[mix_full][0], 0, 2 * lanes),
    )
    recur = compute(
        20.2,
        [branches, small],
        lambda v: recur_forward(v[branches], doc_ends, v[small][1], v[small][0], parts),
    )
    mixed = compute(0.0, [recur], lambda v: v[recur][0], 30.0)
    mixed_out = compute(
        9.2,
        [mixed, mix_full],
        lambda v: matmul_halves(v[mixed], v[mix_full][0], row_places, cores, 2 * lanes),
    )
    branch_out = reduce_rows(mixed_out)

    def middle_of(v):
        residual = v[norm_in][1].astype(floats) + v[branch_out]
        return residual, rms_norm(residual, gain_ffn).astype(halves)

    middle = compute(3.0, [norm_in, branch_out], middle_of)
    mid = compute(0.0, [middle], lambda v: v[middle][1], 30.0)
    mid_full = gather_rows(mid)

    gated = compute(
        19.7,
        [mid_full, both_full],
        lambda v: gated_forward(v[mid_full], v[both_full]),
    )
    hidden = compute(0.0, [gated], lambda v: v[gated][2], 30.0)

    def gradient(needs, groups, tile, keep, quarters, costs, bias):
        first, parts = 0, []
        for n, (quarter, cost) in enumerate(zip(quarters, costs)):
            count = quarter * dp.count // 4

            def blocks(v, first=first, count=count):
                return gradient_blocks(groups(v), order, first, count, tile, keep)

            parts.append((compute(cost, needs, blocks, -0.5 * n if n else bias), first, count))
            first += count
        return parts

    back_both = compute(
        14.7,
        [gated, cot_full, mix_full],
        lambda v: gated_backward(v[cot_full], v[mix_full][1], *v[gated][:2]),
    )
    back_product = compute(
        20.5,
        [back_both, both_full],
        lambda v: pair_halves(v[back_both], v[both_full], row_places, cores),
    )
    back_mid = reduce_rows(back_product)
    tile = tile_of(hidden_width)
    grad_ffn = ring_reduce(
        plan,
        dp,
        gradient(
            [hidden, cot_full, back_both, mid_full],
            lambda v: [(v[hidden][None], v[cot_full]), (v[back_both], v[mid_full])],
            tile, tile, (1, 1, 2), (12.0, 12.0, 17.5), 2.0,
        ),
        3 * hidden_width * block,
        lambda total: (
            total[:hidden_width],
            total[hidden_width : 2 * hidden_width].T,
            total[2 * hidden_width :].T,
        ),
        False,
    )
    ffn_product = compute(
        12.0,
        [hidden, mix_full],
        lambda v: matmul_halves(v[hidden], v[mix_full][1], row_places, cores),
        -2.0,
    )

    def norm_back(inputs, gain, back):
        scale = lax.rsqrt(jnp.mean(inputs * inputs, axis=-1, keepdims=True) + epsilon)
        scaled = back * gain
        mean = jnp.mean(scaled * inputs, axis=-1, keepdims=True)
        through = scale * scaled - inputs * (scale * scale * scale * mean)
        return through

    def back_middle_of(v):
        residual, back = v[middle][0], v[back_mid]
        scale = lax.rsqrt(jnp.mean(residual * residual, axis=-1, keepdims=True) + epsilon)
        gain = jnp.sum((back * residual * scale).reshape(part // 8, 8, width), axis=0)
        back = v[cot].astype(floats) + norm_back(residual, gain_ffn, back)
        return back, back.astype(halves), gain

    back_middle = compute(4.0, [middle, back_mid, cot], back_middle_of)
    back_resid = compute(0.0, [back_middle], lambda v: v[back_middle][1], 30.0)
    branch_full = gather_rows(back_resid)
    ffn_out = reduce_rows(ffn_product, [branch_full])
    output = compute(
        4.0, [middle, ffn_out], lambda v: (v[middle][0] + v[ffn_out]).astype(halves), -1.0
    )
    back_mixed = compute(
        6.7,
        [branch_full, mix_full],
        lambda v: matmul_across(v[branch_full], v[mix_full][0], 2 * lanes, lanes),
    )
    recur_back = compute(
        26.5,
        [back_mixed, branches, recur, small],
        lambda v: recur_backward(
            v[back_mixed], v[branches], *v[recur][1:], doc_ends, v[small][1], v[small][0], parts
        ),
    )
    grad_mix = ring_reduce(
        plan,
        dp,
        gradient(
            [recur_back, norm_in, mixed, branch_full],
            lambda v: [(v[recur_back][0][None], v[norm_in][0]), (v[mixed][None], v[branch_full])],
            lanes, sent, (1, 3), (6.0, 14.0), 4.0,
        ),
        3 * sent * block,
        lambda total: (
            total[:channels].T,
            total[sent : sent + channels].T,
            total[2 * sent : 2 * sent + channels],
        ),
        True,
    )
    back_pair = compute(
        13.0,
        [recur_back, mix_full, norm_in],
        lambda v: matmul_halves(
            v[recur_back][0], v[mix_full][0], row_places, cores, 0,
            (tokens.reshape(seq_len, width), v[norm_in][2]),
        ),
        2.0,
    )
    back_norm_in = reduce_rows(back_pair)

    def back_first_of(v):
        through = norm_back(v[norm_in][1].astype(floats), gain_mix, v[back_norm_in])
        return v[back_middle][0] + through

    back_first = compute(5.0, [norm_in, back_norm_in, back_middle], back_first_of)

    def gate_grads_of(v):
        whole = lax.dot_general(
            v[recur][1], v[recur_back][1], contract_first, preferred_element_type=floats
        )
        return jnp.stack(
            [
                whole[
                    h * head_width : (h + 1) * head_width,
                    side * lanes + h * head_width : side * lanes + (h + 1) * head_width,
                ]
                for side in range(2)
                for h in range(heads)
            ]
        )

    gate_terms = compute(
        5.0, [recur, recur_back], lambda v: gate_grads_of(v).astype(halves), 3.5
    )
    gate_sums = plan.add(CHIPS, 110.0, [gate_terms], lambda v: lax.psum(v[gate_terms], DP), 3.0)
    gate_result = compute(
        4.0, [gate_sums], lambda v: tuple(jnp.split(v[gate_sums].astype(floats), 2)), -5.0
    )

    def both_gains(v):
        gains = [jnp.sum(terms, axis=0).reshape(8, -1) for terms in (v[back_middle][2], v[back_pair][2])]
        return jnp.concatenate(gains, axis=1)

    gain_rows = small_total(compute(2.0, [back_middle, back_pair], both_gains, 1.0), [CHAN])
    sums = small_total(
        compute(
            1.0,
            [recur_back, gain_rows],
            lambda v: jnp.concatenate([v[recur_back][2], v[gain_rows]], axis=1),
        ),
        [DP],
    )

    def sum_results_of(v):
        total = v[sums][:, :channels]
        decay = total[5] * (-decay_scale * jax.nn.sigmoid(decay_param))
        gains = v[sums][:, lanes:]
        return (
            total[:4], total[4], total[6], total[7], decay,
            gains[:, : width // 8].reshape(width), gains[:, width // 8 :].reshape(width),
        )

    sum_results = compute(3.0, [sums], sum_results_of)

    done = plan.execute(
        [
            output, back_first, grad_mix, sum_results, gate_result, grad_ffn,
        ]
    )
    output, first, (value, branch, out), summed, (recur, admit), (down, gate, up) = done
    return (
        output.reshape(part, 1, width),
        first.reshape(part, 1, width),
        summed[6],
        value,
        branch,
        summed[0],
        summed[1],
        recur,
        admit,
        summed[2],
        summed[3],
        summed[4],
        out,
        summed[5],
        gate,
        up,
        down,
    )


def solution(mesh):
    tokens, split, columns = P(None, DP, None), P(DP, CHAN), P(CHAN, DP)
    own, channels, heads = P(CHAN, DP, None), P(CHAN), P(CHAN, None, None)
    in_specs = (
        tokens, P(DP, None), P(), split, split, P(None, CHAN), channels, heads, heads,
        channels, channels, channels, columns, P(), split, split, columns, own,
    )
    out_specs = (
        own, own, P(), split, split, P(None, CHAN), channels, heads, heads,
        channels, channels, channels, columns, P(), split, split, columns,
    )
    return jax.shard_map(
        on_device, mesh=mesh, in_specs=in_specs, out_specs=out_specs, check_vma=False
    )
```
